32 devices in a mesh: ha: 2 (over core), wa: 4 (over y, x), clip: 4 (over z).
Axes of the slice: x: 2, y: 2, z: 4, core: 2. Of those that a mesh axis runs over, the one named last changes fastest.
Arguments:
- activations: bfloat16 [64, 8, 4, 32, 1024], P('clip', None, 'ha', 'wa'), may hold values from -6 to 6
- stride: int32 [64], replicated, may hold values from 1 to 4, as said below
- clip_order: int32 [64], replicated, may hold values from 0 to 63, each once
- cotangent: bfloat16 [64, 8, 4, 32, 1024], P('clip', None, 'ha', 'wa'), may hold values from -6 to 6
- w_reduce: bfloat16 [2, 1024, 256], replicated, may hold values from -0.1875 to 0.1875
- w_mix: bfloat16 [2, 256, 256], replicated, may hold values from -0.375 to 0.375
- w_depth: bfloat16 [2, 3, 3, 3, 256], replicated, may hold values from -1.25 to 1.25
- w_expand: bfloat16 [2, 256, 1024], replicated, may hold values from -0.375 to 0.375
- gains_narrow: float32 [2, 2, 256], replicated, may hold values from 0.5 to 1.5
- shifts_narrow: float32 [2, 2, 256], replicated, may hold values from -0.5 to 0.5
- gains_wide: float32 [2, 1024], replicated, may hold values from 0.5 to 1.5
- shifts_wide: float32 [2, 1024], replicated, may hold values from -0.5 to 0.5
Outputs:
- outputs: bfloat16 [64, 8, 4, 32, 1024], P('clip', None, 'ha', 'wa')
- grad_activations: bfloat16 [64, 8, 4, 32, 1024], P('clip', None, 'ha', 'wa')
- grad_w_reduce: float32 [2, 1024, 256], replicated
- grad_w_mix: float32 [2, 256, 256], replicated
- grad_w_depth: float32 [2, 3, 3, 3, 256], replicated
- grad_w_expand: float32 [2, 256, 1024], replicated
- grad_gains_narrow: float32 [2, 2, 256], replicated
- grad_shifts_narrow: float32 [2, 2, 256], replicated
- grad_gains_wide: float32 [2, 1024], replicated
- grad_shifts_wide: float32 [2, 1024], replicated
The draws below stay inside these ranges and needn't reach their ends.
Inputs may be any that keep to these rules, and one draw needn't show every extreme that they name: Each clip's stride is 1, 2 or 4 and its clip has 8 // stride frames; every draw has a stride of 1 and one of 4. `clip_order`: each clip number once.
All inputs are finite; a program needn't handle non-finite values.
Results may differ from the reference program's by a relative error of at most 0.019.
Values may be sent and summed in bfloat16 or wider, within the bound.
A program may use at most 192 MiB of HBM per device.

```python
import jax
import jax.numpy as jnp
from jax import lax

C = 1024
BOT = 256
FRAMES = 8
LAYERS = 2
W = 32
CLIPS = 64
H = 4


def draw_stride(key, part):
    key = jax.random.fold_in(key, 11)
    pick_key, order_key = jax.random.split(key)
    powers = jax.random.randint(pick_key, (CLIPS,), 0, 3)
    values = jnp.left_shift(jnp.ones((CLIPS,), jnp.int32), powers.astype(jnp.int32))
    shuffled = jax.random.permutation(order_key, CLIPS)
    values = values.at[shuffled[0]].set(1)
    values = values.at[shuffled[1]].set(4)
    return values.astype(jnp.int32)


def steps_of(stream_key, dims, shards, smallest, top_value):
    gain = 1.0
    for position, blocks in shards:
        steps = jax.random.uniform(jax.random.fold_in(jax.random.fold_in(stream_key, 6), position), (blocks,), jnp.float32, smallest / len(shards), top_value / len(shards))
        gain = gain * jnp.repeat(jnp.exp(steps), dims[position] // blocks).reshape((-1,) + (1,) * (len(dims) - 1 - position))
    return gain


def centred(stream_key, extent, scale, reach, cuts=(), kind=jnp.bfloat16):
    values = scale * jax.random.normal(stream_key, extent, jnp.float32)
    if cuts:
        values = values * steps_of(stream_key, extent, cuts, -0.22, 0.18)
    return jnp.clip(values, -reach, reach).astype(kind)


def setup_inputs(seed: int = 0) -> dict:
    key_list = jax.random.split(jax.random.key(seed), 13)
    activations = centred(key_list[0], (CLIPS, FRAMES, H, W, C), 1.0, 6.0, ((0, 4), (2, 2), (3, 4)))
    stride = draw_stride(jax.random.fold_in(key_list[12], 71), 0)
    clip_order = jax.random.permutation(key_list[2], CLIPS).astype(jnp.int32)
    cotangent = centred(key_list[3], (CLIPS, FRAMES, H, W, C), 1.0, 6.0, ((0, 4), (2, 2), (3, 4)))
    w_reduce = centred(key_list[4], (LAYERS, C, BOT), C ** -0.5, 0.1875)
    w_mix = centred(key_list[5], (LAYERS, BOT, BOT), BOT ** -0.5, 0.375)
    w_depth = centred(key_list[6], (LAYERS, 3, 3, 3, BOT), 27 ** -0.5, 1.25)
    w_expand = centred(key_list[7], (LAYERS, BOT, C), BOT ** -0.5, 0.375)
    gains_narrow = jnp.clip(jax.random.uniform(key_list[8], (LAYERS, 2, BOT), jnp.float32, 0.5, 1.5), 0.5, 1.5)
    shifts_narrow = jnp.clip(jax.random.uniform(key_list[9], (LAYERS, 2, BOT), jnp.float32, -0.5, 0.5), -0.5, 0.5)
    gains_wide = jnp.clip(jax.random.uniform(key_list[10], (LAYERS, C), jnp.float32, 0.5, 1.5), 0.5, 1.5)
    shifts_wide = jnp.clip(jax.random.uniform(key_list[11], (LAYERS, C), jnp.float32, -0.5, 0.5), -0.5, 0.5)
    return {"activations": activations, "stride": stride, "clip_order": clip_order, "cotangent": cotangent, "w_reduce": w_reduce, "w_mix": w_mix, "w_depth": w_depth, "w_expand": w_expand, "gains_narrow": gains_narrow, "shifts_narrow": shifts_narrow, "gains_wide": gains_wide, "shifts_wide": shifts_wide}


EPSILON = 1e-05

@jax.custom_vjp
def low(v):
    return lax.optimization_barrier(v.astype(jnp.bfloat16)).astype(jnp.float32)

@jax.custom_vjp
def low_back(v):
    return v

def low_keep(v):
    return (low(v), None)

def low_pass(kept, grad):
    return (grad,)

def back_keep(v):
    return (v, None)

def back_low(kept, grad):
    return (low(grad),)
low.defvjp(low_keep, low_pass)
low_back.defvjp(back_keep, back_low)

def silu_act(values):
    return values * jax.nn.sigmoid(values)

def product(operand, weight):
    dims_in = operand.shape
    result = jnp.dot(operand.reshape(-1, dims_in[-1]), weight, precision=lax.Precision.HIGHEST, preferred_element_type=jnp.float32)
    return result.reshape(dims_in[:-1] + (weight.shape[-1],))

def normalize(values, frame_mask, voxel_count, gain_vec, offset):
    average = lax.optimization_barrier(jnp.sum(values * frame_mask, axis=(0, 1, 2, 3))) / voxel_count
    centered = values - average
    spread = lax.optimization_barrier(jnp.sum(centered * centered * frame_mask, axis=(0, 1, 2, 3))) / voxel_count
    return centered * lax.rsqrt(spread + EPSILON) * gain_vec + offset

def stencil(values, kernel):
    frame_len, row_count, col_count = (values.shape[1], values.shape[2], values.shape[3])
    padded = jnp.pad(values, ((0, 0), (1, 1), (1, 1), (1, 1), (0, 0)))
    running = jnp.zeros_like(values)
    for step_t in range(3):
        for step_h in range(3):
            for step_w in range(3):
                window = padded[:, step_t:step_t + frame_len, step_h:step_h + row_count, step_w:step_w + col_count, :]
                running = running + window * kernel[step_t, step_h, step_w]
    return running

def bottleneck(inputs, frame_mask, voxel_count, w_in, w_mid, w_dep, w_out, gain_narrow, shift_narrow, gain_wide, shift_wide):
    reduced = low_back(product(inputs, w_in))
    hidden_one = low(silu_act(normalize(reduced, frame_mask, voxel_count, gain_narrow[0], shift_narrow[0])))
    mixed = low(low_back(product(hidden_one, w_mid)))
    spatial = low_back(stencil(mixed * frame_mask, w_dep))
    hidden_two = low(silu_act(normalize(spatial, frame_mask, voxel_count, gain_narrow[1], shift_narrow[1])))
    widened = low_back(product(hidden_two, w_out))
    return low(silu_act(inputs + normalize(widened, frame_mask, voxel_count, gain_wide, shift_wide)))

def reference(activations, stride, clip_order, cotangent, w_reduce, w_mix, w_depth, w_expand, gains_narrow, shifts_narrow, gains_wide, shifts_wide):
    live = FRAMES // stride[clip_order]
    mask_two = (jnp.arange(FRAMES, dtype=jnp.int32)[None, :] < live[:, None]).astype(jnp.float32)
    frame_mask = mask_two[:, :, None, None, None]
    voxel_count = (jnp.sum(live) * H * W).astype(jnp.float32)
    params = (w_reduce.astype(jnp.float32), w_mix.astype(jnp.float32), w_depth.astype(jnp.float32), w_expand.astype(jnp.float32), gains_narrow, shifts_narrow, gains_wide, shifts_wide)

    def forward(inputs, weights):
        values = inputs
        for block_index in range(LAYERS):
            values = bottleneck(values, frame_mask, voxel_count, weights[0][block_index], weights[1][block_index], weights[2][block_index], weights[3][block_index], weights[4][block_index], weights[5][block_index], weights[6][block_index], weights[7][block_index])
        return values * frame_mask
    output, pullback = jax.vjp(forward, activations.astype(jnp.float32), params)
    grad_in, gradients = pullback(cotangent.astype(jnp.float32))
    return (output.astype(jnp.bfloat16), grad_in.astype(jnp.bfloat16), gradients[0], gradients[1], gradients[2], gradients[3], gradients[4], gradients[5], gradients[6], gradients[7])
```

```python
import functools
import math

import jax
import jax.numpy as jnp
from jax import lax
from jax.experimental import pallas as pl
from jax.experimental.pallas import tpu as pltpu
from jax.sharding import PartitionSpec as P

EPSILON = 1e-05
AXES = ("ha", "wa", "clip")
MESH = pl.DeviceIdType.MESH
F32 = jnp.float32
BF16 = jnp.bfloat16
ROWS = 2
COLS = 8
SPOT = ROWS * COLS
CH = 8
LANES = 128


def dot(a, b):
    return jnp.dot(a, b, preferred_element_type=F32)


def dot_first(a, b):
    return lax.dot_general(a, b, (((0,), (0,)), ((), ())), preferred_element_type=F32)


def sigmoid(v):
    return jax.nn.sigmoid(v)


def slope_of(z):
    s = sigmoid(z)
    return s * (1.0 + z * (1.0 - s))


def get(ref, spot):
    return jnp.concatenate([ref[lb, spot, :] for lb in range(ref.shape[0])], axis=-1)


def put(ref, spot, value):
    for lb in range(ref.shape[0]):
        ref[lb, spot, :] = value[:, lb * LANES : (lb + 1) * LANES]


def fold8(v):
    return jnp.sum(v.reshape(v.shape[0] // 8, 8, v.shape[1]), axis=0)


def split_dot(v, w):
    high = v.astype(BF16)
    low = (v - high.astype(F32)).astype(BF16)
    return dot(high, w) + dot(low, w)


def padded_2(block, sides, width):
    for axis, dim in sides:
        count = lax.axis_size(axis)
        forward = [(i, i + 1) for i in range(count - 1)]
        backward = [(target, source) for source, target in forward]
        low = lax.ppermute(
            lax.slice_in_dim(block, block.shape[dim] - width, None, axis=dim), axis, forward
        )
        high = lax.ppermute(lax.slice_in_dim(block, 0, width, axis=dim), axis, backward)
        block = jnp.concatenate([low, block, high], axis=dim)
    return block


def silu_act(values):
    return values * jax.nn.sigmoid(values)


def silu_slope(values):
    sigmoid_v = jax.nn.sigmoid(values)
    return sigmoid_v * (1.0 + values * (1.0 - sigmoid_v))


def project(operand, weight):
    dims_in = operand.shape
    result = jnp.dot(operand.reshape(-1, dims_in[-1]), weight, preferred_element_type=jnp.float32)
    return result.reshape(dims_in[:-1] + (weight.shape[-1],))


def project_back(upstream, weight):
    dims_in = upstream.shape
    result = lax.dot_general(
        upstream.reshape(-1, dims_in[-1]),
        weight,
        (((1,), (1,)), ((), ())),
        preferred_element_type=jnp.float32,
    )
    return result.reshape(dims_in[:-1] + (weight.shape[0],))


def outer_sum(operand, upstream):
    return lax.dot_general(
        operand.reshape(-1, operand.shape[-1]),
        upstream.reshape(-1, upstream.shape[-1]),
        (((0,), (0,)), ((), ())),
        preferred_element_type=jnp.float32,
    )


def moments(values, frame_mask, voxel_count):
    sum_axes = (0, 1, 2, 3)
    average = (
        lax.psum(jnp.sum(values * frame_mask, axis=sum_axes), ("ha", "wa", "clip")) / voxel_count
    )
    centered = values - average
    spread = (
        lax.psum(jnp.sum(centered * centered * frame_mask, axis=sum_axes), ("ha", "wa", "clip"))
        / voxel_count
    )
    inverse_std = lax.rsqrt(spread + EPSILON)
    return ((values - average) * inverse_std, inverse_std)


def norm_back(upstream, normed, inverse_std, gain_vec, frame_mask, voxel_count):
    sum_axes = (0, 1, 2, 3)
    grad_gain, grad_shift = lax.psum(
        (jnp.sum(upstream * normed, axis=sum_axes), jnp.sum(upstream, axis=sum_axes)),
        ("ha", "wa", "clip"),
    )
    result = (
        inverse_std
        * gain_vec
        * (upstream - frame_mask * (grad_shift + normed * grad_gain) / voxel_count)
    )
    return (result, grad_gain, grad_shift)


def pad_frames(values):
    return jnp.pad(values, ((0, 0), (1, 1), (0, 0), (0, 0), (0, 0)))


def forward_rim(values):
    return pad_frames(padded_2(values, (("ha", 2), ("wa", 3)), 1))


def backward_rim(values):
    return pad_frames(padded_2(values, (("ha", 2), ("wa", 3)), 1))


def depth_taps(padded, kernel, dims_out, flipped):
    frame_len, row_count, col_count = (dims_out[1], dims_out[2], dims_out[3])
    running = jnp.zeros(dims_out, jnp.float32)
    for step_t in range(3):
        for step_h in range(3):
            for step_w in range(3):
                if flipped:
                    start_t, start_h, start_w = (2 - step_t, 2 - step_h, 2 - step_w)
                else:
                    start_t, start_h, start_w = (step_t, step_h, step_w)
                window = padded[
                    :,
                    start_t : start_t + frame_len,
                    start_h : start_h + row_count,
                    start_w : start_w + col_count,
                    :,
                ]
                running = running + window.astype(jnp.float32) * kernel[
                    step_t, step_h, step_w
                ].astype(jnp.float32)
    return running


def kernel_grad(padded, upstream):
    frame_len, row_count, col_count = (upstream.shape[1], upstream.shape[2], upstream.shape[3])
    upstream_f = upstream.astype(jnp.float32)
    entries = []
    for step_t in range(3):
        for step_h in range(3):
            for step_w in range(3):
                window = padded[
                    :,
                    step_t : step_t + frame_len,
                    step_h : step_h + row_count,
                    step_w : step_w + col_count,
                    :,
                ]
                entries.append(jnp.sum(window.astype(jnp.float32) * upstream_f, axis=(0, 1, 2, 3)))
    return jnp.stack(entries).reshape(3, 3, 3, upstream.shape[-1])


def block_forward(
    inputs,
    frame_mask,
    mask_low,
    voxel_count,
    w_in,
    w_mid,
    w_dep,
    w_out,
    gain_narrow,
    shift_narrow,
    gain_wide,
    shift_wide,
):
    reduced = project(inputs, w_in)
    normed_one, inverse_one = moments(reduced, frame_mask, voxel_count)
    before_one = normed_one * gain_narrow[0] + shift_narrow[0]
    hidden_one = silu_act(before_one).astype(jnp.bfloat16)
    mixed_out = project(hidden_one, w_mid).astype(jnp.bfloat16) * mask_low
    padded = forward_rim(mixed_out)
    spatial = depth_taps(padded, w_dep, mixed_out.shape, False)
    normed_two, inverse_two = moments(spatial, frame_mask, voxel_count)
    before_two = normed_two * gain_narrow[1] + shift_narrow[1]
    hidden_two = silu_act(before_two).astype(jnp.bfloat16)
    widened = project(hidden_two, w_out)
    normed_three, inverse_three = moments(widened, frame_mask, voxel_count)
    summed = inputs.astype(jnp.float32) + normed_three * gain_wide + shift_wide
    output = silu_act(summed).astype(jnp.bfloat16)
    saved_state = (
        inputs,
        normed_one,
        inverse_one,
        before_one,
        hidden_one,
        padded,
        normed_two,
        inverse_two,
        before_two,
        hidden_two,
        normed_three,
        inverse_three,
        summed,
    )
    return (output, saved_state)


def block_backward(
    upstream,
    saved_state,
    frame_mask,
    voxel_count,
    w_in,
    w_mid,
    w_dep,
    w_out,
    gain_narrow,
    gain_wide,
):
    (
        inputs,
        normed_one,
        inverse_one,
        before_one,
        hidden_one,
        padded,
        normed_two,
        inverse_two,
        before_two,
        hidden_two,
        normed_three,
        inverse_three,
        summed,
    ) = saved_state
    grad_summed = upstream * silu_slope(summed)
    grad_widened, gain_three, shift_three = norm_back(
        grad_summed, normed_three, inverse_three, gain_wide, frame_mask, voxel_count
    )
    grad_widened = grad_widened.astype(jnp.bfloat16)
    grad_out_w = outer_sum(hidden_two, grad_widened)
    grad_two = project_back(grad_widened, w_out) * silu_slope(before_two)
    grad_spatial, gain_two, shift_two = norm_back(
        grad_two, normed_two, inverse_two, gain_narrow[1], frame_mask, voxel_count
    )
    grad_spatial = grad_spatial.astype(jnp.bfloat16)
    grad_dep_w = kernel_grad(padded, grad_spatial)
    grad_padded = backward_rim(grad_spatial)
    grad_mixed = (depth_taps(grad_padded, w_dep, grad_spatial.shape, True) * frame_mask).astype(
        jnp.bfloat16
    )
    grad_mid_w = outer_sum(hidden_one, grad_mixed)
    grad_one = project_back(grad_mixed, w_mid) * silu_slope(before_one)
    grad_reduced, gain_one, shift_one = norm_back(
        grad_one, normed_one, inverse_one, gain_narrow[0], frame_mask, voxel_count
    )
    grad_reduced = grad_reduced.astype(jnp.bfloat16)
    grad_in_w = outer_sum(inputs, grad_reduced)
    grad_inputs = grad_summed + project_back(grad_reduced, w_in)
    weight_parts = (grad_in_w, grad_mid_w, grad_dep_w, grad_out_w)
    norm_parts = (
        jnp.stack([gain_one, gain_two]),
        jnp.stack([shift_one, shift_two]),
        gain_three,
        shift_three,
    )
    return (grad_inputs, weight_parts, norm_parts)


def plain_body(
    activations,
    stride,
    clip_order,
    cotangent,
    w_reduce,
    w_mix,
    w_depth,
    w_expand,
    gains_narrow,
    shifts_narrow,
    gains_wide,
    shifts_wide,
):
    clips_here = activations.shape[0]
    frame_len = activations.shape[1]
    all_clips = stride.shape[0]
    slot_ids = lax.axis_index("clip") * clips_here + jnp.arange(clips_here, dtype=jnp.int32)
    numbers = jnp.arange(all_clips, dtype=jnp.int32)
    slot_clip = jnp.sum(
        jnp.where(slot_ids[:, None] == numbers[None, :], clip_order[None, :], 0), axis=1
    )
    slot_stride = jnp.sum(
        jnp.where(slot_clip[:, None] == numbers[None, :], stride[None, :], 0), axis=1
    )
    live_frames = frame_len // slot_stride
    mask_two = (jnp.arange(frame_len, dtype=jnp.int32)[None, :] < live_frames[:, None]).astype(
        jnp.float32
    )
    frame_mask = mask_two[:, :, None, None, None]
    mask_low = frame_mask.astype(jnp.bfloat16)
    grid_cells = (
        activations.shape[2] * lax.axis_size("ha") * activations.shape[3] * lax.axis_size("wa")
    )
    voxel_count = jnp.sum(frame_len // stride).astype(jnp.float32) * grid_cells
    depth_count = w_reduce.shape[0]
    values = activations
    saved_list = []
    for block_index in range(depth_count):
        values, saved_state = block_forward(
            values,
            frame_mask,
            mask_low,
            voxel_count,
            w_reduce[block_index],
            w_mix[block_index],
            w_depth[block_index],
            w_expand[block_index],
            gains_narrow[block_index],
            shifts_narrow[block_index],
            gains_wide[block_index],
            shifts_wide[block_index],
        )
        saved_list.append(saved_state)
    outputs = values * mask_low
    upstream = cotangent.astype(jnp.float32) * frame_mask
    weight_list = [None] * depth_count
    norm_list = [None] * depth_count
    for block_index in reversed(range(depth_count)):
        upstream, weight_parts, norm_parts = block_backward(
            upstream,
            saved_list[block_index],
            frame_mask,
            voxel_count,
            w_reduce[block_index],
            w_mix[block_index],
            w_depth[block_index],
            w_expand[block_index],
            gains_narrow[block_index],
            gains_wide[block_index],
        )
        weight_list[block_index] = weight_parts
        norm_list[block_index] = norm_parts
    stacked = tuple(
        (
            jnp.stack([weight_list[block_index][member] for block_index in range(depth_count)])
            for member in range(4)
        )
    )
    stacked = lax.psum((stacked[0], stacked[1], stacked[2], stacked[3]), ("ha", "wa", "clip"))
    norm_stacked = tuple(
        (
            jnp.stack([norm_list[block_index][member] for block_index in range(depth_count)])
            for member in range(4)
        )
    )
    return (
        outputs,
        upstream.astype(jnp.bfloat16),
        stacked[0],
        stacked[1],
        stacked[2],
        stacked[3],
        norm_stacked[0],
        norm_stacked[1],
        norm_stacked[2],
        norm_stacked[3],
    )


def mega(sizes, frames, raw_frames, layers, wide, narrow, seg_rows, *refs):
    (
        idx_ref, flag_ref, cnt_ref, x_hbm, cot_hbm, wred_ref, wmix_ref, wdep_ref, wexp_ref,
        gn_ref, sn_ref, gw_ref, sw_ref,
        y_ref, gx_ref, owr_ref, owm_ref, owd_ref, owe_ref, ogn_ref, osn_ref, ogw_ref, osw_ref,
        raw, xc, x1, s0, u, red, h1, mown, spat, h2, g2, gm, mtop, mbot, mside,
        vm8, wtap, hu, tgw, gram, wtr, wtb, wmt,
        row_send, col_send, top_in, bot_in, side_in, top_sp, bot_sp, side_sp,
        nar_a, nar_b, wid_a, wid_b, wb, rs1, rs2, ag1, ag2,
        load_sem, ar_send, ar_recv, halo_send, halo_recv, wg_send, wg_recv,
    ) = refs
    n = frames
    rows = n * SPOT
    na, nw, nc = sizes
    ne = nw * nc
    me = {a: lax.axis_index(a) for a in AXES}
    my_a = me["ha"]
    my_e = me["wa"] * nc + me["clip"]
    exists = {
        (-1, 0): my_a > 0, (1, 0): my_a < na - 1,
    }
    for dw, here in ((-1, me["wa"] > 0), (1, me["wa"] < nw - 1)):
        exists[(0, dw)] = here
        for dh in (-1, 1):
            exists[(dh, dw)] = jnp.logical_and(exists[(dh, 0)], here)

    def at(ha=None, wa=None, clip=None):
        return (
            me["ha"] if ha is None else ha,
            me["wa"] if wa is None else wa,
            me["clip"] if clip is None else clip,
        )

    def a_peer(k):
        return at(ha=lax.rem(my_a + k, na))

    def e_peer(k):
        p = lax.rem(my_e + k, ne)
        return at(wa=p // nc, clip=lax.rem(p, nc))

    barrier = pltpu.get_barrier_semaphore()

    load = pltpu.make_async_copy(x_hbm, raw, load_sem.at[0])
    load.start()

    def greet_a(k, c):
        pl.semaphore_signal(barrier, inc=1, device_id=a_peer(k), device_id_type=MESH)
        return c

    def greet_e(k, c):
        pl.semaphore_signal(barrier, inc=1, device_id=e_peer(k), device_id_type=MESH)
        return c

    lax.fori_loop(1, na, greet_a, 0)
    lax.fori_loop(1, ne, greet_e, 0)
    expected = na - 1 + ne - 1
    for dh in (-1, 1):
        for dw in (-1, 1):
            ok = exists[(dh, dw)]
            expected = expected + ok.astype(jnp.int32)

            @pl.when(ok)
            def _():
                pl.semaphore_signal(
                    barrier, inc=1, device_id=at(ha=my_a + dh, wa=me["wa"] + dw), device_id_type=MESH
                )

    def set_mask(f, c):
        vm8[pl.ds(pl.multiple_of(f * 8, 8), 8), :] = jnp.full((8, LANES), flag_ref[0, f], F32)
        return c

    lax.fori_loop(0, n, set_mask, 0)
    for l in range(layers):
        taps = wdep_ref[l].astype(F32)
        for i in range(27):
            wtap[l, i] = jnp.broadcast_to(taps[i : i + 1], (8, narrow))
        wtr[l] = wred_ref[l].T
        wtb[l] = wexp_ref[l].T
        wmt[l] = wmix_ref[l].T
        for lb in range(narrow // LANES):
            mown[l, lb, 0:SPOT] = jnp.zeros((SPOT, LANES), F32)
            mown[l, lb, SPOT + rows : SPOT + rows + SPOT] = jnp.zeros((SPOT, LANES), F32)
    mtop[...] = jnp.zeros_like(mtop)
    mbot[...] = jnp.zeros_like(mbot)
    mside[...] = jnp.zeros_like(mside)

    pl.semaphore_wait(barrier, expected)

    total_count = cnt_ref[2 * nc]
    total_inv = cnt_ref[2 * nc + 1]
    my_count = cnt_ref[me["clip"]]
    my_count_inv = cnt_ref[nc + me["clip"]]

    def reduce_start(number, buf_a, buf_b, slot, value, moments):
        if na > 1:
            buf_a[slot, my_a] = value

            def send_a(k, c):
                pltpu.make_async_remote_copy(
                    src_ref=buf_a.at[slot, my_a], dst_ref=buf_a.at[slot, my_a],
                    send_sem=ar_send.at[number, 0], recv_sem=ar_recv.at[number, 0],
                    device_id=a_peer(k), device_id_type=MESH,
                ).start()
                return c

            lax.fori_loop(1, na, send_a, 0)
            part = buf_a.at[slot, pl.ds(0, na - 1)]
            pltpu.make_async_copy(part, part, ar_recv.at[number, 0]).wait()
            pltpu.make_async_copy(part, part, ar_send.at[number, 0]).wait()
            got = buf_a[slot]
            total = jnp.sum(got, axis=0)
            if moments:
                off = got[:, 0:1] - (total[0:1] * (1.0 / na))[None]
                extra = jnp.sum(off * off, axis=0) * my_count_inv
                total = jnp.concatenate([total[0:1], total[1:2] + extra], axis=0)
            value = total
        buf_b[slot, my_e] = value

        def send_e(k, c):
            pltpu.make_async_remote_copy(
                src_ref=buf_b.at[slot, my_e], dst_ref=buf_b.at[slot, my_e],
                send_sem=ar_send.at[number, 1], recv_sem=ar_recv.at[number, 1],
                device_id=e_peer(k), device_id_type=MESH,
            ).start()
            return c

        lax.fori_loop(1, ne, send_e, 0)

    def reduce_finish(number, buf_b, slot, moments):
        part = buf_b.at[slot, pl.ds(0, ne - 1)]
        pltpu.make_async_copy(part, part, ar_recv.at[number, 1]).wait()
        pltpu.make_async_copy(part, part, ar_send.at[number, 1]).wait()
        got = buf_b[slot]
        total = jnp.sum(got, axis=0)
        if not moments:
            return total[0:1], total[1:2]
        average = total[0:1] * total_inv
        second = total[1:2]
        for j in range(ne):
            count = cnt_ref[j % nc] * na
            inv = cnt_ref[nc + j % nc] * (1.0 / na)
            off = got[j, 0:1] - average * count
            second = second + off * off * inv
        return average, lax.rsqrt(second * total_inv + EPSILON)

    def local_moments(first, square):
        total = jnp.sum(first, axis=0, keepdims=True)
        second = jnp.sum(square, axis=0, keepdims=True) - total * total * my_count_inv
        return jnp.concatenate([total, second], axis=0)

    def plain_pair(first, second):
        return jnp.concatenate(
            [jnp.sum(first, axis=0, keepdims=True), jnp.sum(second, axis=0, keepdims=True)], axis=0
        )

    def rim_list(r_send, c_send, top, bot, side):
        return [
            (1, 0, r_send.at[1], top), (-1, 0, r_send.at[0], bot),
            (0, 1, c_send.at[1], side.at[pl.ds(1, 2)]), (0, -1, c_send.at[0], side.at[pl.ds(5, 2)]),
            (1, 1, c_send.at[1, 1], side.at[0]), (-1, 1, c_send.at[1, 0], side.at[3]),
            (1, -1, c_send.at[0, 1], side.at[4]), (-1, -1, c_send.at[0, 0], side.at[7]),
        ]

    def rim_copy(number, k, item):
        dh, dw, src, dst = item
        return pltpu.make_async_remote_copy(
            src_ref=src, dst_ref=dst, send_sem=halo_send.at[number, k], recv_sem=halo_recv.at[number, k],
            device_id=at(ha=my_a + dh, wa=me["wa"] + dw), device_id_type=MESH,
        )

    def rim_start(number, items):
        for k, item in enumerate(items):
            @pl.when(exists[(item[0], item[1])])
            def _():
                rim_copy(number, k, item).start()

    def rim_sent(number, items):
        for k, item in enumerate(items):
            @pl.when(exists[(item[0], item[1])])
            def _():
                rim_copy(number, k, item).wait_send()

    def rim_arrived(number, items):
        for k, item in enumerate(items):
            @pl.when(exists[(-item[0], -item[1])])
            def _():
                rim_copy(number, k, item).wait_recv()

    def fill_send(source, base):
        def rows_body(c, carry):
            tile = get(source, pl.ds(pl.multiple_of(base + c * CH * SPOT, SPOT), CH * SPOT))
            tile = tile.reshape(CH, ROWS, COLS, narrow)
            spot = pl.ds(pl.multiple_of(c * CH * COLS, CH * COLS), CH * COLS)
            for h in range(ROWS):
                row_send[h, spot, :] = tile[:, h].reshape(CH * COLS, narrow).astype(BF16)
            return carry

        lax.fori_loop(0, n // CH, rows_body, 0)
        for h in range(ROWS):
            for side, col in ((0, 0), (1, COLS - 1)):
                col_send[side, h] = get(source, pl.ds(base + h * COLS + col, n, stride=SPOT)).astype(BF16)

    def over_rim(apply):
        half = CH * COLS
        for key, which in ((-1, 0), (1, 1)):
            @pl.when(exists[(key, 0)])
            def _():
                dst = (mtop, mbot)[which]

                def body(c, carry):
                    spot = pl.ds(pl.multiple_of(c * half, half), half)
                    put(dst, spot, apply(
                        lambda: (top_in, bot_in)[which][spot, :].astype(F32),
                        lambda l: (top_sp, bot_sp)[which][l, spot, :].astype(F32),
                    ))
                    return carry

                lax.fori_loop(0, n // CH, body, 0)
        for dw, base in ((-1, 0), (1, 4)):
            for r in range(4):
                dh = -1 if r == 0 else (1 if r == 3 else 0)

                @pl.when(exists[(dh, dw)])
                def _():
                    put(mside, pl.ds(base + r, n, stride=8), apply(
                        lambda: side_in[base + r].astype(F32), lambda l: side_sp[l, base + r].astype(F32)
                    ))

    row_id = lax.broadcasted_iota(jnp.int32, (8, LANES), 0)

    def shifted(own, own_base, f, lb):
        side = mside[lb, pl.ds(pl.multiple_of(f * 8, 8), 8), :]
        start = own_base + f * SPOT
        lines = [
            mtop[lb, pl.ds(pl.multiple_of(f * 8, 8), 8), :],
            own[lb, pl.ds(pl.multiple_of(start, 8), 8), :],
            own[lb, pl.ds(pl.multiple_of(start + 8, 8), 8), :],
            mbot[lb, pl.ds(pl.multiple_of(f * 8, 8), 8), :],
        ]
        out = []
        for r, v in enumerate(lines):
            left = jnp.where(row_id == 0, jnp.broadcast_to(side[r : r + 1], (8, LANES)), pltpu.roll(v, 1, 0))
            right = jnp.where(row_id == 7, jnp.broadcast_to(side[4 + r : 5 + r], (8, LANES)), pltpu.roll(v, 7, 0))
            out.append((left, v, right))
        return out

    def tap_sum(grid, l, lanes, a, flip):
        res = []
        for h in range(ROWS):
            total = None
            for b in range(3):
                for e in range(3):
                    i = (a * 3 + b) * 3 + e
                    term = grid[h + b][e] * wtap[l, 26 - i if flip else i, :, lanes]
                    total = term if total is None else total + term
            res.append(total)
        return res

    def vmask(c):
        m = vm8[pl.ds(pl.multiple_of(c * CH * 8, CH * 8), CH * 8), :]
        m = jnp.broadcast_to(m.reshape(CH, 1, 8, LANES), (CH, ROWS, 8, LANES)).reshape(CH * SPOT, LANES)
        return jnp.concatenate([m] * (narrow // LANES), axis=1)

    def chunk(c):
        return pl.ds(pl.multiple_of(c * CH * SPOT, CH * SPOT), CH * SPOT)

    def chunk_off(c, base):
        return pl.ds(pl.multiple_of(base + c * CH * SPOT, SPOT), CH * SPOT)

    zero8 = jnp.zeros((8, narrow), F32)
    blocks = [pl.ds(k * narrow, narrow) for k in range(wide // narrow)]
    steps = n // CH
    scal = {}

    def reduce_phase(l):
        source = xc if l == 0 else x1

        def body(c, carry):
            first, square = carry
            if l == 0:
                for j in range(CH):
                    f = c * CH + j
                    tile = raw[idx_ref[f]]
                    xc[pl.ds(pl.multiple_of(f * SPOT, SPOT), SPOT), :] = (
                        tile.astype(F32) * flag_ref[0, f]
                    ).astype(BF16)
            r = dot(source[chunk(c), :], wred_ref[l])
            put(red.at[l], chunk(c), r)
            return first + fold8(r), square + fold8(r * r)

        first, square = lax.fori_loop(0, steps, body, (zero8, zero8))
        fill_send(red.at[l], 0)
        rim_start(l, rims)
        reduce_start(3 * l, nar_a, nar_b, 2 * l, local_moments(first, square), True)

    def mix_phase(l):
        average, inv = reduce_finish(3 * l, nar_b, 2 * l, True)
        scale = gn_ref[l, 0:1] * inv
        shift = sn_ref[l, 0:1] - average * scale
        scal["one", l] = (average, inv, scale, shift)

        def body(c, carry):
            z = get(red.at[l], chunk(c)) * scale + shift
            h = (z * sigmoid(z)).astype(BF16)
            h1[l, chunk(c), :] = h
            put(mown.at[l], chunk_off(c, SPOT), dot(h, wmix_ref[l]))
            return carry

        lax.fori_loop(0, steps, body, 0)
        rim_arrived(l, rims)

        def apply(arrived, second):
            z = arrived() * scale + shift
            return dot((z * sigmoid(z)).astype(BF16), wmix_ref[l])

        over_rim(apply)
        rim_sent(l, rims)

    def spatial_phase(l):
        stats = []
        for lb in range(narrow // LANES):
            lanes = pl.ds(lb * LANES, LANES)

            def body(f, carry):
                cur, nxt, first, square = carry
                grid = shifted(mown.at[l], SPOT, f, lb)
                here = flag_ref[1, f]
                t2 = tap_sum(grid, l, lanes, 2, False)
                t1 = tap_sum(grid, l, lanes, 1, False)
                t0 = tap_sum(grid, l, lanes, 0, False)
                alive = flag_ref[2, f]
                for h in range(ROWS):
                    done = (cur[h] + here * t2[h]) * alive
                    spat[l, lb, pl.ds(pl.multiple_of(f * SPOT + 8 * h, 8), 8), :] = done
                    first = first + done
                    square = square + done * done
                cur = tuple(t1[h] + here * nxt[h] for h in range(ROWS))
                return cur, tuple(t0), first, square

            z = jnp.zeros((8, LANES), F32)
            cur, nxt, first, square = lax.fori_loop(0, n, body, ((z, z), (z, z), z, z))
            for h in range(ROWS):
                done = cur[h] * flag_ref[2, n]
                spat[l, lb, rows + 8 * h : rows + 8 * h + 8, :] = done
                first = first + done
                square = square + done * done
            stats.append((first, square))
        first = jnp.concatenate([s[0] for s in stats], axis=1)
        square = jnp.concatenate([s[1] for s in stats], axis=1)
        reduce_start(3 * l + 1, nar_a, nar_b, 2 * l + 1, local_moments(first, square), True)
        fill_send(spat.at[l], SPOT)
        rim_start(layers + l, rims_sp[l])

    def hidden_phase(l):
        average, inv = reduce_finish(3 * l + 1, nar_b, 2 * l + 1, True)
        scale = gn_ref[l, 1:2] * inv
        shift = sn_ref[l, 1:2] - average * scale
        scal["two", l] = (average, inv, scale, shift)

        def body(c, first):
            z = get(spat.at[l], chunk_off(c, SPOT)) * scale + shift
            h = z * sigmoid(z) * vmask(c)
            low = h.astype(BF16)
            h2[l, chunk(c), :] = low
            return first + fold8(low.astype(F32))

        first = lax.fori_loop(0, steps, body, zero8)
        g = dot_first(h2[l], h2[l])
        gram[l] = g
        high = g.astype(BF16)
        low = (g - high.astype(F32)).astype(BF16)
        t = dot(high, wexp_ref[l]) + dot(low, wexp_ref[l])
        tgw[l] = t
        square = jnp.sum(t * wexp_ref[l].astype(F32), axis=0, keepdims=True)
        hsum = jnp.sum(first, axis=0, keepdims=True)
        scal["hsum", l] = hsum
        both = split_dot(jnp.broadcast_to(hsum, (8, narrow)), wexp_ref[l])[0:1]
        second = square - both * both * my_count_inv
        reduce_start(3 * l + 2, wid_a, wid_b, l, jnp.concatenate([both, second], axis=0), True)
        rim_sent(layers + l, rims_sp[l])

    def widen_phase(l):
        average, inv = reduce_finish(3 * l + 2, wid_b, l, True)
        scale = gw_ref[l : l + 1] * inv
        shift = sw_ref[l : l + 1] - average * scale
        scal["wide", l] = (average, inv, scale, shift)
        source = xc if l == 0 else x1
        last = l == layers - 1

        def body(c, sums):
            out = []
            hid = h2[l, chunk(c), :]
            mask = vmask(c)
            for k, blk in enumerate(blocks):
                cut = slice(k * narrow, (k + 1) * narrow)
                w = dot(hid, wexp_ref[l, :, blk])
                summed = source[chunk(c), blk].astype(F32) + (w * scale[:, cut] + shift[:, cut])
                s = sigmoid(summed)
                y = summed * s
                if not last:
                    x1[chunk(c), blk] = (y * mask).astype(BF16)
                    s0[chunk(c), blk] = summed.astype(BF16)
                else:
                    g = jnp.concatenate([raw[idx_ref[c * CH + j], :, blk] for j in range(CH)], axis=0)
                    raw[pl.ds(c * CH, CH), :, blk] = y.astype(BF16).reshape(CH, SPOT, narrow)
                    up = g.astype(F32) * (s * (1.0 + summed * (1.0 - s))) * mask
                    low = up.astype(BF16)
                    u[chunk(c), blk] = low
                    out.append(sums[k] + fold8(low.astype(F32)))
            return tuple(out)

        return lax.fori_loop(0, steps, body, tuple(zero8 for _ in blocks) if last else ())

    def back_wide(l, sums):
        total = jnp.concatenate([jnp.sum(s, axis=0, keepdims=True) for s in sums], axis=1)
        second = []
        for blk in blocks:
            part = dot_first(h2[l], u[:, blk])
            hu[:, blk] = part
            second.append(jnp.sum(part * wexp_ref[l, :, blk].astype(F32), axis=0, keepdims=True))
        second = jnp.concatenate(second, axis=1)
        reduce_start(
            3 * layers + 3 * l, wid_a, wid_b, layers + l, jnp.concatenate([total, second], axis=0), False
        )

    def back_expand(l):
        gshift, gsec = reduce_finish(3 * layers + 3 * l, wid_b, layers + l, False)
        average, inv, scale, _ = scal["wide", l]
        ggain = inv * (gsec - average * gshift)
        ogw_ref[l : l + 1] = ggain
        osw_ref[l : l + 1] = gshift
        drift = inv * ggain * total_inv
        weight = wexp_ref[l].astype(F32)
        awt = (weight * scale).T.astype(BF16)
        mx = dot((weight * (scale * drift)).astype(BF16), wtb[l])
        base = scale * (gshift * total_inv - average * drift)
        const = split_dot(jnp.broadcast_to(base, (8, wide)), wtb[l])[0:1]
        mx = mx.astype(BF16)
        wtb[l] = awt
        _, _, scale2, shift2 = scal["two", l]
        avg2, inv2, _, _ = scal["two", l]

        def body(c, carry):
            first, square = carry
            p = dot(u[chunk(c), :], wtb[l]) - dot(h2[l, chunk(c), :], mx) - const
            sp = get(spat.at[l], chunk_off(c, SPOT))
            g = p * slope_of(sp * scale2 + shift2) * vmask(c)
            put(g2, chunk(c), g)
            normed = (sp - avg2) * inv2
            return first + fold8(g), square + fold8(g * normed)

        first, square = lax.fori_loop(0, steps, body, (zero8, zero8))
        fill_send(g2, 0)
        rim_start(2 * layers + l, rims)
        reduce_start(
            3 * layers + 3 * l + 1, nar_a, nar_b, 2 * layers + 2 * l, plain_pair(first, square), False
        )
        hcol = jnp.broadcast_to(scal["hsum", l], (8, narrow)).T[:, 0:1]
        grad = scale * (
            hu[...] - hcol * (gshift * total_inv - average * drift) - tgw[l] * drift
        )
        for k in range(wide // narrow):
            wb[l, wide + k * narrow : wide + (k + 1) * narrow, :] = grad[
                :, k * narrow : (k + 1) * narrow
            ].astype(BF16)

    def back_spatial(l):
        gshift, ggain = reduce_finish(3 * layers + 3 * l + 1, nar_b, 2 * layers + 2 * l, False)
        ogn_ref[l, 1:2] = ggain
        osn_ref[l, 1:2] = gshift
        avg2, inv2, scale2, _ = scal["two", l]
        a_u = scale2
        a_s = scale2 * inv2 * ggain * total_inv
        a_c = scale2 * gshift * total_inv - a_s * avg2

        def body(c, carry):
            put(g2, chunk(c), a_u * get(g2, chunk(c)) - a_s * get(spat.at[l], chunk_off(c, SPOT)) - a_c)
            return carry

        lax.fori_loop(0, steps, body, 0)
        rim_arrived(2 * layers + l, rims)
        rim_arrived(layers + l, rims_sp[l])
        over_rim(lambda arrived, second: a_u * arrived() - a_s * second(l) - a_c)
        rim_sent(2 * layers + l, rims)

        for lb in range(narrow // LANES):
            lanes = pl.ds(lb * LANES, LANES)

            def body(f, carry):
                cur, nxt, grads = carry
                grid = shifted(g2, 0, f, lb)
                here = flag_ref[1, f]
                after = flag_ref[1, f + 1]
                live = flag_ref[0, f]
                t2 = tap_sum(grid, l, lanes, 2, True)
                t1 = tap_sum(grid, l, lanes, 1, True)
                t0 = tap_sum(grid, l, lanes, 0, True)
                alive = flag_ref[2, f]
                done = [(cur[h] + here * t2[h]) * alive for h in range(ROWS)]
                spat[l, lb, pl.ds(pl.multiple_of(f * SPOT, SPOT), SPOT), :] = jnp.concatenate(done, axis=0)
                grads = list(grads)
                for a, flag in ((0, here), (1, live), (2, after)):
                    for h in range(ROWS):
                        m = flag * mown[l, lb, pl.ds(pl.multiple_of((f + a) * SPOT + 8 * h, 8), 8), :]
                        for b in range(3):
                            for e in range(3):
                                i = (a * 3 + b) * 3 + e
                                grads[i] = grads[i] + m * grid[h + 2 - b][2 - e]
                cur = tuple(t1[h] + here * nxt[h] for h in range(ROWS))
                return cur, tuple(t0), tuple(grads)

            z = jnp.zeros((8, LANES), F32)
            cur, nxt, grads = lax.fori_loop(0, n, body, ((z, z), (z, z), tuple(z for _ in range(27))))
            spat[l, lb, rows : rows + SPOT, :] = jnp.concatenate(
                [cur[h] * flag_ref[2, n] for h in range(ROWS)], axis=0
            )
            folded = [jnp.sum(g, axis=0, keepdims=True) for g in grads]
            folded += [jnp.zeros((1, LANES), F32)] * 5
            wb[l, 2 * wide + narrow : 2 * wide + narrow + 32, lanes] = jnp.concatenate(folded, axis=0).astype(BF16)

        avg1, inv1, scale1, shift1 = scal["one", l]

        def body2(c, carry):
            first, square = carry
            low = get(spat.at[l], chunk_off(c, SPOT)).astype(BF16)
            gm[chunk(c), :] = low
            r = get(red.at[l], chunk(c))
            g = dot(low, wmt[l]) * slope_of(r * scale1 + shift1)
            put(g2, chunk(c), g)
            return first + fold8(g), square + fold8(g * ((r - avg1) * inv1))

        first, square = lax.fori_loop(0, steps, body2, (zero8, zero8))
        reduce_start(
            3 * layers + 3 * l + 2, nar_a, nar_b, 2 * layers + 2 * l + 1, plain_pair(first, square), False
        )
        wb[l, 2 * wide : 2 * wide + narrow, :] = dot_first(h1[l], gm[...]).astype(BF16)

    def back_reduce(l):
        gshift, ggain = reduce_finish(3 * layers + 3 * l + 2, nar_b, 2 * layers + 2 * l + 1, False)
        ogn_ref[l, 0:1] = ggain
        osn_ref[l, 0:1] = gshift
        avg1, inv1, scale1, _ = scal["one", l]
        a_u = scale1
        a_s = scale1 * inv1 * ggain * total_inv
        a_c = scale1 * gshift * total_inv - a_s * avg1

        def body(c, sums):
            gr = (a_u * get(g2, chunk(c)) - a_s * get(red.at[l], chunk(c)) - a_c) * vmask(c)
            gr = gr.astype(BF16)
            gm[chunk(c), :] = gr
            out = []
            for k, blk in enumerate(blocks):
                g = u[chunk(c), blk].astype(F32) + dot(gr, wtr[l, :, blk])
                if l > 0:
                    up = g * slope_of(s0[chunk(c), blk].astype(F32))
                    low = up.astype(BF16)
                    u[chunk(c), blk] = low
                    out.append(sums[k] + fold8(low.astype(F32)))
                else:
                    u[chunk(c), blk] = g.astype(BF16)
            if l == 0:
                pltpu.make_async_copy(u.at[chunk(c)], gx_ref.at[chunk(c)], load_sem.at[3]).start()
            return tuple(out)

        sums = lax.fori_loop(0, steps, body, tuple(zero8 for _ in blocks) if l > 0 else ())
        return sums

    def back_reduce_weight(l):
        source = xc if l == 0 else x1
        for k, blk in enumerate(blocks):
            wb[l, k * narrow : (k + 1) * narrow, :] = dot_first(gm[...], source[:, blk]).T.astype(BF16)

    sub_rows = seg_rows // ne

    def grads_one(l):
        wb[l, 2 * wide + narrow + 32 :, :] = jnp.zeros((wb.shape[1] - 2 * wide - narrow - 32, narrow), BF16)

        def send(k, c):
            target = lax.rem(my_a + k, na)
            pltpu.make_async_remote_copy(
                src_ref=wb.at[l, pl.ds(pl.multiple_of(target * seg_rows, 16), seg_rows)], dst_ref=rs1.at[my_a],
                send_sem=wg_send.at[l, 0], recv_sem=wg_recv.at[l, 0],
                device_id=a_peer(k), device_id_type=MESH,
            ).start()
            return c

        lax.fori_loop(1, na, send, 0)
        rs1[my_a] = wb[l, pl.ds(pl.multiple_of(my_a * seg_rows, 16), seg_rows), :]

    def wait_bytes(ref, count, sems):
        part = ref.at[pl.ds(0, count)]
        for sem in sems:
            pltpu.make_async_copy(part, part, sem).wait()

    def grads_two(l):
        if na > 1:
            wait_bytes(rs1, na - 1, (wg_send.at[l, 0], wg_recv.at[l, 0]))

        def add(c, carry):
            spot = pl.ds(pl.multiple_of(c * 16, 16), 16)
            total = rs1[0, spot, :].astype(F32)
            for i in range(1, na):
                total = total + rs1[i, spot, :].astype(F32)
            rs1[my_a, spot, :] = total.astype(BF16)
            return carry

        lax.fori_loop(0, seg_rows // 16, add, 0)

        def send(k, c):
            target = lax.rem(my_e + k, ne)
            pltpu.make_async_remote_copy(
                src_ref=rs1.at[my_a, pl.ds(pl.multiple_of(target * sub_rows, 16), sub_rows)], dst_ref=rs2.at[l, my_e],
                send_sem=wg_send.at[l, 1], recv_sem=wg_recv.at[l, 1],
                device_id=e_peer(k), device_id_type=MESH,
            ).start()
            return c

        lax.fori_loop(1, ne, send, 0)
        rs2[l, my_e] = rs1[my_a, pl.ds(pl.multiple_of(my_e * sub_rows, 16), sub_rows), :]

    def grads_three(l):
        wait_bytes(rs2.at[l], ne - 1, (wg_send.at[l, 1], wg_recv.at[l, 1]))

        def add(c, carry):
            spot = pl.ds(pl.multiple_of(c * 16, 16), 16)
            total = rs2[l, 0, spot, :].astype(F32)
            for i in range(1, ne):
                total = total + rs2[l, i, spot, :].astype(F32)
            ag1[my_e, spot, :] = total.astype(BF16)
            return carry

        lax.fori_loop(0, sub_rows // 16, add, 0)

        def send(k, c):
            pltpu.make_async_remote_copy(
                src_ref=ag1.at[my_e], dst_ref=ag1.at[my_e],
                send_sem=wg_send.at[l, 2], recv_sem=wg_recv.at[l, 2],
                device_id=e_peer(k), device_id_type=MESH,
            ).start()
            return c

        lax.fori_loop(1, ne, send, 0)

    def grads_four(l):
        wait_bytes(ag1, ne - 1, (wg_send.at[l, 2], wg_recv.at[l, 2]))

        def keep(j, c):
            ag2[pl.ds(pl.multiple_of(my_a * seg_rows + j * sub_rows, 16), sub_rows), :] = ag1[j]
            return c

        lax.fori_loop(0, ne, keep, 0)
        mine = pl.ds(pl.multiple_of(my_a * seg_rows, 16), seg_rows)

        def send(k, c):
            pltpu.make_async_remote_copy(
                src_ref=ag2.at[mine], dst_ref=ag2.at[mine],
                send_sem=wg_send.at[l, 3], recv_sem=wg_recv.at[l, 3],
                device_id=a_peer(k), device_id_type=MESH,
            ).start()
            return c

        lax.fori_loop(1, na, send, 0)

    def grads_five(l):
        if na > 1:
            wait_bytes(ag2, (na - 1) * seg_rows, (wg_send.at[l, 3], wg_recv.at[l, 3]))
        owr_ref[l] = ag2[0:wide, :].astype(F32)
        for k in range(wide // narrow):
            owe_ref[l, :, k * narrow : (k + 1) * narrow] = ag2[wide + k * narrow : wide + (k + 1) * narrow, :].astype(F32)
        owm_ref[l] = ag2[2 * wide : 2 * wide + narrow, :].astype(F32)
        owd_ref[l] = ag2[2 * wide + narrow : 2 * wide + narrow + 32, :].astype(F32)

    rims = rim_list(row_send, col_send, top_in, bot_in, side_in)
    rims_sp = [rim_list(row_send, col_send, top_sp.at[l], bot_sp.at[l], side_sp.at[l]) for l in range(layers)]

    load.wait()
    load2 = pltpu.make_async_copy(cot_hbm, raw, load_sem.at[1])
    for l in range(layers):
        reduce_phase(l)
        if l == 0:
            load2.start()
        mix_phase(l)
        spatial_phase(l)
        hidden_phase(l)
        if l == layers - 1:
            load2.wait()
        sums = widen_phase(l)
    store_y = pltpu.make_async_copy(raw.at[pl.ds(0, n)], y_ref, load_sem.at[2])
    store_y.start()
    for l in reversed(range(layers)):
        back_wide(l, sums)
        if l < layers - 1:
            back_reduce_weight(l + 1)
            grads_one(l + 1)
        back_expand(l)
        if l < layers - 1:
            grads_two(l + 1)
        back_spatial(l)
        if l < layers - 1:
            grads_three(l + 1)
        sums = back_reduce(l)
        if l < layers - 1:
            grads_four(l + 1)
            grads_five(l + 1)
    back_reduce_weight(0)
    store_y.wait()
    pltpu.make_async_copy(u, gx_ref, load_sem.at[3]).wait()
    grads_one(0)
    grads_two(0)
    grads_three(0)
    grads_four(0)
    grads_five(0)


def mega_call(sizes, frames, x, cot, idx, flags, counts, w_reduce, w_mix, w_depth, w_expand, gn, sn, gw, sw):
    na, nw, nc = sizes
    ne = nw * nc
    layers, wide, narrow = w_reduce.shape
    raw_frames = x.shape[0]
    n = frames
    rows = n * SPOT
    per = 16 * ne
    seg_rows = -(-(2 * wide + narrow + 32) // (na * per)) * per
    vmem = lambda shape, kind: pltpu.VMEM(shape, kind)
    half = n * COLS
    kernel = functools.partial(mega, sizes, frames, raw_frames, layers, wide, narrow, seg_rows)
    spec = pl.BlockSpec(memory_space=pltpu.VMEM)
    smem = pl.BlockSpec(memory_space=pltpu.SMEM)
    hbm = pl.BlockSpec(memory_space=pl.ANY)
    n_sync = 6 * layers
    nb = narrow // LANES
    scratch = [
        vmem((raw_frames, SPOT, wide), BF16), vmem((rows, wide), BF16), vmem((rows, wide), BF16),
        vmem((rows, wide), BF16), vmem((rows, wide), BF16),
        vmem((layers, nb, rows, LANES), F32), vmem((layers, rows, narrow), BF16),
        vmem((layers, nb, rows + 2 * SPOT, LANES), F32), vmem((layers, nb, rows + SPOT, LANES), F32),
        vmem((layers, rows, narrow), BF16), vmem((nb, rows, LANES), F32), vmem((rows, narrow), BF16),
        vmem((nb, half, LANES), F32), vmem((nb, half, LANES), F32), vmem((nb, half, LANES), F32),
        vmem((half, LANES), F32), vmem((layers, 27, 8, narrow), F32), vmem((narrow, wide), F32),
        vmem((layers, narrow, wide), F32), vmem((layers, narrow, narrow), F32),
        vmem((layers, narrow, wide), BF16), vmem((layers, wide, narrow), BF16), vmem((layers, narrow, narrow), BF16),
        vmem((2, half, narrow), BF16), vmem((2, 2, n, narrow), BF16),
        vmem((half, narrow), BF16), vmem((half, narrow), BF16), vmem((8, n, narrow), BF16),
        vmem((layers, half, narrow), BF16), vmem((layers, half, narrow), BF16), vmem((layers, 8, n, narrow), BF16),
        vmem((4 * layers, na, 2, narrow), F32), vmem((4 * layers, ne, 2, narrow), F32),
        vmem((2 * layers, na, 2, wide), F32), vmem((2 * layers, ne, 2, wide), F32),
        vmem((layers, na * seg_rows, narrow), BF16), vmem((na, seg_rows, narrow), BF16),
        vmem((layers, ne, seg_rows // ne, narrow), BF16), vmem((ne, seg_rows // ne, narrow), BF16),
        vmem((na * seg_rows, narrow), BF16),
        pltpu.SemaphoreType.DMA((4,)), pltpu.SemaphoreType.DMA((n_sync, 2)), pltpu.SemaphoreType.DMA((n_sync, 2)),
        pltpu.SemaphoreType.DMA((3 * layers, 8)), pltpu.SemaphoreType.DMA((3 * layers, 8)),
        pltpu.SemaphoreType.DMA((layers, 4)), pltpu.SemaphoreType.DMA((layers, 4)),
    ]
    shape = jax.ShapeDtypeStruct
    outs = (
        shape((n, SPOT, wide), BF16), shape((rows, wide), BF16),
        shape((layers, wide, narrow), F32), shape((layers, narrow, narrow), F32), shape((layers, 32, narrow), F32),
        shape((layers, narrow, wide), F32),
        shape((layers, 2, narrow), F32), shape((layers, 2, narrow), F32), shape((layers, wide), F32), shape((layers, wide), F32),
    )
    return pl.pallas_call(
        kernel,
        out_shape=outs,
        in_specs=[smem, smem, smem, hbm, hbm] + [spec] * 8,
        out_specs=(hbm, hbm) + (spec,) * 8,
        scratch_shapes=scratch,
        compiler_params=pltpu.CompilerParams(
            collective_id=frames, has_side_effects=True, vmem_limit_bytes=63 * 1024 * 1024
        ),
    )(idx, flags, counts, x, cot, w_reduce, w_mix, w_depth, w_expand, gn, sn, gw, sw)


def spread_kernel(pos_ref, y_ref, g_ref, oy_ref, og_ref):
    i = pl.program_id(0)
    for j in range(oy_ref.shape[0]):
        p = pos_ref[i * oy_ref.shape[0] + j]
        live = p >= 0
        q = jnp.maximum(p, 0)
        for src, dst in ((y_ref, oy_ref), (g_ref, og_ref)):
            tile = src[q]
            dst[j] = jnp.where(live, tile, jnp.zeros_like(tile))


def spread(pos, y, g, raw_frames):
    n, _, wide = y.shape
    per = 16
    spec = pl.BlockSpec((n, SPOT, wide), lambda i, p: (0, 0, 0), pipeline_mode=pl.Buffered(1))
    out_spec = pl.BlockSpec((per, SPOT, wide), lambda i, p: (i, 0, 0))
    shape = jax.ShapeDtypeStruct((raw_frames, SPOT, wide), BF16)
    return pl.pallas_call(
        spread_kernel,
        out_shape=(shape, shape),
        grid_spec=pltpu.PrefetchScalarGridSpec(
            num_scalar_prefetch=1, grid=(raw_frames // per,), in_specs=[spec, spec], out_specs=(out_spec, out_spec)
        ),
        compiler_params=pltpu.CompilerParams(vmem_limit_bytes=40 * 1024 * 1024),
    )(pos, y, g)


def fast_body(
    sizes, frames, live_all, activations, cotangent, w_reduce, w_mix, w_depth, w_expand,
    gains_narrow, shifts_narrow, gains_wide, shifts_wide,
):
    na, nw, nc = sizes
    clips, frame_len, hh, ww, wide = activations.shape
    narrow = w_reduce.shape[2]
    layers = w_reduce.shape[0]
    raw_frames = clips * frame_len
    group = jnp.sum(live_all, axis=1)
    mine = jnp.sum(jnp.where(jnp.arange(nc)[:, None] == lax.axis_index("clip"), live_all, 0), axis=0)
    slots = jnp.arange(clips, dtype=jnp.int32)
    ends = jnp.sum(jnp.where(slots[None, :] <= slots[:, None], mine[None, :], 0), axis=1)
    k = jnp.arange(frames, dtype=jnp.int32)
    before = ends[None, :] <= k[:, None]
    clip_of = jnp.sum(before.astype(jnp.int32), axis=1)
    start_of = jnp.sum(jnp.where(before, mine[None, :], 0), axis=1)
    valid = k < ends[-1]
    step = k - start_of
    idx = jnp.where(valid, clip_of * frame_len + step, 0).astype(jnp.int32)
    zero = jnp.zeros((1,), jnp.float32)
    validf = valid.astype(jnp.float32)
    flags = jnp.stack([
        jnp.concatenate([validf, zero]),
        jnp.concatenate([jnp.logical_and(valid, step > 0).astype(jnp.float32), zero]),
        jnp.concatenate([zero, validf]),
    ])
    count = (group * (hh * ww)).astype(jnp.float32)
    total = jnp.sum(count) * (na * nw)
    counts = jnp.concatenate([count, 1.0 / count, total[None], 1.0 / total[None]])
    raw = jnp.arange(raw_frames, dtype=jnp.int32)
    raw_clip, raw_step = raw // frame_len, raw % frame_len
    starts = ends - mine
    pos = jnp.sum(jnp.where(raw_clip[:, None] == slots[None, :], jnp.where(raw_step[:, None] < mine[None, :], (starts[None, :] + raw_step[:, None]), -1), 0), axis=1).astype(jnp.int32)
    res = mega_call(
        sizes, frames, activations.reshape(raw_frames, SPOT, wide), cotangent.reshape(raw_frames, SPOT, wide),
        idx, flags, counts, w_reduce, w_mix, w_depth.reshape(layers, 27, narrow), w_expand,
        gains_narrow, shifts_narrow, gains_wide, shifts_wide,
    )
    y, gx = res[0], res[1].reshape(frames, SPOT, wide)
    y, gx = spread(pos, y, gx, raw_frames)
    return (
        y.reshape(activations.shape), gx.reshape(activations.shape), res[2], res[3],
        res[4][:, :27].reshape(layers, 3, 3, 3, narrow), res[5], res[6], res[7], res[8], res[9],
    )


def body(
    sizes, frames, activations, stride, clip_order, cotangent, w_reduce, w_mix, w_depth, w_expand,
    gains_narrow, shifts_narrow, gains_wide, shifts_wide,
):
    clips, frame_len = activations.shape[:2]
    numbers = jnp.arange(stride.shape[0], dtype=jnp.int32)
    picked = jnp.sum(jnp.where(clip_order[:, None] == numbers[None, :], stride[None, :], 0), axis=1)
    live_all = (frame_len // picked).reshape(sizes[2], clips)
    params = (w_reduce, w_mix, w_depth, w_expand, gains_narrow, shifts_narrow, gains_wide, shifts_wide)
    fits = jnp.max(jnp.sum(live_all, axis=1)) <= frames
    return lax.cond(
        fits,
        lambda: fast_body(sizes, frames, live_all, activations, cotangent, *params),
        lambda: plain_body(activations, stride, clip_order, cotangent, *params),
    )


def solution(mesh, frames=96):
    sizes = tuple(mesh.shape[a] for a in AXES)
    big = P("clip", None, "ha", "wa", None)
    return jax.shard_map(
        functools.partial(body, sizes, frames),
        mesh=mesh,
        in_specs=(big, P(), P(), big) + (P(),) * 8,
        out_specs=(big, big) + (P(),) * 8,
        check_vma=False,
    )
```

```python
import functools
import math

import jax
import jax.numpy as jnp
from jax import lax
from jax.experimental import pallas as pl
from jax.experimental.pallas import tpu as pltpu
from jax.sharding import PartitionSpec as P

EPSILON = 1e-05
AXES = ("ha", "wa", "clip")
MESH = pl.DeviceIdType.MESH
F32 = jnp.float32
BF16 = jnp.bfloat16
ROWS = 2
COLS = 8
SPOT = ROWS * COLS
LANES = 128


def dot(a, b):
    return jnp.dot(a, b, preferred_element_type=F32)


def dot_first(a, b):
    return lax.dot_general(a, b, (((0,), (0,)), ((), ())), preferred_element_type=F32)


def sigmoid(v):
    return jax.nn.sigmoid(v)


def slope_of(z):
    s = sigmoid(z)
    return s * (1.0 + z * (1.0 - s))


def get(ref, spot):
    return jnp.concatenate([ref[lb, spot, :] for lb in range(ref.shape[0])], axis=-1)


def put(ref, spot, value):
    for lb in range(ref.shape[0]):
        ref[lb, spot, :] = value[:, lb * LANES : (lb + 1) * LANES]


def fold8(v):
    return jnp.sum(v.reshape(v.shape[0] // 8, 8, v.shape[1]), axis=0)


def split_dot(v, w):
    high = v.astype(BF16)
    low = (v - high.astype(F32)).astype(BF16)
    return dot(high, w) + dot(low, w)


def padded_2(block, sides, width):
    for axis, dim in sides:
        count = lax.axis_size(axis)
        forward = [(i, i + 1) for i in range(count - 1)]
        backward = [(target, source) for source, target in forward]
        low = lax.ppermute(
            lax.slice_in_dim(block, block.shape[dim] - width, None, axis=dim), axis, forward
        )
        high = lax.ppermute(lax.slice_in_dim(block, 0, width, axis=dim), axis, backward)
        block = jnp.concatenate([low, block, high], axis=dim)
    return block


def silu_act(values):
    return values * jax.nn.sigmoid(values)


def silu_slope(values):
    sigmoid_v = jax.nn.sigmoid(values)
    return sigmoid_v * (1.0 + values * (1.0 - sigmoid_v))


def project(operand, weight):
    dims_in = operand.shape
    result = jnp.dot(operand.reshape(-1, dims_in[-1]), weight, preferred_element_type=jnp.float32)
    return result.reshape(dims_in[:-1] + (weight.shape[-1],))


def project_back(upstream, weight):
    dims_in = upstream.shape
    result = lax.dot_general(
        upstream.reshape(-1, dims_in[-1]),
        weight,
        (((1,), (1,)), ((), ())),
        preferred_element_type=jnp.float32,
    )
    return result.reshape(dims_in[:-1] + (weight.shape[0],))


def outer_sum(operand, upstream):
    return lax.dot_general(
        operand.reshape(-1, operand.shape[-1]),
        upstream.reshape(-1, upstream.shape[-1]),
        (((0,), (0,)), ((), ())),
        preferred_element_type=jnp.float32,
    )


def moments(values, frame_mask, voxel_count):
    sum_axes = (0, 1, 2, 3)
    average = (
        lax.psum(jnp.sum(values * frame_mask, axis=sum_axes), ("ha", "wa", "clip")) / voxel_count
    )
    centered = values - average
    spread = (
        lax.psum(jnp.sum(centered * centered * frame_mask, axis=sum_axes), ("ha", "wa", "clip"))
        / voxel_count
    )
    inverse_std = lax.rsqrt(spread + EPSILON)
    return ((values - average) * inverse_std, inverse_std)


def norm_back(upstream, normed, inverse_std, gain_vec, frame_mask, voxel_count):
    sum_axes = (0, 1, 2, 3)
    grad_gain, grad_shift = lax.psum(
        (jnp.sum(upstream * normed, axis=sum_axes), jnp.sum(upstream, axis=sum_axes)),
        ("ha", "wa", "clip"),
    )
    result = (
        inverse_std
        * gain_vec
        * (upstream - frame_mask * (grad_shift + normed * grad_gain) / voxel_count)
    )
    return (result, grad_gain, grad_shift)


def pad_frames(values):
    return jnp.pad(values, ((0, 0), (1, 1), (0, 0), (0, 0), (0, 0)))


def forward_rim(values):
    return pad_frames(padded_2(values, (("ha", 2), ("wa", 3)), 1))


def backward_rim(values):
    return pad_frames(padded_2(values, (("ha", 2), ("wa", 3)), 1))


def depth_taps(padded, kernel, dims_out, flipped):
    frame_len, row_count, col_count = (dims_out[1], dims_out[2], dims_out[3])
    running = jnp.zeros(dims_out, jnp.float32)
    for step_t in range(3):
        for step_h in range(3):
            for step_w in range(3):
                if flipped:
                    start_t, start_h, start_w = (2 - step_t, 2 - step_h, 2 - step_w)
                else:
                    start_t, start_h, start_w = (step_t, step_h, step_w)
                window = padded[
                    :,
                    start_t : start_t + frame_len,
                    start_h : start_h + row_count,
                    start_w : start_w + col_count,
                    :,
                ]
                running = running + window.astype(jnp.float32) * kernel[
                    step_t, step_h, step_w
                ].astype(jnp.float32)
    return running


def kernel_grad(padded, upstream):
    frame_len, row_count, col_count = (upstream.shape[1], upstream.shape[2], upstream.shape[3])
    upstream_f = upstream.astype(jnp.float32)
    entries = []
    for step_t in range(3):
        for step_h in range(3):
            for step_w in range(3):
                window = padded[
                    :,
                    step_t : step_t + frame_len,
                    step_h : step_h + row_count,
                    step_w : step_w + col_count,
                    :,
                ]
                entries.append(jnp.sum(window.astype(jnp.float32) * upstream_f, axis=(0, 1, 2, 3)))
    return jnp.stack(entries).reshape(3, 3, 3, upstream.shape[-1])


def block_forward(
    inputs,
    frame_mask,
    mask_low,
    voxel_count,
    w_in,
    w_mid,
    w_dep,
    w_out,
    gain_narrow,
    shift_narrow,
    gain_wide,
    shift_wide,
):
    reduced = project(inputs, w_in)
    normed_one, inverse_one = moments(reduced, frame_mask, voxel_count)
    before_one = normed_one * gain_narrow[0] + shift_narrow[0]
    hidden_one = silu_act(before_one).astype(jnp.bfloat16)
    mixed_out = project(hidden_one, w_mid).astype(jnp.bfloat16) * mask_low
    padded = forward_rim(mixed_out)
    spatial = depth_taps(padded, w_dep, mixed_out.shape, False)
    normed_two, inverse_two = moments(spatial, frame_mask, voxel_count)
    before_two = normed_two * gain_narrow[1] + shift_narrow[1]
    hidden_two = silu_act(before_two).astype(jnp.bfloat16)
    widened = project(hidden_two, w_out)
    normed_three, inverse_three = moments(widened, frame_mask, voxel_count)
    summed = inputs.astype(jnp.float32) + normed_three * gain_wide + shift_wide
    output = silu_act(summed).astype(jnp.bfloat16)
    saved_state = (
        inputs,
        normed_one,
        inverse_one,
        before_one,
        hidden_one,
        padded,
        normed_two,
        inverse_two,
        before_two,
        hidden_two,
        normed_three,
        inverse_three,
        summed,
    )
    return (output, saved_state)


def block_backward(
    upstream,
    saved_state,
    frame_mask,
    voxel_count,
    w_in,
    w_mid,
    w_dep,
    w_out,
    gain_narrow,
    gain_wide,
):
    (
        inputs,
        normed_one,
        inverse_one,
        before_one,
        hidden_one,
        padded,
        normed_two,
        inverse_two,
        before_two,
        hidden_two,
        normed_three,
        inverse_three,
        summed,
    ) = saved_state
    grad_summed = upstream * silu_slope(summed)
    grad_widened, gain_three, shift_three = norm_back(
        grad_summed, normed_three, inverse_three, gain_wide, frame_mask, voxel_count
    )
    grad_widened = grad_widened.astype(jnp.bfloat16)
    grad_out_w = outer_sum(hidden_two, grad_widened)
    grad_two = project_back(grad_widened, w_out) * silu_slope(before_two)
    grad_spatial, gain_two, shift_two = norm_back(
        grad_two, normed_two, inverse_two, gain_narrow[1], frame_mask, voxel_count
    )
    grad_spatial = grad_spatial.astype(jnp.bfloat16)
    grad_dep_w = kernel_grad(padded, grad_spatial)
    grad_padded = backward_rim(grad_spatial)
    grad_mixed = (depth_taps(grad_padded, w_dep, grad_spatial.shape, True) * frame_mask).astype(
        jnp.bfloat16
    )
    grad_mid_w = outer_sum(hidden_one, grad_mixed)
    grad_one = project_back(grad_mixed, w_mid) * silu_slope(before_one)
    grad_reduced, gain_one, shift_one = norm_back(
        grad_one, normed_one, inverse_one, gain_narrow[0], frame_mask, voxel_count
    )
    grad_reduced = grad_reduced.astype(jnp.bfloat16)
    grad_in_w = outer_sum(inputs, grad_reduced)
    grad_inputs = grad_summed + project_back(grad_reduced, w_in)
    weight_parts = (grad_in_w, grad_mid_w, grad_dep_w, grad_out_w)
    norm_parts = (
        jnp.stack([gain_one, gain_two]),
        jnp.stack([shift_one, shift_two]),
        gain_three,
        shift_three,
    )
    return (grad_inputs, weight_parts, norm_parts)


def plain_body(
    activations,
    stride,
    clip_order,
    cotangent,
    w_reduce,
    w_mix,
    w_depth,
    w_expand,
    gains_narrow,
    shifts_narrow,
    gains_wide,
    shifts_wide,
):
    clips_here = activations.shape[0]
    frame_len = activations.shape[1]
    all_clips = stride.shape[0]
    slot_ids = lax.axis_index("clip") * clips_here + jnp.arange(clips_here, dtype=jnp.int32)
    numbers = jnp.arange(all_clips, dtype=jnp.int32)
    slot_clip = jnp.sum(
        jnp.where(slot_ids[:, None] == numbers[None, :], clip_order[None, :], 0), axis=1
    )
    slot_stride = jnp.sum(
        jnp.where(slot_clip[:, None] == numbers[None, :], stride[None, :], 0), axis=1
    )
    live_frames = frame_len // slot_stride
    mask_two = (jnp.arange(frame_len, dtype=jnp.int32)[None, :] < live_frames[:, None]).astype(
        jnp.float32
    )
    frame_mask = mask_two[:, :, None, None, None]
    mask_low = frame_mask.astype(jnp.bfloat16)
    grid_cells = (
        activations.shape[2] * lax.axis_size("ha") * activations.shape[3] * lax.axis_size("wa")
    )
    voxel_count = jnp.sum(frame_len // stride).astype(jnp.float32) * grid_cells
    depth_count = w_reduce.shape[0]
    values = activations
    saved_list = []
    for block_index in range(depth_count):
        values, saved_state = block_forward(
            values,
            frame_mask,
            mask_low,
            voxel_count,
            w_reduce[block_index],
            w_mix[block_index],
            w_depth[block_index],
            w_expand[block_index],
            gains_narrow[block_index],
            shifts_narrow[block_index],
            gains_wide[block_index],
            shifts_wide[block_index],
        )
        saved_list.append(saved_state)
    outputs = values * mask_low
    upstream = cotangent.astype(jnp.float32) * frame_mask
    weight_list = [None] * depth_count
    norm_list = [None] * depth_count
    for block_index in reversed(range(depth_count)):
        upstream, weight_parts, norm_parts = block_backward(
            upstream,
            saved_list[block_index],
            frame_mask,
            voxel_count,
            w_reduce[block_index],
            w_mix[block_index],
            w_depth[block_index],
            w_expand[block_index],
            gains_narrow[block_index],
            gains_wide[block_index],
        )
        weight_list[block_index] = weight_parts
        norm_list[block_index] = norm_parts
    stacked = tuple(
        (
            jnp.stack([weight_list[block_index][member] for block_index in range(depth_count)])
            for member in range(4)
        )
    )
    stacked = lax.psum((stacked[0], stacked[1], stacked[2], stacked[3]), ("ha", "wa", "clip"))
    norm_stacked = tuple(
        (
            jnp.stack([norm_list[block_index][member] for block_index in range(depth_count)])
            for member in range(4)
        )
    )
    return (
        outputs,
        upstream.astype(jnp.bfloat16),
        stacked[0],
        stacked[1],
        stacked[2],
        stacked[3],
        norm_stacked[0],
        norm_stacked[1],
        norm_stacked[2],
        norm_stacked[3],
    )


def mega(sizes, frames, clips, frame_len, layers, wide, narrow, plan, *refs):
    (
        stride_ref, order_ref, x_hbm, cot_hbm, wred_ref, wmix_ref, wdep_ref, wexp_ref,
        gn_ref, sn_ref, gw_ref, sw_ref,
        y_ref, gx_ref, packed_a, packed_b, packed_c, small_n, small_w,
        idx_ref, flag_ref, raw, xc, x1, s0, u, red, h1, mown, spat, h2, g2, gm, mtop, mbot, mside,
        vm8, vflag, wtap, hu, gram, wtr, wtb, wmt,
        row_send, col_send, top_in, bot_in, side_in, top_sp, bot_sp, side_sp,
        nar_a, nar_b, wid_a, wid_b,
        load_sem, ar_send, ar_recv, halo_send, halo_recv, wg_send, wg_recv, *pack_refs
    ) = refs
    n = frames
    CH = n // 2
    rows = n * SPOT
    na, nw, nc = sizes
    ne = nw * nc
    me = {a: lax.axis_index(a) for a in AXES}
    my_a = me["ha"]
    my_e = me["wa"] * nc + me["clip"]
    exists = {
        (-1, 0): my_a > 0, (1, 0): my_a < na - 1,
    }
    for dw, here in ((-1, me["wa"] > 0), (1, me["wa"] < nw - 1)):
        exists[(0, dw)] = here
        for dh in (-1, 1):
            exists[(dh, dw)] = jnp.logical_and(exists[(dh, 0)], here)

    def at(ha=None, wa=None, clip=None):
        return (
            me["ha"] if ha is None else ha,
            me["wa"] if wa is None else wa,
            me["clip"] if clip is None else clip,
        )

    def a_peer(k):
        return at(ha=lax.rem(my_a + k, na))

    def e_peer(k):
        p = lax.rem(my_e + k, ne)
        return at(wa=p // nc, clip=lax.rem(p, nc))

    world = na * ne
    one_shot = world <= 64 and world & (world - 1) == 0
    my_d = (me["clip"] * nw + me["wa"]) * na + my_a

    def d_peer(k):
        k = world - k
        p = 0
        bit = 1
        while bit < world:
            p = p + bit * lax.rem(lax.rem(my_d // bit, 2) + lax.rem(k // bit, 2), 2)
            bit *= 2
        return at(ha=lax.rem(p, na), wa=lax.rem(p // na, nw), clip=p // (na * nw))

    barrier = pltpu.get_barrier_semaphore()

    load = pltpu.make_async_copy(x_hbm, raw, load_sem.at[0])
    load.start()

    def greet_a(k, c):
        pl.semaphore_signal(barrier, inc=1, device_id=a_peer(k), device_id_type=MESH)
        return c

    def greet_e(k, c):
        pl.semaphore_signal(barrier, inc=1, device_id=e_peer(k), device_id_type=MESH)
        return c

    def greet_d(k, c):
        pl.semaphore_signal(barrier, inc=1, device_id=d_peer(k), device_id_type=MESH)
        return c

    if one_shot:
        lax.fori_loop(1, world, greet_d, 0)
        expected = world - 1
    else:
        lax.fori_loop(1, na, greet_a, 0)
        lax.fori_loop(1, ne, greet_e, 0)
        expected = na - 1 + ne - 1
        for dh in (-1, 1):
            for dw in (-1, 1):
                ok = exists[(dh, dw)]
                expected = expected + ok.astype(jnp.int32)

                @pl.when(ok)
                def _():
                    pl.semaphore_signal(
                        barrier, inc=1, device_id=at(ha=my_a + dh, wa=me["wa"] + dw), device_id_type=MESH
                    )

    def live_of(slot):
        return stride_ref[order_ref[slot]]

    base_slot = me["clip"] * clips

    def list_frame(k, carry):
        clip, step = carry
        inside = clip < clips
        pace = live_of(base_slot + jnp.minimum(clip, clips - 1))
        one = jnp.where(inside, 1.0, 0.0)
        idx_ref[k] = jnp.where(inside, clip * frame_len + step, 0)
        flag_ref[0, k] = one
        flag_ref[1, k] = jnp.where(step > 0, one, 0.0)
        flag_ref[2, k + 1] = one
        more = (step + 2) * pace <= frame_len
        return jnp.where(more, clip, clip + 1), jnp.where(more, step + 1, 0)

    lax.fori_loop(0, n, list_frame, (jnp.int32(0), jnp.int32(0)))
    flag_ref[0, n] = 0.0
    flag_ref[1, n] = 0.0
    flag_ref[2, 0] = 0.0

    def group_frames(group):
        def add(slot, total):
            pace = live_of(group * clips + slot)
            one = jnp.where(pace == 1, frame_len, jnp.where(pace == 2, frame_len // 2, frame_len // 4))
            return total + one

        return lax.fori_loop(0, clips, add, jnp.int32(0))

    group_count = [(group_frames(g) * SPOT).astype(F32) for g in range(nc)]
    total_count = sum(group_count) * float(na * nw)
    my_frames = group_count[0]
    for g in range(1, nc):
        my_frames = jnp.where(me["clip"] == g, group_count[g], my_frames)
    widths = (narrow, wide)
    total_inv = {w: 1.0 / jnp.full((1, w), total_count, F32) for w in widths}
    my_count_inv = {w: 1.0 / jnp.full((1, w), my_frames, F32) for w in widths}
    group_inv = [{w: 1.0 / jnp.full((1, w), c, F32) for w in widths} for c in group_count]

    def set_mask(f, c):
        vm8[pl.ds(pl.multiple_of(f * 8, 8), 8), :] = jnp.full((8, LANES), flag_ref[0, f], F32)
        for i, flag in enumerate((flag_ref[1, f], flag_ref[0, f], flag_ref[1, f + 1])):
            vflag[i, pl.ds(f, 1), :] = jnp.full((1, LANES), flag, F32)
        return c

    lax.fori_loop(0, n, set_mask, 0)
    for l in range(layers):
        for i in range(27):
            tap = wdep_ref[l, i // 9, i // 3 % 3].astype(F32)[i % 3 : i % 3 + 1]
            wtap[l, i] = jnp.broadcast_to(tap, (8, narrow))
        wtr[l] = wred_ref[l].T
        wtb[l] = wexp_ref[l].T
        wmt[l] = wmix_ref[l].T
        for lb in range(narrow // LANES):
            mown[l, lb, 0:SPOT] = jnp.zeros((SPOT, LANES), F32)
            mown[l, lb, SPOT + rows : SPOT + rows + SPOT] = jnp.zeros((SPOT, LANES), F32)
    mtop[...] = jnp.zeros_like(mtop)
    mbot[...] = jnp.zeros_like(mbot)
    mside[...] = jnp.zeros_like(mside)

    pl.semaphore_wait(barrier, expected)

    def finish(got, moments, slots, group_of, share):
        total = jnp.sum(got, axis=0)
        if not moments:
            return total[0:1], total[1:2]
        w = got.shape[-1]
        average = total[0:1] * total_inv[w]
        extra = [jnp.zeros((1, w), F32)] * 4
        for j in range(slots):
            g = group_of(j)
            off = got[j, 0:1] * (group_inv[g][w] * (1.0 / share)) - average
            extra[j % 4] = extra[j % 4] + off * off * (group_count[g] * float(share))
        second = total[1:2] + ((extra[0] + extra[1]) + (extra[2] + extra[3]))
        return average, lax.rsqrt(second * total_inv[w] + EPSILON)

    def pair_start(number, buf_a, buf_b, slot, value, moments):
        w = value.shape[-1]
        if na > 1:
            buf_a[slot, my_a] = value

            def send_a(k, c):
                pltpu.make_async_remote_copy(
                    src_ref=buf_a.at[slot, my_a], dst_ref=buf_a.at[slot, my_a],
                    send_sem=ar_send.at[number, 0], recv_sem=ar_recv.at[number, 0],
                    device_id=a_peer(k), device_id_type=MESH,
                ).start()
                return c

            lax.fori_loop(1, na, send_a, 0)
            part = buf_a.at[slot, pl.ds(0, na - 1)]
            pltpu.make_async_copy(part, part, ar_recv.at[number, 0]).wait()
            pltpu.make_async_copy(part, part, ar_send.at[number, 0]).wait()
            got = buf_a[slot]
            total = jnp.sum(got, axis=0)
            if moments:
                off = got[:, 0:1] - (total[0:1] * (1.0 / na))[None]
                extra = jnp.sum(off * off, axis=0) * my_count_inv[w]
                total = jnp.concatenate([total[0:1], total[1:2] + extra], axis=0)
            value = total
        buf_b[slot, my_e] = value

        def send_e(k, c):
            pltpu.make_async_remote_copy(
                src_ref=buf_b.at[slot, my_e], dst_ref=buf_b.at[slot, my_e],
                send_sem=ar_send.at[number, 1], recv_sem=ar_recv.at[number, 1],
                device_id=e_peer(k), device_id_type=MESH,
            ).start()
            return c

        lax.fori_loop(1, ne, send_e, 0)

    def bulk_wait(number, buf, slot, count):
        part = buf.at[slot, pl.ds(0, count)]
        pltpu.make_async_copy(part, part, ar_recv.at[number, 1]).wait()
        pltpu.make_async_copy(part, part, ar_send.at[number, 1]).wait()

    def reduce_start(number, buf_a, buf_b, slot, value, moments):
        if not (one_shot and value.shape[-1] == narrow):
            pair_start(number, buf_a, buf_b, slot, value, moments)
            return
        buf_b[slot, my_d] = value

        def send_d(k, c):
            pltpu.make_async_remote_copy(
                src_ref=buf_b.at[slot, my_d], dst_ref=buf_b.at[slot, my_d],
                send_sem=ar_send.at[number, 1], recv_sem=ar_recv.at[number, 1],
                device_id=d_peer(k), device_id_type=MESH,
            ).start()
            return c

        lax.fori_loop(1, world, send_d, 0)

    def reduce_finish(number, buf_b, slot, moments):
        if one_shot and buf_b.shape[-1] == narrow:
            bulk_wait(number, buf_b, slot, world - 1)
            return finish(buf_b[slot], moments, world, lambda j: j // (na * nw), 1)
        bulk_wait(number, buf_b, slot, ne - 1)
        return finish(buf_b[slot], moments, ne, lambda j: j % nc, na)

    def local_moments(first, square):
        total = jnp.sum(first, axis=0, keepdims=True)
        second = jnp.sum(square, axis=0, keepdims=True) - total * total * my_count_inv[total.shape[-1]]
        return jnp.concatenate([total, second], axis=0)

    def plain_pair(first, second):
        return jnp.concatenate(
            [jnp.sum(first, axis=0, keepdims=True), jnp.sum(second, axis=0, keepdims=True)], axis=0
        )

    def rim_list(r_send, c_send, top, bot, side):
        return [
            (1, 0, r_send.at[1], top), (-1, 0, r_send.at[0], bot),
            (0, 1, c_send.at[1], side.at[pl.ds(1, 2)]), (0, -1, c_send.at[0], side.at[pl.ds(5, 2)]),
            (1, 1, c_send.at[1, 1], side.at[0]), (-1, 1, c_send.at[1, 0], side.at[3]),
            (1, -1, c_send.at[0, 1], side.at[4]), (-1, -1, c_send.at[0, 0], side.at[7]),
        ]

    def rim_copy(number, k, item):
        dh, dw, src, dst = item
        return pltpu.make_async_remote_copy(
            src_ref=src, dst_ref=dst, send_sem=halo_send.at[number, k], recv_sem=halo_recv.at[number, k],
            device_id=at(ha=my_a + dh, wa=me["wa"] + dw), device_id_type=MESH,
        )

    def rim_start(number, items):
        for k, item in enumerate(items):
            @pl.when(exists[(item[0], item[1])])
            def _():
                rim_copy(number, k, item).start()

    def rim_sent(number, items):
        for k, item in enumerate(items):
            @pl.when(exists[(item[0], item[1])])
            def _():
                rim_copy(number, k, item).wait_send()

    def rim_arrived(number, items, which):
        for k in which:
            item = items[k]

            @pl.when(exists[(-item[0], -item[1])])
            def _():
                rim_copy(number, k, item).wait_recv()

    def fill_send(source, base):
        def rows_body(c, carry):
            tile = get(source, pl.ds(pl.multiple_of(base + c * CH * SPOT, SPOT), CH * SPOT))
            tile = tile.reshape(CH, ROWS, COLS, narrow)
            spot = pl.ds(pl.multiple_of(c * CH * COLS, CH * COLS), CH * COLS)
            for h in range(ROWS):
                row_send[h, spot, :] = tile[:, h].reshape(CH * COLS, narrow).astype(BF16)
            return carry

        lax.fori_loop(0, n // CH, rows_body, 0)
        for h in range(ROWS):
            for side, col in ((0, 0), (1, COLS - 1)):
                col_send[side, h] = get(source, pl.ds(base + h * COLS + col, n, stride=SPOT)).astype(BF16)

    def over_rim(apply):
        half = CH * COLS
        for key, which in ((-1, 0), (1, 1)):
            @pl.when(exists[(key, 0)])
            def _():
                dst = (mtop, mbot)[which]

                def body(c, carry):
                    spot = pl.ds(pl.multiple_of(c * half, half), half)
                    put(dst, spot, apply(
                        lambda: (top_in, bot_in)[which][spot, :].astype(F32),
                        lambda l: (top_sp, bot_sp)[which][l, spot, :].astype(F32),
                    ))
                    return carry

                lax.fori_loop(0, n // CH, body, 0)

    def over_sides(apply):
        for dw, base in ((-1, 0), (1, 4)):
            for r in range(4):
                dh = -1 if r == 0 else (1 if r == 3 else 0)

                @pl.when(exists[(dh, dw)])
                def _():
                    put(mside.at[base + r], pl.ds(8, n), apply(
                        lambda: side_in[base + r].astype(F32), lambda l: side_sp[l, base + r].astype(F32)
                    ))

    def side_sums(l, flip, target, base):
        stats = []
        for lb in range(narrow // LANES):
            lanes = pl.ds(lb * LANES, LANES)
            first = jnp.zeros((8, LANES), F32)
            square = jnp.zeros((8, LANES), F32)
            for side, e, col in ((0, 0, 0), (4, 2, COLS - 1)):
                for h in range(ROWS):
                    total = None
                    for a in range(3):
                        part = None
                        for b in range(3):
                            i = (a * 3 + b) * 3 + e
                            weight = wtap[l, 26 - i if flip else i, 0:1, lanes]
                            term = mside[side + h + b, lb, 7 + a : 7 + a + n, :] * weight
                            part = term if part is None else part + term
                        part = part * vflag[a] if a != 1 else part
                        total = part if total is None else total + part
                    total = total * vflag[1]
                    spot = pl.ds(base + 8 * h + col, n, stride=SPOT)
                    old = target[lb, spot, :]
                    new = old + total
                    target[lb, spot, :] = new
                    first = first + fold8(total)
                    square = square + fold8((new - old) * (new + old))
            stats.append((first, square))
        return stats

    row_id = lax.broadcasted_iota(jnp.int32, (8, LANES), 0)

    def shifted(own, own_base, f, lb):
        start = own_base + f * SPOT
        lines = [
            mtop[lb, pl.ds(pl.multiple_of(f * 8, 8), 8), :],
            own[lb, pl.ds(pl.multiple_of(start, 8), 8), :],
            own[lb, pl.ds(pl.multiple_of(start + 8, 8), 8), :],
            mbot[lb, pl.ds(pl.multiple_of(f * 8, 8), 8), :],
        ]
        out = []
        for v in lines:
            left = jnp.where(row_id == 0, 0.0, pltpu.roll(v, 1, 0))
            right = jnp.where(row_id == 7, 0.0, pltpu.roll(v, 7, 0))
            out.append((left, v, right))
        return out

    def tap_sum(grid, l, lanes, a, flip):
        res = []
        for h in range(ROWS):
            total = None
            for b in range(3):
                for e in range(3):
                    i = (a * 3 + b) * 3 + e
                    term = grid[h + b][e] * wtap[l, 26 - i if flip else i, :, lanes]
                    total = term if total is None else total + term
            res.append(total)
        return res

    def vmask(c):
        m = vm8[pl.ds(pl.multiple_of(c * CH * 8, CH * 8), CH * 8), :]
        m = jnp.broadcast_to(m.reshape(CH, 1, 8, LANES), (CH, ROWS, 8, LANES)).reshape(CH * SPOT, LANES)
        return jnp.concatenate([m] * (narrow // LANES), axis=1)

    def chunk(c):
        return pl.ds(pl.multiple_of(c * CH * SPOT, CH * SPOT), CH * SPOT)

    def chunk_off(c, base):
        return pl.ds(pl.multiple_of(base + c * CH * SPOT, SPOT), CH * SPOT)

    zero8 = jnp.zeros((8, narrow), F32)
    blocks = [pl.ds(k * narrow, narrow) for k in range(wide // narrow)]
    steps = n // CH
    scal = {}

    def reduce_phase(l):
        source = xc if l == 0 else x1

        def body(c, carry):
            first, square = carry
            if l == 0:
                for j in range(CH):
                    f = c * CH + j
                    tile = raw[idx_ref[f]]
                    xc[pl.ds(pl.multiple_of(f * SPOT, SPOT), SPOT), :] = (
                        tile.astype(F32) * flag_ref[0, f]
                    ).astype(BF16)
            r = dot(source[chunk(c), :], wred_ref[l])
            put(red.at[l], chunk(c), r)
            return first + fold8(r), square + fold8(r * r)

        first, square = lax.fori_loop(0, steps, body, (zero8, zero8))
        reduce_start(3 * l, nar_a, nar_b, 2 * l, local_moments(first, square), True)
        fill_send(red.at[l], 0)
        rim_start(l, rims)

    def mix_phase(l):
        average, inv = reduce_finish(3 * l, nar_b, 2 * l, True)
        scale = gn_ref[l, 0:1] * inv
        shift = sn_ref[l, 0:1] - average * scale
        scal["one", l] = (average, inv, scale, shift)

        def body(c, carry):
            z = get(red.at[l], chunk(c)) * scale + shift
            h = (z * sigmoid(z)).astype(BF16)
            h1[l, chunk(c), :] = h
            put(mown.at[l], chunk_off(c, SPOT), dot(h, wmix_ref[l]))
            return carry

        lax.fori_loop(0, steps, body, 0)
        rim_arrived(l, rims, range(2))

        def apply(arrived, second):
            z = arrived() * scale + shift
            return dot((z * sigmoid(z)).astype(BF16), wmix_ref[l])

        over_rim(apply)
        return apply

    def spatial_phase(l, apply):
        stats = []
        for lb in range(narrow // LANES):
            lanes = pl.ds(lb * LANES, LANES)

            def body(f, carry):
                cur, nxt, first, square = carry
                grid = shifted(mown.at[l], SPOT, f, lb)
                here = flag_ref[1, f]
                t2 = tap_sum(grid, l, lanes, 2, False)
                t1 = tap_sum(grid, l, lanes, 1, False)
                t0 = tap_sum(grid, l, lanes, 0, False)
                alive = flag_ref[2, f]
                for h in range(ROWS):
                    done = (cur[h] + here * t2[h]) * alive
                    spat[l, lb, pl.ds(pl.multiple_of(f * SPOT + 8 * h, 8), 8), :] = done
                    first = first + done
                    square = square + done * done
                cur = tuple(t1[h] + here * nxt[h] for h in range(ROWS))
                return cur, tuple(t0), first, square

            z = jnp.zeros((8, LANES), F32)
            cur, nxt, first, square = lax.fori_loop(0, n, body, ((z, z), (z, z), z, z))
            for h in range(ROWS):
                done = cur[h] * flag_ref[2, n]
                spat[l, lb, rows + 8 * h : rows + 8 * h + 8, :] = done
                first = first + done
                square = square + done * done
            stats.append((first, square))
        rim_arrived(l, rims, range(2, 8))
        over_sides(apply)
        more = side_sums(l, False, spat.at[l], SPOT)
        rim_sent(l, rims)
        first = jnp.concatenate([s[0] + m[0] for s, m in zip(stats, more)], axis=1)
        square = jnp.concatenate([s[1] + m[1] for s, m in zip(stats, more)], axis=1)
        reduce_start(3 * l + 1, nar_a, nar_b, 2 * l + 1, local_moments(first, square), True)
        fill_send(spat.at[l], SPOT)
        rim_start(layers + l, rims_sp[l])

    def hidden_phase(l):
        average, inv = reduce_finish(3 * l + 1, nar_b, 2 * l + 1, True)
        scale = gn_ref[l, 1:2] * inv
        shift = sn_ref[l, 1:2] - average * scale
        scal["two", l] = (average, inv, scale, shift)

        def body(c, first):
            z = get(spat.at[l], chunk_off(c, SPOT)) * scale + shift
            h = z * sigmoid(z) * vmask(c)
            low = h.astype(BF16)
            h2[l, chunk(c), :] = low
            return first + fold8(low.astype(F32))

        first = lax.fori_loop(0, steps, body, zero8)
        g = dot_first(h2[l], h2[l])
        gram[l] = g
        t = split_dot(g, wexp_ref[l])
        square = jnp.sum(t * wexp_ref[l].astype(F32), axis=0, keepdims=True)
        hsum = jnp.sum(first, axis=0, keepdims=True)
        scal["hsum", l] = hsum
        both = split_dot(jnp.broadcast_to(hsum, (8, narrow)), wexp_ref[l])[0:1]
        second = square - both * both * my_count_inv[wide]
        reduce_start(3 * l + 2, wid_a, wid_b, l, jnp.concatenate([both, second], axis=0), True)
        rim_sent(layers + l, rims_sp[l])

    def widen_phase(l):
        average, inv = reduce_finish(3 * l + 2, wid_b, l, True)
        scale = gw_ref[l : l + 1] * inv
        shift = sw_ref[l : l + 1] - average * scale
        scal["wide", l] = (average, inv, scale, shift)
        source = xc if l == 0 else x1
        last = l == layers - 1

        def body(c, sums):
            out = []
            hid = h2[l, chunk(c), :]
            mask = vmask(c)
            for k, blk in enumerate(blocks):
                cut = slice(k * narrow, (k + 1) * narrow)
                w = dot(hid, wexp_ref[l, :, blk])
                summed = source[chunk(c), blk].astype(F32) + (w * scale[:, cut] + shift[:, cut])
                s = sigmoid(summed)
                y = summed * s
                if not last:
                    x1[chunk(c), blk] = (y * mask).astype(BF16)
                    s0[chunk(c), blk] = summed.astype(BF16)
                else:
                    g = jnp.concatenate([raw[idx_ref[c * CH + j], :, blk] for j in range(CH)], axis=0)
                    raw[pl.ds(c * CH, CH), :, blk] = y.astype(BF16).reshape(CH, SPOT, narrow)
                    up = g.astype(F32) * (s * (1.0 + summed * (1.0 - s))) * mask
                    low = up.astype(BF16)
                    u[chunk(c), blk] = low
                    out.append(sums[k] + fold8(low.astype(F32)))
            return tuple(out)

        return lax.fori_loop(0, steps, body, tuple(zero8 for _ in blocks) if last else ())

    def back_wide(l, sums):
        total = jnp.concatenate([jnp.sum(s, axis=0, keepdims=True) for s in sums], axis=1)
        second = []
        for blk in blocks:
            part = dot_first(h2[l], u[:, blk])
            hu[:, blk] = part
            second.append(jnp.sum(part * wexp_ref[l, :, blk].astype(F32), axis=0, keepdims=True))
        second = jnp.concatenate(second, axis=1)
        reduce_start(
            3 * layers + 3 * l, wid_a, wid_b, layers + l, jnp.concatenate([total, second], axis=0), False
        )

    def back_expand(l):
        gshift, gsec = reduce_finish(3 * layers + 3 * l, wid_b, layers + l, False)
        average, inv, scale, _ = scal["wide", l]
        ggain = inv * (gsec - average * gshift)
        small_w[l : l + 1] = ggain
        small_w[layers + l : layers + l + 1] = gshift
        drift = inv * ggain * total_inv[wide]
        weight = wexp_ref[l].astype(F32)
        awt = (weight * scale).T.astype(BF16)
        mx = dot((weight * (scale * drift)).astype(BF16), wtb[l])
        base = scale * (gshift * total_inv[wide] - average * drift)
        const = split_dot(jnp.broadcast_to(base, (8, wide)), wtb[l])[0:1]
        mx = mx.astype(BF16)
        wtb[l] = awt
        _, _, scale2, shift2 = scal["two", l]
        avg2, inv2, _, _ = scal["two", l]

        def body(c, carry):
            first, square = carry
            p = dot(u[chunk(c), :], wtb[l]) - dot(h2[l, chunk(c), :], mx) - const
            sp = get(spat.at[l], chunk_off(c, SPOT))
            g = p * slope_of(sp * scale2 + shift2) * vmask(c)
            put(g2, chunk(c), g)
            normed = (sp - avg2) * inv2
            return first + fold8(g), square + fold8(g * normed)

        first, square = lax.fori_loop(0, steps, body, (zero8, zero8))
        reduce_start(
            3 * layers + 3 * l + 1, nar_a, nar_b, 2 * layers + 2 * l, plain_pair(first, square), False
        )
        fill_send(g2, 0)
        rim_start(2 * layers + l, rims)
        hcol = jnp.broadcast_to(scal["hsum", l], (8, narrow)).T[:, 0:1]
        grad = scale * (
            hu[...] - hcol * (gshift * total_inv[wide] - average * drift) - split_dot(gram[l], wexp_ref[l]) * drift
        )
        buf, row = place[("expand", l)]
        for k in range(wide // LANES):
            buf[row + k * narrow : row + (k + 1) * narrow, :] = grad[:, k * LANES : (k + 1) * LANES].astype(BF16)

    def back_spatial(l):
        gshift, ggain = reduce_finish(3 * layers + 3 * l + 1, nar_b, 2 * layers + 2 * l, False)
        small_n[4 * l + 1 : 4 * l + 2] = ggain
        small_n[4 * l + 3 : 4 * l + 4] = gshift
        avg2, inv2, scale2, _ = scal["two", l]
        a_u = scale2
        a_s = scale2 * inv2 * ggain * total_inv[narrow]
        a_c = scale2 * gshift * total_inv[narrow] - a_s * avg2

        def body(c, carry):
            put(g2, chunk(c), a_u * get(g2, chunk(c)) - a_s * get(spat.at[l], chunk_off(c, SPOT)) - a_c)
            return carry

        lax.fori_loop(0, steps, body, 0)
        rim_arrived(2 * layers + l, rims, range(2))
        rim_arrived(layers + l, rims_sp[l], range(8))
        apply = lambda arrived, second: a_u * arrived() - a_s * second(l) - a_c
        over_rim(apply)
        tap_grads = []

        for lb in range(narrow // LANES):
            lanes = pl.ds(lb * LANES, LANES)
            if l == 0 and lb == 0:
                step_b(1)
            if l == 0 and lb == 1:
                step_a(4)
                step_b(2)

            def body(f, carry):
                cur, nxt, grads = carry
                grid = shifted(g2, 0, f, lb)
                here = flag_ref[1, f]
                after = flag_ref[1, f + 1]
                live = flag_ref[0, f]
                t2 = tap_sum(grid, l, lanes, 2, True)
                t1 = tap_sum(grid, l, lanes, 1, True)
                t0 = tap_sum(grid, l, lanes, 0, True)
                alive = flag_ref[2, f]
                done = [(cur[h] + here * t2[h]) * alive for h in range(ROWS)]
                spat[l, lb, pl.ds(pl.multiple_of(f * SPOT, SPOT), SPOT), :] = jnp.concatenate(done, axis=0)
                grads = list(grads)
                for a, flag in ((0, here), (1, live), (2, after)):
                    for h in range(ROWS):
                        m = flag * mown[l, lb, pl.ds(pl.multiple_of((f + a) * SPOT + 8 * h, 8), 8), :]
                        for b in range(3):
                            for e in range(3):
                                i = (a * 3 + b) * 3 + e
                                grads[i] = grads[i] + m * grid[h + 2 - b][2 - e]
                cur = tuple(t1[h] + here * nxt[h] for h in range(ROWS))
                return cur, tuple(t0), tuple(grads)

            z = jnp.zeros((8, LANES), F32)
            cur, nxt, grads = lax.fori_loop(0, n, body, ((z, z), (z, z), tuple(z for _ in range(27))))
            spat[l, lb, rows : rows + SPOT, :] = jnp.concatenate(
                [cur[h] * flag_ref[2, n] for h in range(ROWS)], axis=0
            )
            tap_grads.append(list(grads))

        rim_arrived(2 * layers + l, rims, range(2, 8))
        over_sides(apply)
        side_sums(l, True, spat.at[l], SPOT)
        rim_sent(2 * layers + l, rims)
        for lb in range(narrow // LANES):
            grads = tap_grads[lb]
            for side, e, col in ((0, 2, 0), (4, 0, COLS - 1)):
                for a in range(3):
                    for h in range(ROWS):
                        m = mown[l, lb, pl.ds(a * SPOT + 8 * h + col, n, stride=SPOT), :] * vflag[a]
                        for b in range(3):
                            i = (a * 3 + b) * 3 + e
                            grads[i] = grads[i] + fold8(m * mside[side + h + 2 - b, lb, 8 : 8 + n, :])
            folded = [jnp.sum(g, axis=0, keepdims=True) for g in grads]
            folded += [jnp.zeros((1, LANES), F32)] * 5
            buf, row = place[("depth", l)]
            buf[row + lb * 32 : row + lb * 32 + 32, :] = jnp.concatenate(folded, axis=0).astype(BF16)

        avg1, inv1, scale1, shift1 = scal["one", l]

        def body2(c, carry):
            first, square = carry
            low = get(spat.at[l], chunk_off(c, SPOT)).astype(BF16)
            gm[chunk(c), :] = low
            r = get(red.at[l], chunk(c))
            g = dot(low, wmt[l]) * slope_of(r * scale1 + shift1)
            put(g2, chunk(c), g)
            return first + fold8(g), square + fold8(g * ((r - avg1) * inv1))

        first, square = lax.fori_loop(0, steps, body2, (zero8, zero8))
        reduce_start(
            3 * layers + 3 * l + 2, nar_a, nar_b, 2 * layers + 2 * l + 1, plain_pair(first, square), False
        )
        buf, row = place[("mix", l)]
        grad = dot_first(h1[l], gm[...]).astype(BF16)
        for k in range(narrow // LANES):
            buf[row + k * narrow : row + (k + 1) * narrow, :] = grad[:, k * LANES : (k + 1) * LANES]

    def back_reduce(l):
        gshift, ggain = reduce_finish(3 * layers + 3 * l + 2, nar_b, 2 * layers + 2 * l + 1, False)
        small_n[4 * l : 4 * l + 1] = ggain
        small_n[4 * l + 2 : 4 * l + 3] = gshift
        avg1, inv1, scale1, _ = scal["one", l]
        a_u = scale1
        a_s = scale1 * inv1 * ggain * total_inv[narrow]
        a_c = scale1 * gshift * total_inv[narrow] - a_s * avg1

        def body(c, sums):
            gr = (a_u * get(g2, chunk(c)) - a_s * get(red.at[l], chunk(c)) - a_c) * vmask(c)
            gr = gr.astype(BF16)
            gm[chunk(c), :] = gr
            if l == 0:
                return ()
            out = []
            for k, blk in enumerate(blocks):
                g = u[chunk(c), blk].astype(F32) + dot(gr, wtr[l, :, blk])
                up = g * slope_of(s0[chunk(c), blk].astype(F32))
                low = up.astype(BF16)
                u[chunk(c), blk] = low
                out.append(sums[k] + fold8(low.astype(F32)))
            return tuple(out)

        sums = lax.fori_loop(0, steps, body, tuple(zero8 for _ in blocks) if l > 0 else ())
        return sums

    def input_grads(c):
        for blk in blocks:
            g = u[chunk(c), blk].astype(F32) + dot(gm[chunk(c), :], wtr[0, :, blk])
            u[chunk(c), blk] = g.astype(BF16)
        pltpu.make_async_copy(u.at[chunk(c)], gx_ref.at[chunk(c)], load_sem.at[3]).start()

    def back_reduce_weight(l):
        source = xc if l == 0 else x1
        for k, blk in enumerate(blocks):
            buf, row = place[("reduce", l)]
            grad = dot_first(gm[...], source[:, blk]).T.astype(BF16)
            for lb in range(narrow // LANES):
                first = row + lb * wide + k * narrow
                buf[first : first + narrow, :] = grad[:, lb * LANES : (lb + 1) * LANES]

    groups = {
        "ha": (na, my_a, a_peer),
        "wa": (nw, me["wa"], lambda k: at(wa=lax.rem(me["wa"] + k, nw))),
        "clip": (nc, me["clip"], lambda k: at(clip=lax.rem(me["clip"] + k, nc))),
        "all": (ne, my_e, e_peer),
    }

    def bytes_wait(ref, count, sem):
        part = ref.at[pl.ds(0, count)]
        pltpu.make_async_copy(part, part, sem).wait()

    def pack_step(number, stages, bufs, out_hbm):
        wb, recvs, gats = bufs
        total_rows = wb.shape[0]
        sizes_of = []
        left = total_rows
        for st in stages:
            sizes_of.append((left, left // groups[st][0]))
            left //= groups[st][0]
        last = len(stages) - 1

        def send_seg(i):
            size, mine, peer = groups[stages[i]]
            seg = sizes_of[i][1]
            src = wb if i == 0 else gats[i - 1].at[groups[stages[i - 1]][1]]

            def send(k, c):
                target = lax.rem(mine + k, size)
                pltpu.make_async_remote_copy(
                    src_ref=src.at[pl.ds(pl.multiple_of(target * seg, 16), seg)], dst_ref=recvs[i].at[mine],
                    send_sem=wg_send.at[number, i], recv_sem=wg_recv.at[number, i],
                    device_id=peer(k), device_id_type=MESH,
                ).start()
                return c

            lax.fori_loop(1, size, send, 0)
            recvs[i][mine] = src[pl.ds(pl.multiple_of(mine * seg, 16), seg), :]

        def add_up(i):
            size, mine, _ = groups[stages[i]]
            seg = sizes_of[i][1]
            if size > 1:
                bytes_wait(recvs[i], size - 1, wg_recv.at[number, i])
                bytes_wait(recvs[i], size - 1, wg_send.at[number, i])

            def add(c, carry):
                spot = pl.ds(pl.multiple_of(c * 16, 16), 16)
                total = recvs[i][0, spot, :].astype(F32)
                for j in range(1, size):
                    total = total + recvs[i][j, spot, :].astype(F32)
                gats[i][mine, spot, :] = total.astype(BF16)
                return carry

            lax.fori_loop(0, seg // 16, add, 0)

        def send_back(i):
            size, mine, peer = groups[stages[i]]
            k_sem = 2 * len(stages) - 1 - i

            def send(k, c):
                pltpu.make_async_remote_copy(
                    src_ref=gats[i].at[mine], dst_ref=gats[i].at[mine],
                    send_sem=wg_send.at[number, k_sem], recv_sem=wg_recv.at[number, k_sem],
                    device_id=peer(k), device_id_type=MESH,
                ).start()
                return c

            lax.fori_loop(1, size, send, 0)

        def got_back(i):
            size = groups[stages[i]][0]
            k_sem = 2 * len(stages) - 1 - i
            if size > 1:
                bytes_wait(gats[i], size - 1, wg_recv.at[number, k_sem])
                bytes_wait(gats[i], size - 1, wg_send.at[number, k_sem])

        def down(i):
            mine = groups[stages[i]][1]
            seg = sizes_of[i + 1][1]

            def keep(j, c):
                gats[i][mine, pl.ds(pl.multiple_of(j * seg, 16), seg), :] = gats[i + 1][j]
                return c

            lax.fori_loop(0, groups[stages[i + 1]][0], keep, 0)

        def step(k):
            if k <= last:
                if k > 0:
                    add_up(k - 1)
                send_seg(k)
            elif k == last + 1:
                add_up(last)
                send_back(last)
            elif k <= 2 * last + 1:
                i = 2 * last + 1 - k
                got_back(i + 1)
                down(i)
                send_back(i)
            else:
                got_back(0)
                copy = pltpu.make_async_copy(gats[0], out_hbm, load_sem.at[4 + number])
                copy.start()

        def stored():
            pltpu.make_async_copy(gats[0], out_hbm, load_sem.at[4 + number]).wait()

        return step, stored

    rims = rim_list(row_send, col_send, top_in, bot_in, side_in)
    rims_sp = [rim_list(row_send, col_send, top_sp.at[l], bot_sp.at[l], side_sp.at[l]) for l in range(layers)]

    place = {}
    packs = []
    at_ref = 0
    for number, (parts, stages, padded, used) in enumerate(plan):
        m = len(stages)
        bufs = (pack_refs[at_ref], pack_refs[at_ref + 1 : at_ref + 1 + m], pack_refs[at_ref + 1 + m : at_ref + 1 + 2 * m])
        at_ref += 1 + 2 * m
        for key, row, _ in parts:
            place[key] = (bufs[0], row)
        if padded > used:
            bufs[0][used:padded, :] = jnp.zeros((padded - used, LANES), BF16)
        packs.append(pack_step(number, stages, bufs, (packed_a, packed_b, packed_c)[number]))
    (step_a, stored_a), (step_b, stored_b), (step_c, stored_c) = packs

    load.wait()
    load2 = pltpu.make_async_copy(cot_hbm, raw, load_sem.at[1])
    for l in range(layers):
        reduce_phase(l)
        if l == 0:
            load2.start()
        spatial_phase(l, mix_phase(l))
        hidden_phase(l)
        if l == layers - 1:
            load2.wait()
        sums = widen_phase(l)
    store_y = pltpu.make_async_copy(raw.at[pl.ds(0, n)], y_ref, load_sem.at[2])
    store_y.start()
    for l in reversed(range(layers)):
        back_wide(l, sums)
        if l == 0:
            back_reduce_weight(1)
            step_a(2)
        back_expand(l)
        if l == 0:
            step_a(3)
            step_b(0)
        back_spatial(l)
        if l == 0:
            step_a(5)
            step_b(3)
        else:
            step_a(0)
        sums = back_reduce(l)
        if l == 0:
            step_a(6)
            step_b(4)
        else:
            step_a(1)
    back_reduce_weight(0)
    step_c(0)
    input_grads(0)
    step_c(1)
    step_b(5)
    input_grads(1)
    step_b(6)
    step_c(2)
    step_c(3)
    step_c(4)
    store_y.wait()
    pltpu.make_async_copy(u, gx_ref, load_sem.at[3]).wait()
    stored_a()
    stored_b()
    stored_c()


def pack_plan(sizes, wide, narrow):
    world = sizes[0] * sizes[1] * sizes[2]
    plan = []
    for names, stages in (
        ((("expand", 1), ("mix", 1), ("depth", 1)), ("ha", "wa", "clip")),
        ((("reduce", 1), ("expand", 0)), ("ha", "wa", "clip")),
        ((("reduce", 0), ("mix", 0), ("depth", 0)), ("ha", "all")),
    ):
        nb = narrow // LANES
        rows = {"reduce": nb * wide, "expand": nb * wide, "mix": nb * narrow, "depth": nb * 32}
        used = 0
        parts = []
        for key in names:
            parts.append((key, used, rows[key[0]]))
            used += rows[key[0]]
        padded = -(-used // (16 * world)) * 16 * world
        plan.append((parts, stages, padded, used))
    return plan


def mega_call(sizes, frames, clips, x, cot, stride, order, w_reduce, w_mix, w_depth, w_expand, gn, sn, gw, sw):
    na, nw, nc = sizes
    ne = nw * nc
    layers, wide, narrow = w_reduce.shape
    raw_frames = x.shape[0]
    n = frames
    rows = n * SPOT
    plan = pack_plan(sizes, wide, narrow)
    group_size = {"ha": na, "wa": nw, "clip": nc, "all": ne}
    vmem = lambda shape, kind: pltpu.VMEM(shape, kind)
    half = n * COLS
    kernel = functools.partial(mega, sizes, frames, clips, raw_frames // clips, layers, wide, narrow, plan)
    spec = pl.BlockSpec(memory_space=pltpu.VMEM)
    smem = pl.BlockSpec(memory_space=pltpu.SMEM)
    hbm = pl.BlockSpec(memory_space=pl.ANY)
    n_sync = 6 * layers
    nb = narrow // LANES
    world = na * ne
    slots = world if world <= 64 and world & (world - 1) == 0 else ne
    scratch = [
        pltpu.SMEM((n,), jnp.int32), pltpu.SMEM((3, n + 1), F32),
        vmem((raw_frames, SPOT, wide), BF16), vmem((rows, wide), BF16), vmem((rows, wide), BF16),
        vmem((rows, wide), BF16), vmem((rows, wide), BF16),
        vmem((layers, nb, rows, LANES), F32), vmem((layers, rows, narrow), BF16),
        vmem((layers, nb, rows + 2 * SPOT, LANES), F32), vmem((layers, nb, rows + SPOT, LANES), F32),
        vmem((layers, rows, narrow), BF16), vmem((nb, rows, LANES), F32), vmem((rows, narrow), BF16),
        vmem((nb, half, LANES), F32), vmem((nb, half, LANES), F32), vmem((8, nb, n + 16, LANES), F32),
        vmem((half, LANES), F32), vmem((3, n, LANES), F32), vmem((layers, 27, 8, narrow), F32), vmem((narrow, wide), F32),
        vmem((layers, narrow, narrow), F32),
        vmem((layers, narrow, wide), BF16), vmem((layers, wide, narrow), BF16), vmem((layers, narrow, narrow), BF16),
        vmem((2, half, narrow), BF16), vmem((2, 2, n, narrow), BF16),
        vmem((half, narrow), BF16), vmem((half, narrow), BF16), vmem((8, n, narrow), BF16),
        vmem((layers, half, narrow), BF16), vmem((layers, half, narrow), BF16), vmem((layers, 8, n, narrow), BF16),
        vmem((4 * layers, na, 2, narrow), F32), vmem((4 * layers, slots, 2, narrow), F32),
        vmem((2 * layers, na, 2, wide), F32), vmem((2 * layers, ne, 2, wide), F32),
        pltpu.SemaphoreType.DMA((4 + len(plan),)), pltpu.SemaphoreType.DMA((n_sync, 2)), pltpu.SemaphoreType.DMA((n_sync, 2)),
        pltpu.SemaphoreType.DMA((3 * layers, 8)), pltpu.SemaphoreType.DMA((3 * layers, 8)),
        pltpu.SemaphoreType.DMA((len(plan), 6)), pltpu.SemaphoreType.DMA((len(plan), 6)),
    ]
    outs_packed = []
    for _, stages, padded, _ in plan:
        scratch.append(vmem((padded, LANES), BF16))
        recvs, gats, left = [], [], padded
        for st in stages:
            left //= group_size[st]
            recvs.append(vmem((group_size[st], left, LANES), BF16))
            gats.append(vmem((group_size[st], left, LANES), BF16))
        scratch += recvs + gats
        outs_packed.append(jax.ShapeDtypeStruct(gats[0].shape, BF16))
    shape = jax.ShapeDtypeStruct
    outs = (
        shape((n, SPOT, wide), BF16), shape((rows, wide), BF16),
        *outs_packed,
        shape((4 * layers, narrow), F32), shape((2 * layers, wide), F32),
    )
    return pl.pallas_call(
        kernel,
        out_shape=outs,
        in_specs=[smem, smem, hbm, hbm] + [spec] * 8,
        out_specs=(hbm,) * 5 + (spec,) * 2,
        scratch_shapes=scratch,
        compiler_params=pltpu.CompilerParams(
            collective_id=frames, has_side_effects=True, vmem_limit_bytes=63 * 1024 * 1024
        ),
    )(stride, order, x, cot, w_reduce, w_mix, w_depth, w_expand, gn, sn, gw, sw)


def finish_kernel(plan, layers, wide, narrow, steps, pos_ref, *refs):
    y_ref, g_ref, pa, pb, pc, sn, sw, oy, og, owr, owm, owd, owe, ogn, osn, ogw, osw = refs
    i = pl.program_id(0)
    per = oy.shape[0]
    for j in range(per):
        p = pos_ref[i * per + j]
        live = p >= 0
        q = jnp.maximum(p, 0)
        for src, dst in ((y_ref, oy), (g_ref, og)):
            tile = src[q]
            dst[j] = jnp.where(live, tile, jnp.zeros_like(tile))
    packed = (pa, pb, pc)
    rows_r, rows_m = wide // steps, narrow // steps
    for number, (parts, _, _, _) in enumerate(plan):
        for (kind, l), row, _ in parts:
            ref = packed[number]
            if kind == "expand":
                for k in range(wide // LANES):
                    spot = pl.ds(pl.multiple_of(row + k * narrow + i * rows_m, 16), rows_m)
                    owe[l, :, k * LANES : (k + 1) * LANES] = ref[spot, :].astype(F32)
            elif kind != "depth":
                dst, size, part = (owr, wide, rows_r) if kind == "reduce" else (owm, narrow, rows_m)
                for lb in range(narrow // LANES):
                    spot = pl.ds(pl.multiple_of(row + lb * size + i * part, 16), part)
                    dst[l, :, lb * LANES : (lb + 1) * LANES] = ref[spot, :].astype(F32)
            else:
                @pl.when(i == 0)
                def _():
                    taps = jnp.concatenate([ref[row + lb * 32 : row + lb * 32 + 32, :] for lb in range(narrow // LANES)], axis=1).astype(F32)
                    for a in range(3):
                        for b in range(3):
                            first = (a * 3 + b) * 3
                            owd[l, a, b] = taps[first : first + 3]

    @pl.when(i == 0)
    def _():
        for l in range(layers):
            ogn[l] = sn[4 * l : 4 * l + 2]
            osn[l] = sn[4 * l + 2 : 4 * l + 4]
        ogw[...] = sw[0:layers]
        osw[...] = sw[layers : 2 * layers]


def finish_call(plan, pos, raw_frames, layers, wide, narrow, y, g, packed, small):
    n = y.shape[0]
    steps = 8
    per = raw_frames // steps
    packed = [p.reshape(-1, LANES) for p in packed]
    whole = lambda a: pl.BlockSpec(a.shape, lambda i, p: (0,) * len(a.shape), pipeline_mode=pl.Buffered(1))
    keep = lambda shape: pl.BlockSpec(shape, lambda i, p: (0,) * len(shape))
    big = pl.BlockSpec((per, SPOT, wide), lambda i, p: (i, 0, 0))
    shape = jax.ShapeDtypeStruct
    tiny = ((layers, 2, narrow), (layers, 2, narrow), (layers, wide), (layers, wide))
    outs = (
        shape((raw_frames, SPOT, wide), BF16), shape((raw_frames, SPOT, wide), BF16),
        shape((layers, wide, narrow), F32), shape((layers, narrow, narrow), F32),
        shape((layers, 3, 3, 3, narrow), F32), shape((layers, narrow, wide), F32),
    ) + tuple(shape(a, F32) for a in tiny)
    return pl.pallas_call(
        functools.partial(finish_kernel, plan, layers, wide, narrow, steps),
        out_shape=outs,
        grid_spec=pltpu.PrefetchScalarGridSpec(
            num_scalar_prefetch=1,
            grid=(steps,),
            in_specs=[whole(y), whole(g)] + [whole(p) for p in packed] + [whole(a) for a in small],
            out_specs=(
                big, big,
                pl.BlockSpec((layers, wide // steps, narrow), lambda i, p: (0, i, 0)),
                pl.BlockSpec((layers, narrow // steps, narrow), lambda i, p: (0, i, 0)),
                keep((layers, 3, 3, 3, narrow)),
                pl.BlockSpec((layers, narrow // steps, wide), lambda i, p: (0, i, 0)),
            ) + tuple(keep(a) for a in tiny),
        ),
        compiler_params=pltpu.CompilerParams(vmem_limit_bytes=62 * 1024 * 1024),
    )(pos, y, g, *packed, *small)


def fast_body(
    sizes, frames, live_all, activations, stride, clip_order, cotangent, w_reduce, w_mix, w_depth, w_expand,
    gains_narrow, shifts_narrow, gains_wide, shifts_wide,
):
    na, nw, nc = sizes
    clips, frame_len, hh, ww, wide = activations.shape
    narrow = w_reduce.shape[2]
    layers = w_reduce.shape[0]
    raw_frames = clips * frame_len
    mine = jnp.sum(jnp.where(jnp.arange(nc)[:, None] == lax.axis_index("clip"), live_all, 0), axis=0)
    slots = jnp.arange(clips, dtype=jnp.int32)
    ends = jnp.sum(jnp.where(slots[None, :] <= slots[:, None], mine[None, :], 0), axis=1)
    raw = jnp.arange(raw_frames, dtype=jnp.int32)
    raw_clip, raw_step = raw // frame_len, raw % frame_len
    starts = ends - mine
    pos = jnp.sum(jnp.where(raw_clip[:, None] == slots[None, :], jnp.where(raw_step[:, None] < mine[None, :], (starts[None, :] + raw_step[:, None]), -1), 0), axis=1).astype(jnp.int32)
    res = mega_call(
        sizes, frames, clips, activations.reshape(raw_frames, SPOT, wide), cotangent.reshape(raw_frames, SPOT, wide),
        stride, clip_order, w_reduce, w_mix, w_depth, w_expand,
        gains_narrow, shifts_narrow, gains_wide, shifts_wide,
    )
    out = finish_call(
        pack_plan(sizes, wide, narrow), pos, raw_frames, layers, wide, narrow, res[0], res[1].reshape(res[0].shape), res[2:5], res[5:]
    )
    return (out[0].reshape(activations.shape), out[1].reshape(activations.shape)) + tuple(out[2:])


def body(
    sizes, frames, activations, stride, clip_order, cotangent, w_reduce, w_mix, w_depth, w_expand,
    gains_narrow, shifts_narrow, gains_wide, shifts_wide,
):
    clips, frame_len = activations.shape[:2]
    numbers = jnp.arange(stride.shape[0], dtype=jnp.int32)
    picked = jnp.sum(jnp.where(clip_order[:, None] == numbers[None, :], stride[None, :], 0), axis=1)
    live_all = (frame_len // picked).reshape(sizes[2], clips)
    params = (w_reduce, w_mix, w_depth, w_expand, gains_narrow, shifts_narrow, gains_wide, shifts_wide)
    fits = jnp.max(jnp.sum(live_all, axis=1)) <= frames
    return lax.cond(
        fits,
        lambda: fast_body(sizes, frames, live_all, activations, stride, clip_order, cotangent, *params),
        lambda: plain_body(activations, stride, clip_order, cotangent, *params),
    )


def solution(mesh, frames=96):
    sizes = tuple(mesh.shape[a] for a in AXES)
    big = P("clip", None, "ha", "wa", None)
    return jax.shard_map(
        functools.partial(body, sizes, frames),
        mesh=mesh,
        in_specs=(big, P(), P(), big) + (P(),) * 8,
        out_specs=(big, big) + (P(),) * 8,
        check_vma=False,
    )
```

```python
import functools
import math

import jax
import jax.numpy as jnp
from jax import lax
from jax.experimental import pallas as pl
from jax.experimental.pallas import tpu as pltpu
from jax.sharding import PartitionSpec as P

EPSILON = 1e-05
AXES = ("ha", "wa", "clip")
MESH = pl.DeviceIdType.MESH
F32 = jnp.float32
BF16 = jnp.bfloat16
ROWS = 2
COLS = 8
SPOT = ROWS * COLS
LANES = 128


def dot(a, b):
    return jnp.dot(a, b, preferred_element_type=F32)


def dot_first(a, b):
    return lax.dot_general(a, b, (((0,), (0,)), ((), ())), preferred_element_type=F32)


def sigmoid(v):
    return jax.nn.sigmoid(v)


def slope_of(z):
    s = sigmoid(z)
    return s * (1.0 + z * (1.0 - s))


def get(ref, spot):
    return jnp.concatenate([ref[lb, spot, :] for lb in range(ref.shape[0])], axis=-1)


def put(ref, spot, value):
    for lb in range(ref.shape[0]):
        ref[lb, spot, :] = value[:, lb * LANES : (lb + 1) * LANES]


def fold8(v):
    return jnp.sum(v.reshape(v.shape[0] // 8, 8, v.shape[1]), axis=0)


def split_dot(v, w):
    high = v.astype(BF16)
    low = (v - high.astype(F32)).astype(BF16)
    return dot(high, w) + dot(low, w)


def mega(sizes, clips, frame_len, layers, wide, narrow, plan, *refs):
    (
        stride_ref, order_ref, x_hbm, cot_hbm, wred_ref, wmix_ref, wdep_ref, wexp_ref,
        gn_ref, sn_ref, gw_ref, sw_ref,
        y_ref, gx_ref, packed_a, packed_b, packed_c, small_n, small_w,
        flag_ref, xc, u, x1, s0, red, mown, spat, h2, g2, gm, mtop, mbot, mside,
        vm8, vflag, wtap, hu, gram, wtr, wtb, wmt,
        row_send, col_send, top_in, bot_in, side_in, top_sp, bot_sp, side_sp,
        nar_a, nar_b, wid_a, wid_b,
        load_sem, ar_send, ar_recv, halo_send, halo_recv, wg_send, wg_recv, *pack_refs
    ) = refs
    n = clips * frame_len
    CH = n // 2
    rows = n * SPOT
    na, nw, nc = sizes
    ne = nw * nc
    me = {a: lax.axis_index(a) for a in AXES}
    my_a = me["ha"]
    my_e = me["wa"] * nc + me["clip"]
    exists = {
        (-1, 0): my_a > 0, (1, 0): my_a < na - 1,
    }
    for dw, here in ((-1, me["wa"] > 0), (1, me["wa"] < nw - 1)):
        exists[(0, dw)] = here
        for dh in (-1, 1):
            exists[(dh, dw)] = jnp.logical_and(exists[(dh, 0)], here)

    def at(ha=None, wa=None, clip=None):
        return (
            me["ha"] if ha is None else ha,
            me["wa"] if wa is None else wa,
            me["clip"] if clip is None else clip,
        )

    def a_peer(k):
        return at(ha=lax.rem(my_a + k, na))

    def e_peer(k):
        p = lax.rem(my_e + k, ne)
        return at(wa=p // nc, clip=lax.rem(p, nc))

    world = na * ne
    one_shot = world <= 64 and world & (world - 1) == 0
    my_d = (me["clip"] * nw + me["wa"]) * na + my_a

    def d_peer(k):
        k = world - k
        p = 0
        bit = 1
        while bit < world:
            p = p + bit * lax.rem(lax.rem(my_d // bit, 2) + lax.rem(k // bit, 2), 2)
            bit *= 2
        return at(ha=lax.rem(p, na), wa=lax.rem(p // na, nw), clip=p // (na * nw))

    barrier = pltpu.get_barrier_semaphore()

    load = pltpu.make_async_copy(x_hbm, xc, load_sem.at[0])
    load.start()
    load2 = pltpu.make_async_copy(cot_hbm, u, load_sem.at[1])
    load2.start()

    def greet_a(k, c):
        pl.semaphore_signal(barrier, inc=1, device_id=a_peer(k), device_id_type=MESH)
        return c

    def greet_e(k, c):
        pl.semaphore_signal(barrier, inc=1, device_id=e_peer(k), device_id_type=MESH)
        return c

    def greet_d(k, c):
        pl.semaphore_signal(barrier, inc=1, device_id=d_peer(k), device_id_type=MESH)
        return c

    if one_shot:
        lax.fori_loop(1, world, greet_d, 0)
        expected = world - 1
    else:
        lax.fori_loop(1, na, greet_a, 0)
        lax.fori_loop(1, ne, greet_e, 0)
        expected = na - 1 + ne - 1
        for dh in (-1, 1):
            for dw in (-1, 1):
                ok = exists[(dh, dw)]
                expected = expected + ok.astype(jnp.int32)

                @pl.when(ok)
                def _():
                    pl.semaphore_signal(
                        barrier, inc=1, device_id=at(ha=my_a + dh, wa=me["wa"] + dw), device_id_type=MESH
                    )

    def live_of(slot):
        return stride_ref[order_ref[slot]]

    base_slot = me["clip"] * clips

    def list_frame(k, c):
        step = k % frame_len
        one = jnp.where((step + 1) * live_of(base_slot + k // frame_len) <= frame_len, 1.0, 0.0)
        flag_ref[0, k] = one
        flag_ref[1, k] = jnp.where(step > 0, one, 0.0)
        flag_ref[2, k + 1] = one
        return c

    lax.fori_loop(0, n, list_frame, 0)
    flag_ref[0, n] = 0.0
    flag_ref[1, n] = 0.0
    flag_ref[2, 0] = 0.0

    def group_frames(group):
        def add(slot, total):
            pace = live_of(group * clips + slot)
            one = jnp.where(pace == 1, frame_len, jnp.where(pace == 2, frame_len // 2, frame_len // 4))
            return total + one

        return lax.fori_loop(0, clips, add, jnp.int32(0))

    group_count = [(group_frames(g) * SPOT).astype(F32) for g in range(nc)]
    total_count = sum(group_count) * float(na * nw)
    my_frames = group_count[0]
    for g in range(1, nc):
        my_frames = jnp.where(me["clip"] == g, group_count[g], my_frames)
    widths = (narrow, wide)
    total_inv = {w: 1.0 / jnp.full((1, w), total_count, F32) for w in widths}
    my_count_inv = {w: 1.0 / jnp.full((1, w), my_frames, F32) for w in widths}
    group_inv = [{w: 1.0 / jnp.full((1, w), c, F32) for w in widths} for c in group_count]

    def set_mask(f, c):
        vm8[pl.ds(pl.multiple_of(f * 8, 8), 8), :] = jnp.full((8, LANES), flag_ref[0, f], F32)
        for i, flag in enumerate((flag_ref[1, f], flag_ref[0, f], flag_ref[1, f + 1])):
            vflag[i, pl.ds(f, 1), :] = jnp.full((1, LANES), flag, F32)
        return c

    lax.fori_loop(0, n, set_mask, 0)
    for l in range(layers):
        for i in range(27):
            tap = wdep_ref[l, i // 9, i // 3 % 3].astype(F32)[i % 3 : i % 3 + 1]
            wtap[l, i] = jnp.broadcast_to(tap, (8, narrow))
        wtr[l] = wred_ref[l].T
        wtb[l] = wexp_ref[l].T
        wmt[l] = wmix_ref[l].T
        for lb in range(narrow // LANES):
            mown[l, lb, 0:SPOT] = jnp.zeros((SPOT, LANES), F32)
            mown[l, lb, SPOT + rows : SPOT + rows + SPOT] = jnp.zeros((SPOT, LANES), F32)
    mtop[...] = jnp.zeros_like(mtop)
    mbot[...] = jnp.zeros_like(mbot)
    mside[...] = jnp.zeros_like(mside)

    pl.semaphore_wait(barrier, expected)

    def finish(got, moments, slots, group_of, share):
        total = jnp.sum(got, axis=0)
        if not moments:
            return total[0:1], total[1:2]
        w = got.shape[-1]
        average = total[0:1] * total_inv[w]
        extra = [jnp.zeros((1, w), F32)] * 4
        for j in range(slots):
            g = group_of(j)
            off = got[j, 0:1] * (group_inv[g][w] * (1.0 / share)) - average
            extra[j % 4] = extra[j % 4] + off * off * (group_count[g] * float(share))
        second = total[1:2] + ((extra[0] + extra[1]) + (extra[2] + extra[3]))
        return average, lax.rsqrt(second * total_inv[w] + EPSILON)

    def pair_start(number, buf_a, buf_b, slot, value, moments):
        w = value.shape[-1]
        if na > 1:
            buf_a[slot, my_a] = value

            def send_a(k, c):
                pltpu.make_async_remote_copy(
                    src_ref=buf_a.at[slot, my_a], dst_ref=buf_a.at[slot, my_a],
                    send_sem=ar_send.at[number, 0], recv_sem=ar_recv.at[number, 0],
                    device_id=a_peer(k), device_id_type=MESH,
                ).start()
                return c

            lax.fori_loop(1, na, send_a, 0)
            part = buf_a.at[slot, pl.ds(0, na - 1)]
            pltpu.make_async_copy(part, part, ar_recv.at[number, 0]).wait()
            pltpu.make_async_copy(part, part, ar_send.at[number, 0]).wait()
            got = buf_a[slot]
            total = jnp.sum(got, axis=0)
            if moments:
                off = got[:, 0:1] - (total[0:1] * (1.0 / na))[None]
                extra = jnp.sum(off * off, axis=0) * my_count_inv[w]
                total = jnp.concatenate([total[0:1], total[1:2] + extra], axis=0)
            value = total
        buf_b[slot, my_e] = value

        def send_e(k, c):
            pltpu.make_async_remote_copy(
                src_ref=buf_b.at[slot, my_e], dst_ref=buf_b.at[slot, my_e],
                send_sem=ar_send.at[number, 1], recv_sem=ar_recv.at[number, 1],
                device_id=e_peer(k), device_id_type=MESH,
            ).start()
            return c

        lax.fori_loop(1, ne, send_e, 0)

    def bulk_wait(number, buf, slot, count):
        part = buf.at[slot, pl.ds(0, count)]
        pltpu.make_async_copy(part, part, ar_recv.at[number, 1]).wait()
        pltpu.make_async_copy(part, part, ar_send.at[number, 1]).wait()

    def reduce_start(number, buf_a, buf_b, slot, value, moments):
        if not (one_shot and value.shape[-1] == narrow):
            pair_start(number, buf_a, buf_b, slot, value, moments)
            return
        buf_b[slot, my_d] = value

        def send_d(k, c):
            pltpu.make_async_remote_copy(
                src_ref=buf_b.at[slot, my_d], dst_ref=buf_b.at[slot, my_d],
                send_sem=ar_send.at[number, 1], recv_sem=ar_recv.at[number, 1],
                device_id=d_peer(k), device_id_type=MESH,
            ).start()
            return c

        lax.fori_loop(1, world, send_d, 0)

    def reduce_finish(number, buf_b, slot, moments):
        if one_shot and buf_b.shape[-1] == narrow:
            bulk_wait(number, buf_b, slot, world - 1)
            return finish(buf_b[slot], moments, world, lambda j: j // (na * nw), 1)
        bulk_wait(number, buf_b, slot, ne - 1)
        return finish(buf_b[slot], moments, ne, lambda j: j % nc, na)

    def local_moments(first, square):
        total = jnp.sum(first, axis=0, keepdims=True)
        second = jnp.sum(square, axis=0, keepdims=True) - total * total * my_count_inv[total.shape[-1]]
        return jnp.concatenate([total, second], axis=0)

    def plain_pair(first, second):
        return jnp.concatenate(
            [jnp.sum(first, axis=0, keepdims=True), jnp.sum(second, axis=0, keepdims=True)], axis=0
        )

    def rim_list(r_send, c_send, top, bot, side):
        return [
            (1, 0, r_send.at[1], top), (-1, 0, r_send.at[0], bot),
            (0, 1, c_send.at[1], side.at[pl.ds(1, 2)]), (0, -1, c_send.at[0], side.at[pl.ds(5, 2)]),
            (1, 1, c_send.at[1, 1], side.at[0]), (-1, 1, c_send.at[1, 0], side.at[3]),
            (1, -1, c_send.at[0, 1], side.at[4]), (-1, -1, c_send.at[0, 0], side.at[7]),
        ]

    def rim_copy(number, k, item):
        dh, dw, src, dst = item
        return pltpu.make_async_remote_copy(
            src_ref=src, dst_ref=dst, send_sem=halo_send.at[number, k], recv_sem=halo_recv.at[number, k],
            device_id=at(ha=my_a + dh, wa=me["wa"] + dw), device_id_type=MESH,
        )

    def rim_start(number, items):
        for k, item in enumerate(items):
            @pl.when(exists[(item[0], item[1])])
            def _():
                rim_copy(number, k, item).start()

    def rim_sent(number, items):
        for k, item in enumerate(items):
            @pl.when(exists[(item[0], item[1])])
            def _():
                rim_copy(number, k, item).wait_send()

    def rim_arrived(number, items, which):
        for k in which:
            item = items[k]

            @pl.when(exists[(-item[0], -item[1])])
            def _():
                rim_copy(number, k, item).wait_recv()

    def fill_send(source, base):
        def rows_body(c, carry):
            tile = get(source, pl.ds(pl.multiple_of(base + c * CH * SPOT, SPOT), CH * SPOT))
            tile = tile.reshape(CH, ROWS, COLS, narrow)
            spot = pl.ds(pl.multiple_of(c * CH * COLS, CH * COLS), CH * COLS)
            for h in range(ROWS):
                row_send[h, spot, :] = tile[:, h].reshape(CH * COLS, narrow).astype(BF16)
            return carry

        lax.fori_loop(0, n // CH, rows_body, 0)
        for h in range(ROWS):
            for side, col in ((0, 0), (1, COLS - 1)):
                col_send[side, h] = get(source, pl.ds(base + h * COLS + col, n, stride=SPOT)).astype(BF16)

    def over_rim(apply):
        half = CH * COLS
        for key, which in ((-1, 0), (1, 1)):
            @pl.when(exists[(key, 0)])
            def _():
                dst = (mtop, mbot)[which]

                def body(c, carry):
                    spot = pl.ds(pl.multiple_of(c * half, half), half)
                    put(dst, spot, apply(
                        lambda: (top_in, bot_in)[which][spot, :].astype(F32),
                        lambda l: (top_sp, bot_sp)[which][l, spot, :].astype(F32),
                    ))
                    return carry

                lax.fori_loop(0, n // CH, body, 0)

    def over_sides(apply):
        for dw, base in ((-1, 0), (1, 4)):
            for r in range(4):
                dh = -1 if r == 0 else (1 if r == 3 else 0)

                @pl.when(exists[(dh, dw)])
                def _():
                    put(mside.at[base + r], pl.ds(8, n), apply(
                        lambda: side_in[base + r].astype(F32), lambda l: side_sp[l, base + r].astype(F32)
                    ))

    def side_sums(l, flip, target, base):
        stats = []
        for lb in range(narrow // LANES):
            lanes = pl.ds(lb * LANES, LANES)
            first = jnp.zeros((8, LANES), F32)
            square = jnp.zeros((8, LANES), F32)
            for side, e, col in ((0, 0, 0), (4, 2, COLS - 1)):
                for h in range(ROWS):
                    total = None
                    for a in range(3):
                        part = None
                        for b in range(3):
                            i = (a * 3 + b) * 3 + e
                            weight = wtap[l, 26 - i if flip else i, 0:1, lanes]
                            term = mside[side + h + b, lb, 7 + a : 7 + a + n, :] * weight
                            part = term if part is None else part + term
                        part = part * vflag[a] if a != 1 else part
                        total = part if total is None else total + part
                    total = total * vflag[1]
                    spot = pl.ds(base + 8 * h + col, n, stride=SPOT)
                    old = target[lb, spot, :]
                    new = old + total
                    target[lb, spot, :] = new
                    first = first + fold8(total)
                    square = square + fold8((new - old) * (new + old))
            stats.append((first, square))
        return stats

    row_id = lax.broadcasted_iota(jnp.int32, (8, LANES), 0)

    def shifted(own, own_base, f, lb):
        start = own_base + f * SPOT
        lines = [
            mtop[lb, pl.ds(pl.multiple_of(f * 8, 8), 8), :],
            own[lb, pl.ds(pl.multiple_of(start, 8), 8), :],
            own[lb, pl.ds(pl.multiple_of(start + 8, 8), 8), :],
            mbot[lb, pl.ds(pl.multiple_of(f * 8, 8), 8), :],
        ]
        out = []
        for v in lines:
            left = jnp.where(row_id == 0, 0.0, pltpu.roll(v, 1, 0))
            right = jnp.where(row_id == 7, 0.0, pltpu.roll(v, 7, 0))
            out.append((left, v, right))
        return out

    def tap_sum(grid, l, lanes, a, flip):
        res = []
        for h in range(ROWS):
            total = None
            for b in range(3):
                for e in range(3):
                    i = (a * 3 + b) * 3 + e
                    term = grid[h + b][e] * wtap[l, 26 - i if flip else i, :, lanes]
                    total = term if total is None else total + term
            res.append(total)
        return res

    def vmask(c):
        m = vm8[pl.ds(pl.multiple_of(c * CH * 8, CH * 8), CH * 8), :]
        m = jnp.broadcast_to(m.reshape(CH, 1, 8, LANES), (CH, ROWS, 8, LANES)).reshape(CH * SPOT, LANES)
        return jnp.concatenate([m] * (narrow // LANES), axis=1)

    def chunk(c):
        return pl.ds(pl.multiple_of(c * CH * SPOT, CH * SPOT), CH * SPOT)

    def chunk_off(c, base):
        return pl.ds(pl.multiple_of(base + c * CH * SPOT, SPOT), CH * SPOT)

    zero8 = jnp.zeros((8, narrow), F32)
    blocks = [pl.ds(k * narrow, narrow) for k in range(wide // narrow)]
    steps = n // CH
    scal = {}

    def reduce_phase(l):
        source = xc if l == 0 else x1

        def body(c, carry):
            first, square = carry
            r = dot(source[chunk(c), :], wred_ref[l])
            put(red.at[l], chunk(c), r)
            kept = r * vmask(c) if l == 0 else r
            return first + fold8(kept), square + fold8(kept * r)

        first, square = lax.fori_loop(0, steps, body, (zero8, zero8))
        reduce_start(3 * l, nar_a, nar_b, 2 * l, local_moments(first, square), True)
        fill_send(red.at[l], 0)
        rim_start(l, rims)

    def mix_phase(l):
        average, inv = reduce_finish(3 * l, nar_b, 2 * l, True)
        scale = gn_ref[l, 0:1] * inv
        shift = sn_ref[l, 0:1] - average * scale
        scal["one", l] = (average, inv, scale, shift)

        def body(c, carry):
            z = get(red.at[l], chunk(c)) * scale + shift
            h = (z * sigmoid(z)).astype(BF16)
            put(mown.at[l], chunk_off(c, SPOT), dot(h, wmix_ref[l]))
            return carry

        lax.fori_loop(0, steps, body, 0)
        rim_arrived(l, rims, range(2))

        def apply(arrived, second):
            z = arrived() * scale + shift
            return dot((z * sigmoid(z)).astype(BF16), wmix_ref[l])

        over_rim(apply)
        return apply

    def spatial_phase(l, apply):
        stats = []
        for lb in range(narrow // LANES):
            lanes = pl.ds(lb * LANES, LANES)

            def body(f, carry):
                cur, nxt, first, square = carry
                grid = shifted(mown.at[l], SPOT, f, lb)
                here = flag_ref[1, f]
                t2 = tap_sum(grid, l, lanes, 2, False)
                t1 = tap_sum(grid, l, lanes, 1, False)
                t0 = tap_sum(grid, l, lanes, 0, False)
                alive = flag_ref[2, f]
                for h in range(ROWS):
                    done = (cur[h] + here * t2[h]) * alive
                    spat[l, lb, pl.ds(pl.multiple_of(f * SPOT + 8 * h, 8), 8), :] = done
                    first = first + done
                    square = square + done * done
                cur = tuple(t1[h] + here * nxt[h] for h in range(ROWS))
                return cur, tuple(t0), first, square

            z = jnp.zeros((8, LANES), F32)
            cur, nxt, first, square = lax.fori_loop(0, n, body, ((z, z), (z, z), z, z))
            for h in range(ROWS):
                done = cur[h] * flag_ref[2, n]
                spat[l, lb, rows + 8 * h : rows + 8 * h + 8, :] = done
                first = first + done
                square = square + done * done
            stats.append((first, square))
        rim_arrived(l, rims, range(2, 8))
        over_sides(apply)
        more = side_sums(l, False, spat.at[l], SPOT)
        rim_sent(l, rims)
        first = jnp.concatenate([s[0] + m[0] for s, m in zip(stats, more)], axis=1)
        square = jnp.concatenate([s[1] + m[1] for s, m in zip(stats, more)], axis=1)
        reduce_start(3 * l + 1, nar_a, nar_b, 2 * l + 1, local_moments(first, square), True)
        fill_send(spat.at[l], SPOT)
        rim_start(layers + l, rims_sp[l])

    def hidden_phase(l):
        average, inv = reduce_finish(3 * l + 1, nar_b, 2 * l + 1, True)
        scale = gn_ref[l, 1:2] * inv
        shift = sn_ref[l, 1:2] - average * scale
        scal["two", l] = (average, inv, scale, shift)

        def body(c, first):
            z = get(spat.at[l], chunk_off(c, SPOT)) * scale + shift
            h = z * sigmoid(z) * vmask(c)
            low = h.astype(BF16)
            h2[l, chunk(c), :] = low
            return first + fold8(low.astype(F32))

        first = lax.fori_loop(0, steps, body, zero8)
        g = dot_first(h2[l], h2[l])
        gram[l] = g
        t = split_dot(g, wexp_ref[l])
        square = jnp.sum(t * wexp_ref[l].astype(F32), axis=0, keepdims=True)
        hsum = jnp.sum(first, axis=0, keepdims=True)
        scal["hsum", l] = hsum
        both = split_dot(jnp.broadcast_to(hsum, (8, narrow)), wexp_ref[l])[0:1]
        second = square - both * both * my_count_inv[wide]
        reduce_start(3 * l + 2, wid_a, wid_b, l, jnp.concatenate([both, second], axis=0), True)
        rim_sent(layers + l, rims_sp[l])

    def widen_phase(l):
        average, inv = reduce_finish(3 * l + 2, wid_b, l, True)
        scale = gw_ref[l : l + 1] * inv
        shift = sw_ref[l : l + 1] - average * scale
        scal["wide", l] = (average, inv, scale, shift)
        source = xc if l == 0 else x1
        last = l == layers - 1

        def body(c, sums):
            out = []
            hid = h2[l, chunk(c), :]
            mask = vmask(c)
            for k, blk in enumerate(blocks):
                cut = slice(k * narrow, (k + 1) * narrow)
                w = dot(hid, wexp_ref[l, :, blk])
                summed = source[chunk(c), blk].astype(F32) + (w * scale[:, cut] + shift[:, cut])
                s = sigmoid(summed)
                y = summed * s
                if not last:
                    x1[chunk(c), blk] = (y * mask).astype(BF16)
                    s0[chunk(c), blk] = summed.astype(BF16)
                else:
                    xc[chunk(c), blk] = (y * mask).astype(BF16)
                    up = u[chunk(c), blk].astype(F32) * (s * (1.0 + summed * (1.0 - s))) * mask
                    low = up.astype(BF16)
                    u[chunk(c), blk] = low
                    out.append(sums[k] + fold8(low.astype(F32)))
            return tuple(out)

        return lax.fori_loop(0, steps, body, tuple(zero8 for _ in blocks) if last else ())

    def back_wide(l, sums):
        total = jnp.concatenate([jnp.sum(s, axis=0, keepdims=True) for s in sums], axis=1)
        second = []
        for blk in blocks:
            part = dot_first(h2[l], u[:, blk])
            hu[:, blk] = part
            second.append(jnp.sum(part * wexp_ref[l, :, blk].astype(F32), axis=0, keepdims=True))
        second = jnp.concatenate(second, axis=1)
        reduce_start(
            3 * layers + 3 * l, wid_a, wid_b, layers + l, jnp.concatenate([total, second], axis=0), False
        )

    def back_expand(l):
        gshift, gsec = reduce_finish(3 * layers + 3 * l, wid_b, layers + l, False)
        average, inv, scale, _ = scal["wide", l]
        ggain = inv * (gsec - average * gshift)
        small_w[l : l + 1] = ggain
        small_w[layers + l : layers + l + 1] = gshift
        drift = inv * ggain * total_inv[wide]
        weight = wexp_ref[l].astype(F32)
        awt = (weight * scale).T.astype(BF16)
        mx = dot((weight * (scale * drift)).astype(BF16), wtb[l])
        base = scale * (gshift * total_inv[wide] - average * drift)
        const = split_dot(jnp.broadcast_to(base, (8, wide)), wtb[l])[0:1]
        mx = mx.astype(BF16)
        wtb[l] = awt
        _, _, scale2, shift2 = scal["two", l]
        avg2, inv2, _, _ = scal["two", l]

        def body(c, carry):
            first, square = carry
            p = dot(u[chunk(c), :], wtb[l]) - dot(h2[l, chunk(c), :], mx) - const
            sp = get(spat.at[l], chunk_off(c, SPOT))
            g = p * slope_of(sp * scale2 + shift2) * vmask(c)
            put(g2, chunk(c), g)
            normed = (sp - avg2) * inv2
            return first + fold8(g), square + fold8(g * normed)

        first, square = lax.fori_loop(0, steps, body, (zero8, zero8))
        reduce_start(
            3 * layers + 3 * l + 1, nar_a, nar_b, 2 * layers + 2 * l, plain_pair(first, square), False
        )
        fill_send(g2, 0)
        rim_start(2 * layers + l, rims)
        hcol = jnp.broadcast_to(scal["hsum", l], (8, narrow)).T[:, 0:1]
        grad = scale * (
            hu[...] - hcol * (gshift * total_inv[wide] - average * drift) - split_dot(gram[l], wexp_ref[l]) * drift
        )
        buf, row = place[("expand", l)]
        for k in range(wide // LANES):
            buf[row + k * narrow : row + (k + 1) * narrow, :] = grad[:, k * LANES : (k + 1) * LANES].astype(BF16)

    def back_spatial(l):
        gshift, ggain = reduce_finish(3 * layers + 3 * l + 1, nar_b, 2 * layers + 2 * l, False)
        small_n[4 * l + 1 : 4 * l + 2] = ggain
        small_n[4 * l + 3 : 4 * l + 4] = gshift
        avg2, inv2, scale2, _ = scal["two", l]
        a_u = scale2
        a_s = scale2 * inv2 * ggain * total_inv[narrow]
        a_c = scale2 * gshift * total_inv[narrow] - a_s * avg2

        def body(c, carry):
            put(g2, chunk(c), a_u * get(g2, chunk(c)) - a_s * get(spat.at[l], chunk_off(c, SPOT)) - a_c)
            return carry

        lax.fori_loop(0, steps, body, 0)
        rim_arrived(2 * layers + l, rims, range(2))
        rim_arrived(layers + l, rims_sp[l], range(8))
        apply = lambda arrived, second: a_u * arrived() - a_s * second(l) - a_c
        over_rim(apply)
        tap_grads = []

        for lb in range(narrow // LANES):
            lanes = pl.ds(lb * LANES, LANES)
            if l == 0 and lb == 0:
                step_b(1)
            if l == 0 and lb == 1:
                step_a(4)
                step_b(2)

            def body(f, carry):
                cur, nxt, grads = carry
                grid = shifted(g2, 0, f, lb)
                here = flag_ref[1, f]
                after = flag_ref[1, f + 1]
                live = flag_ref[0, f]
                t2 = tap_sum(grid, l, lanes, 2, True)
                t1 = tap_sum(grid, l, lanes, 1, True)
                t0 = tap_sum(grid, l, lanes, 0, True)
                alive = flag_ref[2, f]
                done = [(cur[h] + here * t2[h]) * alive for h in range(ROWS)]
                spat[l, lb, pl.ds(pl.multiple_of(f * SPOT, SPOT), SPOT), :] = jnp.concatenate(done, axis=0)
                grads = list(grads)
                for a, flag in ((0, here), (1, live), (2, after)):
                    for h in range(ROWS):
                        m = flag * mown[l, lb, pl.ds(pl.multiple_of((f + a) * SPOT + 8 * h, 8), 8), :]
                        for b in range(3):
                            for e in range(3):
                                i = (a * 3 + b) * 3 + e
                                grads[i] = grads[i] + m * grid[h + 2 - b][2 - e]
                cur = tuple(t1[h] + here * nxt[h] for h in range(ROWS))
                return cur, tuple(t0), tuple(grads)

            z = jnp.zeros((8, LANES), F32)
            cur, nxt, grads = lax.fori_loop(0, n, body, ((z, z), (z, z), tuple(z for _ in range(27))))
            spat[l, lb, rows : rows + SPOT, :] = jnp.concatenate(
                [cur[h] * flag_ref[2, n] for h in range(ROWS)], axis=0
            )
            tap_grads.append(list(grads))

        rim_arrived(2 * layers + l, rims, range(2, 8))
        over_sides(apply)
        side_sums(l, True, spat.at[l], SPOT)
        rim_sent(2 * layers + l, rims)
        for lb in range(narrow // LANES):
            grads = tap_grads[lb]
            for side, e, col in ((0, 2, 0), (4, 0, COLS - 1)):
                for a in range(3):
                    for h in range(ROWS):
                        m = mown[l, lb, pl.ds(a * SPOT + 8 * h + col, n, stride=SPOT), :] * vflag[a]
                        for b in range(3):
                            i = (a * 3 + b) * 3 + e
                            grads[i] = grads[i] + fold8(m * mside[side + h + 2 - b, lb, 8 : 8 + n, :])
            folded = [jnp.sum(g, axis=0, keepdims=True) for g in grads]
            folded += [jnp.zeros((1, LANES), F32)] * 5
            buf, row = place[("depth", l)]
            buf[row + lb * 32 : row + lb * 32 + 32, :] = jnp.concatenate(folded, axis=0).astype(BF16)

        avg1, inv1, scale1, shift1 = scal["one", l]

        def body2(c, carry):
            first, square = carry
            low = get(spat.at[l], chunk_off(c, SPOT)).astype(BF16)
            gm[chunk(c), :] = low
            r = get(red.at[l], chunk(c))
            z = r * scale1 + shift1
            sig = sigmoid(z)
            h2[l, chunk(c), :] = (z * sig).astype(BF16)
            g = dot(low, wmt[l]) * (sig * (1.0 + z * (1.0 - sig)))
            put(g2, chunk(c), g)
            return first + fold8(g), square + fold8(g * ((r - avg1) * inv1))

        first, square = lax.fori_loop(0, steps, body2, (zero8, zero8))
        reduce_start(
            3 * layers + 3 * l + 2, nar_a, nar_b, 2 * layers + 2 * l + 1, plain_pair(first, square), False
        )
        buf, row = place[("mix", l)]
        grad = dot_first(h2[l], gm[...]).astype(BF16)
        for k in range(narrow // LANES):
            buf[row + k * narrow : row + (k + 1) * narrow, :] = grad[:, k * LANES : (k + 1) * LANES]

    def back_reduce(l):
        gshift, ggain = reduce_finish(3 * layers + 3 * l + 2, nar_b, 2 * layers + 2 * l + 1, False)
        small_n[4 * l : 4 * l + 1] = ggain
        small_n[4 * l + 2 : 4 * l + 3] = gshift
        avg1, inv1, scale1, _ = scal["one", l]
        a_u = scale1
        a_s = scale1 * inv1 * ggain * total_inv[narrow]
        a_c = scale1 * gshift * total_inv[narrow] - a_s * avg1

        def body(c, sums):
            gr = (a_u * get(g2, chunk(c)) - a_s * get(red.at[l], chunk(c)) - a_c) * vmask(c)
            gr = gr.astype(BF16)
            gm[chunk(c), :] = gr
            if l == 0:
                return ()
            out = []
            for k, blk in enumerate(blocks):
                g = u[chunk(c), blk].astype(F32) + dot(gr, wtr[l, :, blk])
                up = g * slope_of(s0[chunk(c), blk].astype(F32))
                low = up.astype(BF16)
                u[chunk(c), blk] = low
                out.append(sums[k] + fold8(low.astype(F32)))
            return tuple(out)

        sums = lax.fori_loop(0, steps, body, tuple(zero8 for _ in blocks) if l > 0 else ())
        return sums

    def input_grads(c):
        for blk in blocks:
            g = u[chunk(c), blk].astype(F32) + dot(gm[chunk(c), :], wtr[0, :, blk])
            u[chunk(c), blk] = g.astype(BF16)
        pltpu.make_async_copy(u.at[chunk(c)], gx_ref.at[chunk(c)], load_sem.at[3]).start()

    def back_reduce_weight(l):
        source = xc if l == 0 else x1
        for k, blk in enumerate(blocks):
            buf, row = place[("reduce", l)]
            grad = dot_first(gm[...], source[:, blk]).T.astype(BF16)
            for lb in range(narrow // LANES):
                first = row + lb * wide + k * narrow
                buf[first : first + narrow, :] = grad[:, lb * LANES : (lb + 1) * LANES]

    groups = {
        "ha": (na, my_a, a_peer),
        "wa": (nw, me["wa"], lambda k: at(wa=lax.rem(me["wa"] + k, nw))),
        "clip": (nc, me["clip"], lambda k: at(clip=lax.rem(me["clip"] + k, nc))),
        "all": (ne, my_e, e_peer),
    }

    def bytes_wait(ref, count, sem):
        part = ref.at[pl.ds(0, count)]
        pltpu.make_async_copy(part, part, sem).wait()

    def pack_step(number, stages, bufs, out_hbm):
        wb, recvs, gats = bufs
        total_rows = wb.shape[0]
        sizes_of = []
        left = total_rows
        for st in stages:
            sizes_of.append((left, left // groups[st][0]))
            left //= groups[st][0]
        last = len(stages) - 1

        def send_seg(i):
            size, mine, peer = groups[stages[i]]
            seg = sizes_of[i][1]
            src = wb if i == 0 else gats[i - 1].at[groups[stages[i - 1]][1]]

            def send(k, c):
                target = lax.rem(mine + k, size)
                pltpu.make_async_remote_copy(
                    src_ref=src.at[pl.ds(pl.multiple_of(target * seg, 16), seg)], dst_ref=recvs[i].at[mine],
                    send_sem=wg_send.at[number, i], recv_sem=wg_recv.at[number, i],
                    device_id=peer(k), device_id_type=MESH,
                ).start()
                return c

            lax.fori_loop(1, size, send, 0)
            recvs[i][mine] = src[pl.ds(pl.multiple_of(mine * seg, 16), seg), :]

        def add_up(i):
            size, mine, _ = groups[stages[i]]
            seg = sizes_of[i][1]
            if size > 1:
                bytes_wait(recvs[i], size - 1, wg_recv.at[number, i])
                bytes_wait(recvs[i], size - 1, wg_send.at[number, i])

            def add(c, carry):
                spot = pl.ds(pl.multiple_of(c * 16, 16), 16)
                total = recvs[i][0, spot, :].astype(F32)
                for j in range(1, size):
                    total = total + recvs[i][j, spot, :].astype(F32)
                gats[i][mine, spot, :] = total.astype(BF16)
                return carry

            lax.fori_loop(0, seg // 16, add, 0)

        def send_back(i):
            size, mine, peer = groups[stages[i]]
            k_sem = 2 * len(stages) - 1 - i

            def send(k, c):
                pltpu.make_async_remote_copy(
                    src_ref=gats[i].at[mine], dst_ref=gats[i].at[mine],
                    send_sem=wg_send.at[number, k_sem], recv_sem=wg_recv.at[number, k_sem],
                    device_id=peer(k), device_id_type=MESH,
                ).start()
                return c

            lax.fori_loop(1, size, send, 0)

        def got_back(i):
            size = groups[stages[i]][0]
            k_sem = 2 * len(stages) - 1 - i
            if size > 1:
                bytes_wait(gats[i], size - 1, wg_recv.at[number, k_sem])
                bytes_wait(gats[i], size - 1, wg_send.at[number, k_sem])

        def down(i):
            mine = groups[stages[i]][1]
            seg = sizes_of[i + 1][1]

            def keep(j, c):
                gats[i][mine, pl.ds(pl.multiple_of(j * seg, 16), seg), :] = gats[i + 1][j]
                return c

            lax.fori_loop(0, groups[stages[i + 1]][0], keep, 0)

        def step(k):
            if k <= last:
                if k > 0:
                    add_up(k - 1)
                send_seg(k)
            elif k == last + 1:
                add_up(last)
                send_back(last)
            elif k <= 2 * last + 1:
                i = 2 * last + 1 - k
                got_back(i + 1)
                down(i)
                send_back(i)
            else:
                got_back(0)
                copy = pltpu.make_async_copy(gats[0], out_hbm, load_sem.at[4 + number])
                copy.start()

        def stored():
            pltpu.make_async_copy(gats[0], out_hbm, load_sem.at[4 + number]).wait()

        return step, stored

    rims = rim_list(row_send, col_send, top_in, bot_in, side_in)
    rims_sp = [rim_list(row_send, col_send, top_sp.at[l], bot_sp.at[l], side_sp.at[l]) for l in range(layers)]

    place = {}
    packs = []
    at_ref = 0
    for number, (parts, stages, padded, used) in enumerate(plan):
        m = len(stages)
        bufs = (pack_refs[at_ref] if number < 2 else packs_first, pack_refs[at_ref + 1 : at_ref + 1 + m], pack_refs[at_ref + 1 + m : at_ref + 1 + 2 * m])
        if number == 0:
            packs_first = pack_refs[at_ref]
        at_ref += 1 + 2 * m
        for key, row, _ in parts:
            place[key] = (bufs[0], row)
        if padded > used:
            bufs[0][used:padded, :] = jnp.zeros((padded - used, LANES), BF16)
        packs.append(pack_step(number, stages, bufs, (packed_a, packed_b, packed_c)[number]))
    (step_a, stored_a), (step_b, stored_b), (step_c, stored_c) = packs

    load.wait()
    for l in range(layers):
        reduce_phase(l)
        spatial_phase(l, mix_phase(l))
        hidden_phase(l)
        if l == layers - 1:
            load2.wait()
        sums = widen_phase(l)
    store_y = pltpu.make_async_copy(xc, y_ref, load_sem.at[2])
    store_y.start()
    load_again = pltpu.make_async_copy(x_hbm, xc, load_sem.at[0])
    for l in reversed(range(layers)):
        back_wide(l, sums)
        if l == 0:
            store_y.wait()
            load_again.start()
            back_reduce_weight(1)
            step_a(2)
        back_expand(l)
        if l == 0:
            step_a(3)
            step_b(0)
        back_spatial(l)
        if l == 0:
            step_a(5)
            step_b(3)
        else:
            step_a(0)
        sums = back_reduce(l)
        if l == 0:
            step_a(6)
            step_b(4)
        else:
            step_a(1)
    load_again.wait()
    back_reduce_weight(0)
    step_c(0)
    input_grads(0)
    step_c(1)
    step_b(5)
    input_grads(1)
    step_b(6)
    step_c(2)
    step_c(3)
    step_c(4)
    pltpu.make_async_copy(u, gx_ref, load_sem.at[3]).wait()
    stored_a()
    stored_b()
    stored_c()


def pack_plan(sizes, wide, narrow):
    world = sizes[0] * sizes[1] * sizes[2]
    plan = []
    for names, stages in (
        ((("expand", 1), ("mix", 1), ("depth", 1)), ("ha", "wa", "clip")),
        ((("reduce", 1), ("expand", 0)), ("ha", "wa", "clip")),
        ((("reduce", 0), ("mix", 0), ("depth", 0)), ("ha", "all")),
    ):
        nb = narrow // LANES
        rows = {"reduce": nb * wide, "expand": nb * wide, "mix": nb * narrow, "depth": nb * 32}
        used = 0
        parts = []
        for key in names:
            parts.append((key, used, rows[key[0]]))
            used += rows[key[0]]
        padded = -(-used // (16 * world)) * 16 * world
        plan.append((parts, stages, padded, used))
    return plan


def mega_call(sizes, clips, x, cot, stride, order, w_reduce, w_mix, w_depth, w_expand, gn, sn, gw, sw):
    na, nw, nc = sizes
    ne = nw * nc
    layers, wide, narrow = w_reduce.shape
    n = x.shape[0] // SPOT
    rows = n * SPOT
    plan = pack_plan(sizes, wide, narrow)
    group_size = {"ha": na, "wa": nw, "clip": nc, "all": ne}
    vmem = lambda shape, kind: pltpu.VMEM(shape, kind)
    half = n * COLS
    kernel = functools.partial(mega, sizes, clips, n // clips, layers, wide, narrow, plan)
    spec = pl.BlockSpec(memory_space=pltpu.VMEM)
    smem = pl.BlockSpec(memory_space=pltpu.SMEM)
    hbm = pl.BlockSpec(memory_space=pl.ANY)
    n_sync = 6 * layers
    nb = narrow // LANES
    world = na * ne
    slots = world if world <= 64 and world & (world - 1) == 0 else ne
    scratch = [
        pltpu.SMEM((3, n + 1), F32),
        vmem((rows, wide), BF16), vmem((rows, wide), BF16), vmem((rows, wide), BF16), vmem((rows, wide), BF16),
        vmem((layers, nb, rows, LANES), F32),
        vmem((layers, nb, rows + 2 * SPOT, LANES), F32), vmem((layers, nb, rows + SPOT, LANES), F32),
        vmem((layers, rows, narrow), BF16), vmem((nb, rows, LANES), F32), vmem((rows, narrow), BF16),
        vmem((nb, half, LANES), F32), vmem((nb, half, LANES), F32), vmem((8, nb, n + 16, LANES), F32),
        vmem((half, LANES), F32), vmem((3, n, LANES), F32), vmem((layers, 27, 8, narrow), F32), vmem((narrow, wide), F32),
        vmem((layers, narrow, narrow), F32),
        vmem((layers, narrow, wide), BF16), vmem((layers, wide, narrow), BF16), vmem((layers, narrow, narrow), BF16),
        vmem((2, half, narrow), BF16), vmem((2, 2, n, narrow), BF16),
        vmem((half, narrow), BF16), vmem((half, narrow), BF16), vmem((8, n, narrow), BF16),
        vmem((layers, half, narrow), BF16), vmem((layers, half, narrow), BF16), vmem((layers, 8, n, narrow), BF16),
        vmem((4 * layers, na, 2, narrow), F32), vmem((4 * layers, slots, 2, narrow), F32),
        vmem((2 * layers, na, 2, wide), F32), vmem((2 * layers, ne, 2, wide), F32),
        pltpu.SemaphoreType.DMA((4 + len(plan),)), pltpu.SemaphoreType.DMA((n_sync, 2)), pltpu.SemaphoreType.DMA((n_sync, 2)),
        pltpu.SemaphoreType.DMA((3 * layers, 8)), pltpu.SemaphoreType.DMA((3 * layers, 8)),
        pltpu.SemaphoreType.DMA((len(plan), 6)), pltpu.SemaphoreType.DMA((len(plan), 6)),
    ]
    outs_packed = []
    for number, (_, stages, padded, _) in enumerate(plan):
        scratch.append(vmem((padded if number < 2 else 16, LANES), BF16))
        recvs, gats, left = [], [], padded
        for st in stages:
            left //= group_size[st]
            recvs.append(vmem((group_size[st], left, LANES), BF16))
            gats.append(vmem((group_size[st], left, LANES), BF16))
        scratch += recvs + gats
        outs_packed.append(jax.ShapeDtypeStruct(gats[0].shape, BF16))
    shape = jax.ShapeDtypeStruct
    outs = (
        shape((rows, wide), BF16), shape((rows, wide), BF16),
        *outs_packed,
        shape((4 * layers, narrow), F32), shape((2 * layers, wide), F32),
    )
    return pl.pallas_call(
        kernel,
        out_shape=outs,
        in_specs=[smem, smem, hbm, hbm] + [spec] * 8,
        out_specs=(hbm,) * 5 + (spec,) * 2,
        scratch_shapes=scratch,
        compiler_params=pltpu.CompilerParams(
            collective_id=0, has_side_effects=True, vmem_limit_bytes=63 * 1024 * 1024
        ),
    )(stride, order, x, cot, w_reduce, w_mix, w_depth, w_expand, gn, sn, gw, sw)


def finish_kernel(plan, layers, wide, narrow, steps, *refs):
    y_ref, g_ref, pa, pb, pc, sn, sw, oy, og, owr, owm, owd, owe, ogn, osn, ogw, osw = refs
    i = pl.program_id(0)
    oy[...] = y_ref[...]
    og[...] = g_ref[...]
    packed = (pa, pb, pc)
    rows_r, rows_m = wide // steps, narrow // steps
    for number, (parts, _, _, _) in enumerate(plan):
        for (kind, l), row, _ in parts:
            ref = packed[number]
            if kind == "expand":
                for k in range(wide // LANES):
                    spot = pl.ds(pl.multiple_of(row + k * narrow + i * rows_m, 16), rows_m)
                    owe[l, :, k * LANES : (k + 1) * LANES] = ref[spot, :].astype(F32)
            elif kind != "depth":
                dst, size, part = (owr, wide, rows_r) if kind == "reduce" else (owm, narrow, rows_m)
                for lb in range(narrow // LANES):
                    spot = pl.ds(pl.multiple_of(row + lb * size + i * part, 16), part)
                    dst[l, :, lb * LANES : (lb + 1) * LANES] = ref[spot, :].astype(F32)
            else:
                @pl.when(i == 0)
                def _():
                    taps = jnp.concatenate([ref[row + lb * 32 : row + lb * 32 + 32, :] for lb in range(narrow // LANES)], axis=1).astype(F32)
                    for a in range(3):
                        for b in range(3):
                            first = (a * 3 + b) * 3
                            owd[l, a, b] = taps[first : first + 3]

    @pl.when(i == 0)
    def _():
        for l in range(layers):
            ogn[l] = sn[4 * l : 4 * l + 2]
            osn[l] = sn[4 * l + 2 : 4 * l + 4]
        ogw[...] = sw[0:layers]
        osw[...] = sw[layers : 2 * layers]


def finish_call(plan, layers, wide, narrow, y, g, packed, small):
    steps = 8
    per = y.shape[0] // steps
    packed = [p.reshape(-1, LANES) for p in packed]
    whole = lambda a: pl.BlockSpec(a.shape, lambda i: (0,) * len(a.shape), pipeline_mode=pl.Buffered(1))
    keep = lambda shape: pl.BlockSpec(shape, lambda i: (0,) * len(shape))
    big = pl.BlockSpec((per, wide), lambda i: (i, 0))
    shape = jax.ShapeDtypeStruct
    tiny = ((layers, 2, narrow), (layers, 2, narrow), (layers, wide), (layers, wide))
    outs = (
        shape(y.shape, BF16), shape(y.shape, BF16),
        shape((layers, wide, narrow), F32), shape((layers, narrow, narrow), F32),
        shape((layers, 3, 3, 3, narrow), F32), shape((layers, narrow, wide), F32),
    ) + tuple(shape(a, F32) for a in tiny)
    return pl.pallas_call(
        functools.partial(finish_kernel, plan, layers, wide, narrow, steps),
        out_shape=outs,
        grid=(steps,),
        in_specs=[big, big] + [whole(p) for p in packed] + [whole(a) for a in small],
        out_specs=(
            big, big,
            pl.BlockSpec((layers, wide // steps, narrow), lambda i: (0, i, 0)),
            pl.BlockSpec((layers, narrow // steps, narrow), lambda i: (0, i, 0)),
            keep((layers, 3, 3, 3, narrow)),
            pl.BlockSpec((layers, narrow // steps, wide), lambda i: (0, i, 0)),
        ) + tuple(keep(a) for a in tiny),
        compiler_params=pltpu.CompilerParams(vmem_limit_bytes=62 * 1024 * 1024),
    )(y, g, *packed, *small)


def body(
    sizes, activations, stride, clip_order, cotangent, w_reduce, w_mix, w_depth, w_expand,
    gains_narrow, shifts_narrow, gains_wide, shifts_wide,
):
    clips, frame_len, _, _, wide = activations.shape
    layers, _, narrow = w_reduce.shape
    flat = (clips * frame_len * SPOT, wide)
    res = mega_call(
        sizes, clips, activations.reshape(flat), cotangent.reshape(flat),
        stride, clip_order, w_reduce, w_mix, w_depth, w_expand,
        gains_narrow, shifts_narrow, gains_wide, shifts_wide,
    )
    out = finish_call(pack_plan(sizes, wide, narrow), layers, wide, narrow, res[0], res[1], res[2:5], res[5:])
    return (out[0].reshape(activations.shape), out[1].reshape(activations.shape)) + tuple(out[2:])


def solution(mesh):
    sizes = tuple(mesh.shape[a] for a in AXES)
    big = P("clip", None, "ha", "wa", None)
    return jax.shard_map(
        functools.partial(body, sizes),
        mesh=mesh,
        in_specs=(big, P(), P(), big) + (P(),) * 8,
        out_specs=(big, big) + (P(),) * 8,
        check_vma=False,
    )
```

```python
import functools
import math

import jax
import jax.numpy as jnp
from jax import lax
from jax.experimental import pallas as pl
from jax.experimental.pallas import tpu as pltpu
from jax.sharding import PartitionSpec as P

EPSILON = 1e-05
AXES = ("ha", "wa", "clip")
MESH = pl.DeviceIdType.MESH
F32 = jnp.float32
BF16 = jnp.bfloat16
ROWS = 2
COLS = 8
SPOT = ROWS * COLS
LANES = 128
UNROLL_F = 2
UNROLL_B = 2
FINISH_STEPS = 4
ROOT_COPY = False


def dot(a, b):
    return jnp.dot(a, b, preferred_element_type=F32)


def dot_first(a, b):
    return lax.dot_general(a, b, (((0,), (0,)), ((), ())), preferred_element_type=F32)


def sigmoid(v):
    return jax.nn.sigmoid(v)


def slope_of(z):
    s = sigmoid(z)
    return s * (1.0 + z * (1.0 - s))


def get(ref, spot):
    return jnp.concatenate([ref[lb, spot, :] for lb in range(ref.shape[0])], axis=-1)


def put(ref, spot, value):
    for lb in range(ref.shape[0]):
        ref[lb, spot, :] = value[:, lb * LANES : (lb + 1) * LANES]


def fold8(v):
    return jnp.sum(v.reshape(v.shape[0] // 8, 8, v.shape[1]), axis=0)


def split_dot(v, w):
    high = v.astype(BF16)
    low = (v - high.astype(F32)).astype(BF16)
    return dot(high, w) + dot(low, w)


def mega(sizes, clips, frame_len, layers, wide, narrow, plan, *refs):
    (
        stride_ref, order_ref, x_hbm, cot_hbm, wred_ref, wmix_ref, wdep_ref, wexp_ref,
        gn_ref, sn_ref, gw_ref, sw_ref,
        y_ref, gx_ref, packed_a, packed_b, packed_c, packed_d, small_n, small_w,
        flag_ref, xc, u, x1, s0, red, mown, spat, h2, g2, gm, mtop, mbot, mside,
        vm8, vflag, wtap, hu, gram, wtr, wtb, wmt,
        row_send, col_send, top_in, bot_in, side_in, top_sp, bot_sp, side_sp,
        nar_a, nar_b, wid_a, wid_b,
        load_sem, ar_send, ar_recv, halo_send, halo_recv, wg_send, wg_recv, *pack_refs
    ) = refs
    n = clips * frame_len
    CH = n // 2
    rows = n * SPOT
    na, nw, nc = sizes
    ne = nw * nc
    me = {a: lax.axis_index(a) for a in AXES}
    my_a = me["ha"]
    my_e = me["wa"] * nc + me["clip"]
    exists = {
        (-1, 0): my_a > 0, (1, 0): my_a < na - 1,
    }
    for dw, here in ((-1, me["wa"] > 0), (1, me["wa"] < nw - 1)):
        exists[(0, dw)] = here
        for dh in (-1, 1):
            exists[(dh, dw)] = jnp.logical_and(exists[(dh, 0)], here)

    def at(ha=None, wa=None, clip=None):
        return (
            me["ha"] if ha is None else ha,
            me["wa"] if wa is None else wa,
            me["clip"] if clip is None else clip,
        )

    def a_peer(k):
        return at(ha=lax.rem(my_a + k, na))

    def e_peer(k):
        p = lax.rem(my_e + k, ne)
        return at(wa=p // nc, clip=lax.rem(p, nc))

    world = na * ne
    one_shot = world <= 64 and world & (world - 1) == 0
    my_d = (me["clip"] * nw + me["wa"]) * na + my_a

    def d_peer(k):
        k = world - k
        p = 0
        bit = 1
        while bit < world:
            p = p + bit * lax.rem(lax.rem(my_d // bit, 2) + lax.rem(k // bit, 2), 2)
            bit *= 2
        return at(ha=lax.rem(p, na), wa=lax.rem(p // na, nw), clip=p // (na * nw))

    barrier = pltpu.get_barrier_semaphore()

    load = pltpu.make_async_copy(x_hbm, xc, load_sem.at[0])
    load.start()
    load2 = pltpu.make_async_copy(cot_hbm, u, load_sem.at[1])
    load2.start()

    def greet_a(k, c):
        pl.semaphore_signal(barrier, inc=1, device_id=a_peer(k), device_id_type=MESH)
        return c

    def greet_e(k, c):
        pl.semaphore_signal(barrier, inc=1, device_id=e_peer(k), device_id_type=MESH)
        return c

    def greet_d(k, c):
        pl.semaphore_signal(barrier, inc=1, device_id=d_peer(k), device_id_type=MESH)
        return c

    if one_shot:
        lax.fori_loop(1, world, greet_d, 0)
        expected = world - 1
    else:
        lax.fori_loop(1, na, greet_a, 0)
        lax.fori_loop(1, ne, greet_e, 0)
        expected = na - 1 + ne - 1
        for dh in (-1, 1):
            for dw in (-1, 1):
                ok = exists[(dh, dw)]
                expected = expected + ok.astype(jnp.int32)

                @pl.when(ok)
                def _():
                    pl.semaphore_signal(
                        barrier, inc=1, device_id=at(ha=my_a + dh, wa=me["wa"] + dw), device_id_type=MESH
                    )

    def live_of(slot):
        return stride_ref[order_ref[slot]]

    base_slot = me["clip"] * clips

    def list_frame(k, c):
        step = k % frame_len
        one = jnp.where((step + 1) * live_of(base_slot + k // frame_len) <= frame_len, 1.0, 0.0)
        flag_ref[0, k] = one
        flag_ref[1, k] = jnp.where(step > 0, one, 0.0)
        flag_ref[2, k + 1] = one
        return c

    lax.fori_loop(0, n, list_frame, 0)
    flag_ref[0, n] = 0.0
    flag_ref[1, n] = 0.0
    flag_ref[2, 0] = 0.0

    def group_frames(group):
        def add(slot, total):
            pace = live_of(group * clips + slot)
            one = jnp.where(pace == 1, frame_len, jnp.where(pace == 2, frame_len // 2, frame_len // 4))
            return total + one

        return lax.fori_loop(0, clips, add, jnp.int32(0))

    group_count = [(group_frames(g) * SPOT).astype(F32) for g in range(nc)]
    total_count = sum(group_count) * float(na * nw)
    my_frames = group_count[0]
    for g in range(1, nc):
        my_frames = jnp.where(me["clip"] == g, group_count[g], my_frames)
    widths = (narrow, wide)
    total_inv = {w: 1.0 / jnp.full((1, w), total_count, F32) for w in widths}
    my_count_inv = {w: 1.0 / jnp.full((1, w), my_frames, F32) for w in widths}
    group_inv = [{w: 1.0 / jnp.full((1, w), c, F32) for w in widths} for c in group_count]

    def set_mask(f, c):
        vm8[pl.ds(pl.multiple_of(f * 8, 8), 8), :] = jnp.full((8, LANES), flag_ref[0, f], F32)
        for i, flag in enumerate((flag_ref[1, f], flag_ref[0, f], flag_ref[1, f + 1])):
            vflag[i, pl.ds(f, 1), :] = jnp.full((1, LANES), flag, F32)
        return c

    lax.fori_loop(0, n, set_mask, 0)
    for l in range(layers):
        for lb in range(narrow // LANES):
            mown[l, lb, 0:SPOT] = jnp.zeros((SPOT, LANES), F32)
            mown[l, lb, SPOT + rows : SPOT + rows + SPOT] = jnp.zeros((SPOT, LANES), F32)
    mtop[...] = jnp.zeros_like(mtop)
    mbot[...] = jnp.zeros_like(mbot)
    mside[...] = jnp.zeros_like(mside)

    pl.semaphore_wait(barrier, expected)

    def set_taps():
        for l in range(layers):
            for i in range(27):
                tap = wdep_ref[i // 9, i // 3 % 3, i % 3].astype(F32)[l : l + 1]
                wtap[l, i] = jnp.broadcast_to(tap, (8, narrow))

    def turn_weights():
        for l in range(layers):
            wtr[l] = wred_ref[l].T
            wmt[l] = wmix_ref[l].T

    def finish(got, moments, slots, group_of, share):
        total = jnp.sum(got, axis=0)
        if not moments:
            return total[0:1], total[1:2]
        w = got.shape[-1]
        average = total[0:1] * total_inv[w]
        extra = [jnp.zeros((1, w), F32)] * 4
        for j in range(slots):
            g = group_of(j)
            off = got[j, 0:1] * (group_inv[g][w] * (1.0 / share)) - average
            extra[j % 4] = extra[j % 4] + off * off * (group_count[g] * float(share))
        second = total[1:2] + ((extra[0] + extra[1]) + (extra[2] + extra[3]))
        return average, lax.rsqrt(second * total_inv[w] + EPSILON)

    def pair_start(number, buf_a, buf_b, slot, value, moments):
        w = value.shape[-1]
        if na > 1:
            buf_a[slot, my_a] = value

            def send_a(k, c):
                pltpu.make_async_remote_copy(
                    src_ref=buf_a.at[slot, my_a], dst_ref=buf_a.at[slot, my_a],
                    send_sem=ar_send.at[number, 0], recv_sem=ar_recv.at[number, 0],
                    device_id=a_peer(k), device_id_type=MESH,
                ).start()
                return c

            lax.fori_loop(1, na, send_a, 0)
            part = buf_a.at[slot, pl.ds(0, na - 1)]
            pltpu.make_async_copy(part, part, ar_recv.at[number, 0]).wait()
            pltpu.make_async_copy(part, part, ar_send.at[number, 0]).wait()
            got = buf_a[slot]
            total = jnp.sum(got, axis=0)
            if moments:
                off = got[:, 0:1] - (total[0:1] * (1.0 / na))[None]
                extra = jnp.sum(off * off, axis=0) * my_count_inv[w]
                total = jnp.concatenate([total[0:1], total[1:2] + extra], axis=0)
            value = total
        buf_b[slot, my_e] = value

        def send_e(k, c):
            pltpu.make_async_remote_copy(
                src_ref=buf_b.at[slot, my_e], dst_ref=buf_b.at[slot, my_e],
                send_sem=ar_send.at[number, 1], recv_sem=ar_recv.at[number, 1],
                device_id=e_peer(k), device_id_type=MESH,
            ).start()
            return c

        lax.fori_loop(1, ne, send_e, 0)

    def bulk_wait(number, buf, slot, count):
        part = buf.at[slot, pl.ds(0, count)]
        pltpu.make_async_copy(part, part, ar_recv.at[number, 1]).wait()
        pltpu.make_async_copy(part, part, ar_send.at[number, 1]).wait()

    def reduce_start(number, buf_a, buf_b, slot, value, moments):
        if not (one_shot and value.shape[-1] == narrow):
            pair_start(number, buf_a, buf_b, slot, value, moments)
            return
        buf_b[slot, my_d] = value

        def send_d(k, c):
            pltpu.make_async_remote_copy(
                src_ref=buf_b.at[slot, my_d], dst_ref=buf_b.at[slot, my_d],
                send_sem=ar_send.at[number, 1], recv_sem=ar_recv.at[number, 1],
                device_id=d_peer(k), device_id_type=MESH,
            ).start()
            return c

        lax.fori_loop(1, world, send_d, 0)

    def reduce_finish(number, buf_b, slot, moments):
        if one_shot and buf_b.shape[-1] == narrow:
            bulk_wait(number, buf_b, slot, world - 1)
            return finish(buf_b[slot], moments, world, lambda j: j // (na * nw), 1)
        bulk_wait(number, buf_b, slot, ne - 1)
        return finish(buf_b[slot], moments, ne, lambda j: j % nc, na)

    def local_moments(first, square):
        total = jnp.sum(first, axis=0, keepdims=True)
        second = jnp.sum(square, axis=0, keepdims=True) - total * total * my_count_inv[total.shape[-1]]
        return jnp.concatenate([total, second], axis=0)

    def plain_pair(first, second):
        return jnp.concatenate(
            [jnp.sum(first, axis=0, keepdims=True), jnp.sum(second, axis=0, keepdims=True)], axis=0
        )

    def rim_list(r_send, c_send, top, bot, side):
        return [
            (1, 0, r_send.at[1], top), (-1, 0, r_send.at[0], bot),
            (0, 1, c_send.at[1], side.at[pl.ds(1, 2)]), (0, -1, c_send.at[0], side.at[pl.ds(5, 2)]),
            (1, 1, c_send.at[1, 1], side.at[0]), (-1, 1, c_send.at[1, 0], side.at[3]),
            (1, -1, c_send.at[0, 1], side.at[4]), (-1, -1, c_send.at[0, 0], side.at[7]),
        ]

    def rim_copy(number, k, item):
        dh, dw, src, dst = item
        return pltpu.make_async_remote_copy(
            src_ref=src, dst_ref=dst, send_sem=halo_send.at[number, k], recv_sem=halo_recv.at[number, k],
            device_id=at(ha=my_a + dh, wa=me["wa"] + dw), device_id_type=MESH,
        )

    def rim_start(number, items):
        for k, item in enumerate(items):
            @pl.when(exists[(item[0], item[1])])
            def _():
                rim_copy(number, k, item).start()

    def rim_sent(number, items):
        for k, item in enumerate(items):
            @pl.when(exists[(item[0], item[1])])
            def _():
                rim_copy(number, k, item).wait_send()

    def rim_arrived(number, items, which):
        for k in which:
            item = items[k]

            @pl.when(exists[(-item[0], -item[1])])
            def _():
                rim_copy(number, k, item).wait_recv()

    def fill_send(source, base):
        def rows_body(c, carry):
            tile = get(source, pl.ds(pl.multiple_of(base + c * CH * SPOT, SPOT), CH * SPOT))
            tile = tile.reshape(CH, ROWS, COLS, narrow)
            spot = pl.ds(pl.multiple_of(c * CH * COLS, CH * COLS), CH * COLS)
            for h in range(ROWS):
                row_send[h, spot, :] = tile[:, h].reshape(CH * COLS, narrow).astype(BF16)
            return carry

        lax.fori_loop(0, n // CH, rows_body, 0)
        for h in range(ROWS):
            for side, col in ((0, 0), (1, COLS - 1)):
                col_send[side, h] = get(source, pl.ds(base + h * COLS + col, n, stride=SPOT)).astype(BF16)

    def over_rim(apply):
        half = CH * COLS
        for key, which in ((-1, 0), (1, 1)):
            @pl.when(exists[(key, 0)])
            def _():
                dst = (mtop, mbot)[which]

                def body(c, carry):
                    spot = pl.ds(pl.multiple_of(c * half, half), half)
                    put(dst, spot, apply(
                        lambda: (top_in, bot_in)[which][spot, :].astype(F32),
                        lambda l: (top_sp, bot_sp)[which][l, spot, :].astype(F32),
                    ))
                    return carry

                lax.fori_loop(0, n // CH, body, 0)

    def over_sides(apply):
        for dw, base in ((-1, 0), (1, 4)):
            for r in range(4):
                dh = -1 if r == 0 else (1 if r == 3 else 0)

                @pl.when(exists[(dh, dw)])
                def _():
                    put(mside.at[base + r], pl.ds(8, n), apply(
                        lambda: side_in[base + r].astype(F32), lambda l: side_sp[l, base + r].astype(F32)
                    ))

    def side_sums(l, flip, target, base):
        stats = []
        for lb in range(narrow // LANES):
            lanes = pl.ds(lb * LANES, LANES)
            first = jnp.zeros((8, LANES), F32)
            square = jnp.zeros((8, LANES), F32)
            for side, e, col in ((0, 0, 0), (4, 2, COLS - 1)):
                for h in range(ROWS):
                    total = None
                    for a in range(3):
                        part = None
                        for b in range(3):
                            i = (a * 3 + b) * 3 + e
                            weight = wtap[l, 26 - i if flip else i, 0:1, lanes]
                            term = mside[side + h + b, lb, 7 + a : 7 + a + n, :] * weight
                            part = term if part is None else part + term
                        part = part * vflag[a] if a != 1 else part
                        total = part if total is None else total + part
                    total = total * vflag[1]
                    spot = pl.ds(base + 8 * h + col, n, stride=SPOT)
                    old = target[lb, spot, :]
                    new = old + total
                    target[lb, spot, :] = new
                    first = first + fold8(total)
                    square = square + fold8((new - old) * (new + old))
            stats.append((first, square))
        return stats

    row_id = lax.broadcasted_iota(jnp.int32, (8, LANES), 0)

    def shifted(own, own_base, f, lb):
        start = own_base + f * SPOT
        lines = [
            mtop[lb, pl.ds(pl.multiple_of(f * 8, 8), 8), :],
            own[lb, pl.ds(pl.multiple_of(start, 8), 8), :],
            own[lb, pl.ds(pl.multiple_of(start + 8, 8), 8), :],
            mbot[lb, pl.ds(pl.multiple_of(f * 8, 8), 8), :],
        ]
        out = []
        for v in lines:
            left = jnp.where(row_id == 0, 0.0, pltpu.roll(v, 1, 0))
            right = jnp.where(row_id == 7, 0.0, pltpu.roll(v, 7, 0))
            out.append((left, v, right))
        return out

    def tap_sum(grid, l, lanes, a, flip):
        res = []
        for h in range(ROWS):
            total = None
            for b in range(3):
                for e in range(3):
                    i = (a * 3 + b) * 3 + e
                    term = grid[h + b][e] * wtap[l, 26 - i if flip else i, :, lanes]
                    total = term if total is None else total + term
            res.append(total)
        return res

    def vmask(c):
        m = vm8[pl.ds(pl.multiple_of(c * CH * 8, CH * 8), CH * 8), :]
        m = jnp.broadcast_to(m.reshape(CH, 1, 8, LANES), (CH, ROWS, 8, LANES)).reshape(CH * SPOT, LANES)
        return jnp.concatenate([m] * (narrow // LANES), axis=1)

    def chunk(c):
        return pl.ds(pl.multiple_of(c * CH * SPOT, CH * SPOT), CH * SPOT)

    def chunk_off(c, base):
        return pl.ds(pl.multiple_of(base + c * CH * SPOT, SPOT), CH * SPOT)

    zero8 = jnp.zeros((8, narrow), F32)
    blocks = [pl.ds(k * narrow, narrow) for k in range(wide // narrow)]
    steps = n // CH
    scal = {}

    def reduce_phase(l):
        source = xc if l == 0 else x1

        def body(c, carry):
            first, square = carry
            r = dot(source[chunk(c), :], wred_ref[l])
            put(red.at[l], chunk(c), r)
            kept = r * vmask(c) if l == 0 else r
            return first + fold8(kept), square + fold8(kept * r)

        first, square = lax.fori_loop(0, steps, body, (zero8, zero8))
        reduce_start(3 * l, nar_a, nar_b, 2 * l, local_moments(first, square), True)
        fill_send(red.at[l], 0)
        rim_start(l, rims)
        if l == 0:
            set_taps()

    def mix_phase(l):
        average, inv = reduce_finish(3 * l, nar_b, 2 * l, True)
        scale = gn_ref[l, 0:1] * inv
        shift = sn_ref[l, 0:1] - average * scale
        scal["one", l] = (average, inv, scale, shift)

        def body(c, carry):
            z = get(red.at[l], chunk(c)) * scale + shift
            h = (z * sigmoid(z)).astype(BF16)
            put(mown.at[l], chunk_off(c, SPOT), dot(h, wmix_ref[l]))
            return carry

        lax.fori_loop(0, steps, body, 0)
        rim_arrived(l, rims, range(2))

        def apply(arrived, second):
            z = arrived() * scale + shift
            return dot((z * sigmoid(z)).astype(BF16), wmix_ref[l])

        over_rim(apply)
        return apply

    def spatial_phase(l, apply):
        stats = []
        for lb in range(narrow // LANES):
            lanes = pl.ds(lb * LANES, LANES)

            def body(f, carry):
                cur, nxt, first, square = carry
                grid = shifted(mown.at[l], SPOT, f, lb)
                here = flag_ref[1, f]
                t2 = tap_sum(grid, l, lanes, 2, False)
                t1 = tap_sum(grid, l, lanes, 1, False)
                t0 = tap_sum(grid, l, lanes, 0, False)
                alive = flag_ref[2, f]
                for h in range(ROWS):
                    done = (cur[h] + here * t2[h]) * alive
                    spat[l, lb, pl.ds(pl.multiple_of(f * SPOT + 8 * h, 8), 8), :] = done
                    first = first + done
                    square = square + done * done
                cur = tuple(t1[h] + here * nxt[h] for h in range(ROWS))
                return cur, tuple(t0), first, square

            z = jnp.zeros((8, LANES), F32)
            cur, nxt, first, square = lax.fori_loop(0, n, body, ((z, z), (z, z), z, z), unroll=UNROLL_F)
            for h in range(ROWS):
                done = cur[h] * flag_ref[2, n]
                spat[l, lb, rows + 8 * h : rows + 8 * h + 8, :] = done
                first = first + done
                square = square + done * done
            stats.append((first, square))
        rim_arrived(l, rims, range(2, 8))
        over_sides(apply)
        more = side_sums(l, False, spat.at[l], SPOT)
        rim_sent(l, rims)
        first = jnp.concatenate([s[0] + m[0] for s, m in zip(stats, more)], axis=1)
        square = jnp.concatenate([s[1] + m[1] for s, m in zip(stats, more)], axis=1)
        reduce_start(3 * l + 1, nar_a, nar_b, 2 * l + 1, local_moments(first, square), True)
        fill_send(spat.at[l], SPOT)
        rim_start(layers + l, rims_sp[l])
        if l == 0:
            turn_weights()

    def hidden_phase(l):
        average, inv = reduce_finish(3 * l + 1, nar_b, 2 * l + 1, True)
        scale = gn_ref[l, 1:2] * inv
        shift = sn_ref[l, 1:2] - average * scale
        scal["two", l] = (average, inv, scale, shift)

        def body(c, first):
            z = get(spat.at[l], chunk_off(c, SPOT)) * scale + shift
            h = z * sigmoid(z) * vmask(c)
            low = h.astype(BF16)
            h2[l, chunk(c), :] = low
            return first + fold8(low.astype(F32))

        first = lax.fori_loop(0, steps, body, zero8)
        g = dot_first(h2[l], h2[l])
        gram[l] = g
        t = split_dot(g, wexp_ref[l])
        square = jnp.sum(t * wexp_ref[l].astype(F32), axis=0, keepdims=True)
        hsum = jnp.sum(first, axis=0, keepdims=True)
        scal["hsum", l] = hsum
        both = split_dot(jnp.broadcast_to(hsum, (8, narrow)), wexp_ref[l])[0:1]
        second = square - both * both * my_count_inv[wide]
        reduce_start(3 * l + 2, wid_a, wid_b, l, jnp.concatenate([both, second], axis=0), True)
        rim_sent(layers + l, rims_sp[l])

    def widen_phase(l):
        average, inv = reduce_finish(3 * l + 2, wid_b, l, True)
        scale = gw_ref[l : l + 1] * inv
        shift = sw_ref[l : l + 1] - average * scale
        scal["wide", l] = (average, inv, scale, shift)
        source = xc if l == 0 else x1
        last = l == layers - 1

        def body(c, sums):
            out = []
            hid = h2[l, chunk(c), :]
            mask = vmask(c)
            for k, blk in enumerate(blocks):
                cut = slice(k * narrow, (k + 1) * narrow)
                w = dot(hid, wexp_ref[l, :, blk])
                summed = source[chunk(c), blk].astype(F32) + (w * scale[:, cut] + shift[:, cut])
                s = sigmoid(summed)
                y = summed * s
                if not last:
                    x1[chunk(c), blk] = (y * mask).astype(BF16)
                    s0[chunk(c), blk] = summed.astype(BF16)
                else:
                    xc[chunk(c), blk] = (y * mask).astype(BF16)
                    up = u[chunk(c), blk].astype(F32) * (s * (1.0 + summed * (1.0 - s))) * mask
                    low = up.astype(BF16)
                    u[chunk(c), blk] = low
                    out.append(sums[k] + fold8(low.astype(F32)))
            return tuple(out)

        return lax.fori_loop(0, steps, body, tuple(zero8 for _ in blocks) if last else ())

    def back_wide(l, sums):
        total = jnp.concatenate([jnp.sum(s, axis=0, keepdims=True) for s in sums], axis=1)
        second = []
        for blk in blocks:
            part = dot_first(h2[l], u[:, blk])
            hu[:, blk] = part
            second.append(jnp.sum(part * wexp_ref[l, :, blk].astype(F32), axis=0, keepdims=True))
        second = jnp.concatenate(second, axis=1)
        reduce_start(
            3 * layers + 3 * l, wid_a, wid_b, layers + l, jnp.concatenate([total, second], axis=0), False
        )
        wtb[...] = (wexp_ref[l].astype(F32) * scal["wide", l][2]).T.astype(BF16)

        def body(c, carry):
            put(g2, chunk(c), dot(u[chunk(c), :], wtb[...]))
            return carry

        lax.fori_loop(0, steps, body, 0)

    def back_expand(l):
        gshift, gsec = reduce_finish(3 * layers + 3 * l, wid_b, layers + l, False)
        average, inv, scale, _ = scal["wide", l]
        ggain = inv * (gsec - average * gshift)
        small_w[l : l + 1] = ggain
        small_w[layers + l : layers + l + 1] = gshift
        drift = inv * ggain * total_inv[wide]
        mx = dot((wexp_ref[l].astype(F32) * drift).astype(BF16), wtb[...]).astype(BF16)
        base = gshift * total_inv[wide] - average * drift
        const = split_dot(jnp.broadcast_to(base, (8, wide)), wtb[...])[0:1]
        _, _, scale2, shift2 = scal["two", l]
        avg2, inv2, _, _ = scal["two", l]

        def body(c, carry):
            first, square = carry
            p = get(g2, chunk(c)) - dot(h2[l, chunk(c), :], mx) - const
            sp = get(spat.at[l], chunk_off(c, SPOT))
            g = p * slope_of(sp * scale2 + shift2) * vmask(c)
            put(g2, chunk(c), g)
            normed = (sp - avg2) * inv2
            return first + fold8(g), square + fold8(g * normed)

        first, square = lax.fori_loop(0, steps, body, (zero8, zero8))
        reduce_start(
            3 * layers + 3 * l + 1, nar_a, nar_b, 2 * layers + 2 * l, plain_pair(first, square), False
        )
        fill_send(g2, 0)
        rim_start(2 * layers + l, rims)
        hcol = jnp.broadcast_to(scal["hsum", l], (8, narrow)).T[:, 0:1]
        grad = scale * (
            hu[...] - hcol * (gshift * total_inv[wide] - average * drift) - split_dot(gram[l], wexp_ref[l]) * drift
        )
        buf, row = place[("expand", l)]
        for k in range(wide // LANES):
            buf[row + k * narrow : row + (k + 1) * narrow, :] = grad[:, k * LANES : (k + 1) * LANES].astype(BF16)

    def back_spatial(l):
        gshift, ggain = reduce_finish(3 * layers + 3 * l + 1, nar_b, 2 * layers + 2 * l, False)
        small_n[4 * l + 1 : 4 * l + 2] = ggain
        small_n[4 * l + 3 : 4 * l + 4] = gshift
        avg2, inv2, scale2, _ = scal["two", l]
        a_u = scale2
        a_s = scale2 * inv2 * ggain * total_inv[narrow]
        a_c = scale2 * gshift * total_inv[narrow] - a_s * avg2

        def body(c, carry):
            put(g2, chunk(c), a_u * get(g2, chunk(c)) - a_s * get(spat.at[l], chunk_off(c, SPOT)) - a_c)
            return carry

        lax.fori_loop(0, steps, body, 0)
        rim_arrived(2 * layers + l, rims, range(2))
        rim_arrived(layers + l, rims_sp[l], range(8))
        apply = lambda arrived, second: a_u * arrived() - a_s * second(l) - a_c
        over_rim(apply)
        tap_grads = []

        for lb in range(narrow // LANES):
            lanes = pl.ds(lb * LANES, LANES)
            if l == 0 and lb == 0:
                step_b(1)
            if l == 0 and lb == 1:
                step_a(4)
                step_b(2)

            def body(f, carry):
                cur, nxt, grads = carry
                grid = shifted(g2, 0, f, lb)
                here = flag_ref[1, f]
                after = flag_ref[1, f + 1]
                live = flag_ref[0, f]
                t2 = tap_sum(grid, l, lanes, 2, True)
                t1 = tap_sum(grid, l, lanes, 1, True)
                t0 = tap_sum(grid, l, lanes, 0, True)
                alive = flag_ref[2, f]
                done = [(cur[h] + here * t2[h]) * alive for h in range(ROWS)]
                spat[l, lb, pl.ds(pl.multiple_of(f * SPOT, SPOT), SPOT), :] = jnp.concatenate(done, axis=0)
                grads = list(grads)
                for a, flag in ((0, here), (1, live), (2, after)):
                    for h in range(ROWS):
                        m = flag * mown[l, lb, pl.ds(pl.multiple_of((f + a) * SPOT + 8 * h, 8), 8), :]
                        for b in range(3):
                            for e in range(3):
                                i = (a * 3 + b) * 3 + e
                                grads[i] = grads[i] + m * grid[h + 2 - b][2 - e]
                cur = tuple(t1[h] + here * nxt[h] for h in range(ROWS))
                return cur, tuple(t0), tuple(grads)

            z = jnp.zeros((8, LANES), F32)
            cur, nxt, grads = lax.fori_loop(0, n, body, ((z, z), (z, z), tuple(z for _ in range(27))), unroll=UNROLL_B)
            spat[l, lb, rows : rows + SPOT, :] = jnp.concatenate(
                [cur[h] * flag_ref[2, n] for h in range(ROWS)], axis=0
            )
            tap_grads.append(list(grads))

        rim_arrived(2 * layers + l, rims, range(2, 8))
        over_sides(apply)
        side_sums(l, True, spat.at[l], SPOT)
        rim_sent(2 * layers + l, rims)
        for lb in range(narrow // LANES):
            grads = tap_grads[lb]
            for side, e, col in ((0, 2, 0), (4, 0, COLS - 1)):
                for a in range(3):
                    for h in range(ROWS):
                        m = mown[l, lb, pl.ds(a * SPOT + 8 * h + col, n, stride=SPOT), :] * vflag[a]
                        for b in range(3):
                            i = (a * 3 + b) * 3 + e
                            grads[i] = grads[i] + fold8(m * mside[side + h + 2 - b, lb, 8 : 8 + n, :])
            folded = [jnp.sum(g, axis=0, keepdims=True) for g in grads]
            folded += [jnp.zeros((1, LANES), F32)] * 5
            buf, row = place[("depth", l)]
            buf[row + lb * 32 : row + lb * 32 + 32, :] = jnp.concatenate(folded, axis=0).astype(BF16)

        avg1, inv1, scale1, shift1 = scal["one", l]

        def body2(c, carry):
            first, square = carry
            low = get(spat.at[l], chunk_off(c, SPOT)).astype(BF16)
            gm[chunk(c), :] = low
            r = get(red.at[l], chunk(c))
            z = r * scale1 + shift1
            sig = sigmoid(z)
            h2[l, chunk(c), :] = (z * sig).astype(BF16)
            g = dot(low, wmt[l]) * (sig * (1.0 + z * (1.0 - sig)))
            put(g2, chunk(c), g)
            return first + fold8(g), square + fold8(g * ((r - avg1) * inv1))

        first, square = lax.fori_loop(0, steps, body2, (zero8, zero8))
        reduce_start(
            3 * layers + 3 * l + 2, nar_a, nar_b, 2 * layers + 2 * l + 1, plain_pair(first, square), False
        )
        buf, row = place[("mix", l)]
        grad = dot_first(h2[l], gm[...]).astype(BF16)
        for k in range(narrow // LANES):
            buf[row + k * narrow : row + (k + 1) * narrow, :] = grad[:, k * LANES : (k + 1) * LANES]

    def back_reduce(l):
        gshift, ggain = reduce_finish(3 * layers + 3 * l + 2, nar_b, 2 * layers + 2 * l + 1, False)
        small_n[4 * l : 4 * l + 1] = ggain
        small_n[4 * l + 2 : 4 * l + 3] = gshift
        avg1, inv1, scale1, _ = scal["one", l]
        a_u = scale1
        a_s = scale1 * inv1 * ggain * total_inv[narrow]
        a_c = scale1 * gshift * total_inv[narrow] - a_s * avg1

        def body(c, sums):
            gr = (a_u * get(g2, chunk(c)) - a_s * get(red.at[l], chunk(c)) - a_c) * vmask(c)
            gr = gr.astype(BF16)
            gm[chunk(c), :] = gr
            if l == 0:
                return ()
            out = []
            for k, blk in enumerate(blocks):
                g = u[chunk(c), blk].astype(F32) + dot(gr, wtr[l, :, blk])
                up = g * slope_of(s0[chunk(c), blk].astype(F32))
                low = up.astype(BF16)
                u[chunk(c), blk] = low
                out.append(sums[k] + fold8(low.astype(F32)))
            return tuple(out)

        sums = lax.fori_loop(0, steps, body, tuple(zero8 for _ in blocks) if l > 0 else ())
        return sums

    def input_grads(c):
        for blk in blocks:
            g = u[chunk(c), blk].astype(F32) + dot(gm[chunk(c), :], wtr[0, :, blk])
            u[chunk(c), blk] = g.astype(BF16)
        pltpu.make_async_copy(u.at[chunk(c)], gx_ref.at[chunk(c)], load_sem.at[3]).start()

    def back_reduce_weight(l):
        source = xc if l == 0 else x1
        for k, blk in enumerate(blocks):
            buf, row = place[("reduce", l)]
            grad = dot_first(gm[...], source[:, blk]).T.astype(BF16)
            for lb in range(narrow // LANES):
                first = row + lb * wide + k * narrow
                buf[first : first + narrow, :] = grad[:, lb * LANES : (lb + 1) * LANES]

    groups = {
        "ha": (na, my_a, a_peer),
        "wa": (nw, me["wa"], lambda k: at(wa=lax.rem(me["wa"] + k, nw))),
        "clip": (nc, me["clip"], lambda k: at(clip=lax.rem(me["clip"] + k, nc))),
        "all": (ne, my_e, e_peer),
    }

    def bytes_wait(ref, count, sem):
        part = ref.at[pl.ds(0, count)]
        pltpu.make_async_copy(part, part, sem).wait()

    def pack_step(number, stages, padded, bufs, out_hbm):
        wb, recvs, gats = bufs
        sizes_of = []
        left = padded
        for st in stages:
            sizes_of.append((left, left // groups[st][0]))
            left //= groups[st][0]
        last = len(stages) - 1

        def send_seg(i):
            size, mine, peer = groups[stages[i]]
            seg = sizes_of[i][1]
            src = wb if i == 0 else gats[i - 1].at[groups[stages[i - 1]][1]]

            def send(k, c):
                target = lax.rem(mine + k, size)
                pltpu.make_async_remote_copy(
                    src_ref=src.at[pl.ds(pl.multiple_of(target * seg, 16), seg)], dst_ref=recvs[i].at[mine],
                    send_sem=wg_send.at[number, i], recv_sem=wg_recv.at[number, i],
                    device_id=peer(k), device_id_type=MESH,
                ).start()
                return c

            lax.fori_loop(1, size, send, 0)
            recvs[i][mine] = src[pl.ds(pl.multiple_of(mine * seg, 16), seg), :]

        def add_up(i):
            size, mine, _ = groups[stages[i]]
            seg = sizes_of[i][1]
            if size > 1:
                bytes_wait(recvs[i], size - 1, wg_recv.at[number, i])
                bytes_wait(recvs[i], size - 1, wg_send.at[number, i])

            def add(c, carry):
                spot = pl.ds(pl.multiple_of(c * 16, 16), 16)
                total = recvs[i][0, spot, :].astype(F32)
                for j in range(1, size):
                    total = total + recvs[i][j, spot, :].astype(F32)
                gats[i][mine, spot, :] = total.astype(BF16)
                return carry

            lax.fori_loop(0, seg // 16, add, 0)

        def send_back(i):
            size, mine, peer = groups[stages[i]]
            k_sem = 2 * len(stages) - 1 - i

            def send(k, c):
                pltpu.make_async_remote_copy(
                    src_ref=gats[i].at[mine], dst_ref=gats[i].at[mine],
                    send_sem=wg_send.at[number, k_sem], recv_sem=wg_recv.at[number, k_sem],
                    device_id=peer(k), device_id_type=MESH,
                ).start()
                return c

            lax.fori_loop(1, size, send, 0)

        def got_back(i):
            size = groups[stages[i]][0]
            k_sem = 2 * len(stages) - 1 - i
            if size > 1:
                bytes_wait(gats[i], size - 1, wg_recv.at[number, k_sem])
                bytes_wait(gats[i], size - 1, wg_send.at[number, k_sem])

        def down(i):
            mine = groups[stages[i]][1]
            seg = sizes_of[i + 1][1]

            def keep(j, c):
                gats[i][mine, pl.ds(pl.multiple_of(j * seg, 16), seg), :] = gats[i + 1][j]
                return c

            lax.fori_loop(0, groups[stages[i + 1]][0], keep, 0)

        def step(k):
            if k <= last:
                if k > 0:
                    add_up(k - 1)
                send_seg(k)
            elif k == last + 1:
                add_up(last)
                send_back(last)
            elif k <= 2 * last + 1:
                i = 2 * last + 1 - k
                got_back(i + 1)
                down(i)
                send_back(i)
            else:
                got_back(0)
                copy = pltpu.make_async_copy(gats[0], out_hbm, load_sem.at[4 + number])
                copy.start()

        def stored():
            pltpu.make_async_copy(gats[0], out_hbm, load_sem.at[4 + number]).wait()

        return step, stored

    rims = rim_list(row_send, col_send, top_in, bot_in, side_in)
    rims_sp = [rim_list(row_send, col_send, top_sp.at[l], bot_sp.at[l], side_sp.at[l]) for l in range(layers)]

    place = {}
    packs = []
    first_bufs = []
    at_ref = 0
    for number, (parts, stages, padded, used) in enumerate(plan):
        m = len(stages)
        bufs = (pack_refs[at_ref] if number < 2 else first_bufs[number - 2], pack_refs[at_ref + 1 : at_ref + 1 + m], pack_refs[at_ref + 1 + m : at_ref + 1 + 2 * m])
        first_bufs.append(pack_refs[at_ref])
        at_ref += 1 + 2 * m
        for key, row, _ in parts:
            place[key] = (bufs[0], row)
        if padded > used and number < 2:
            bufs[0][used:padded, :] = jnp.zeros((padded - used, LANES), BF16)
        packs.append(pack_step(number, stages, padded, bufs, (packed_a, packed_b, packed_c, packed_d)[number]))
    (step_a, stored_a), (step_b, stored_b), (step_c, stored_c), (step_d, stored_d) = packs

    load.wait()
    for l in range(layers):
        reduce_phase(l)
        spatial_phase(l, mix_phase(l))
        hidden_phase(l)
        if l == layers - 1:
            load2.wait()
        sums = widen_phase(l)
    store_y = pltpu.make_async_copy(xc, y_ref, load_sem.at[2])
    store_y.start()
    load_again = pltpu.make_async_copy(x_hbm, xc, load_sem.at[0])
    for l in reversed(range(layers)):
        back_wide(l, sums)
        if l == 0:
            store_y.wait()
            load_again.start()
            back_reduce_weight(1)
            step_a(2)
        back_expand(l)
        if l == 0:
            step_a(3)
            step_b(0)
        back_spatial(l)
        if l == 0:
            step_a(5)
            step_b(3)
            step_d(0)
        else:
            step_a(0)
        sums = back_reduce(l)
        if l == 0:
            step_a(6)
            step_b(4)
        else:
            step_a(1)
    load_again.wait()
    back_reduce_weight(0)
    step_c(0)
    step_d(1)
    input_grads(0)
    step_c(1)
    step_b(5)
    input_grads(1)
    step_d(2)
    step_b(6)
    step_d(3)
    step_c(2)
    step_d(4)
    step_c(3)
    step_c(4)
    pltpu.make_async_copy(u, gx_ref, load_sem.at[3]).wait()
    stored_a()
    stored_b()
    stored_c()
    stored_d()


def pack_plan(sizes, wide, narrow):
    world = sizes[0] * sizes[1] * sizes[2]
    plan = []
    for names, stages in (
        ((("expand", 1), ("mix", 1), ("depth", 1)), ("ha", "wa", "clip")),
        ((("reduce", 1), ("expand", 0)), ("ha", "wa", "clip")),
        ((("reduce", 0),), ("ha", "all")),
        ((("mix", 0), ("depth", 0)), ("ha", "all")),
    ):
        nb = narrow // LANES
        rows = {"reduce": nb * wide, "expand": nb * wide, "mix": nb * narrow, "depth": nb * 32}
        used = 0
        parts = []
        for key in names:
            parts.append((key, used, rows[key[0]]))
            used += rows[key[0]]
        padded = -(-used // (16 * world)) * 16 * world
        plan.append((parts, stages, padded, used))
    return plan


def mega_call(sizes, clips, x, cot, stride, order, w_reduce, w_mix, w_depth, w_expand, gn, sn, gw, sw):
    na, nw, nc = sizes
    ne = nw * nc
    layers, wide, narrow = w_reduce.shape
    n = x.shape[0] // SPOT
    rows = n * SPOT
    plan = pack_plan(sizes, wide, narrow)
    group_size = {"ha": na, "wa": nw, "clip": nc, "all": ne}
    vmem = lambda shape, kind: pltpu.VMEM(shape, kind)
    half = n * COLS
    kernel = functools.partial(mega, sizes, clips, n // clips, layers, wide, narrow, plan)
    spec = pl.BlockSpec(memory_space=pltpu.VMEM)
    smem = pl.BlockSpec(memory_space=pltpu.SMEM)
    hbm = pl.BlockSpec(memory_space=pl.ANY)
    n_sync = 6 * layers
    nb = narrow // LANES
    world = na * ne
    slots = world if world <= 64 and world & (world - 1) == 0 else ne
    scratch = [
        pltpu.SMEM((3, n + 1), F32),
        vmem((rows, wide), BF16), vmem((rows, wide), BF16), vmem((rows, wide), BF16), vmem((rows, wide), BF16),
        vmem((layers, nb, rows, LANES), F32),
        vmem((layers, nb, rows + 2 * SPOT, LANES), F32), vmem((layers, nb, rows + SPOT, LANES), F32),
        vmem((layers, rows, narrow), BF16), vmem((nb, rows, LANES), F32), vmem((rows, narrow), BF16),
        vmem((nb, half, LANES), F32), vmem((nb, half, LANES), F32), vmem((8, nb, n + 16, LANES), F32),
        vmem((half, LANES), F32), vmem((3, n, LANES), F32), vmem((layers, 27, 8, narrow), F32), vmem((narrow, wide), F32),
        vmem((layers, narrow, narrow), F32),
        vmem((layers, narrow, wide), BF16), vmem((wide, narrow), BF16), vmem((layers, narrow, narrow), BF16),
        vmem((2, half, narrow), BF16), vmem((2, 2, n, narrow), BF16),
        vmem((half, narrow), BF16), vmem((half, narrow), BF16), vmem((8, n, narrow), BF16),
        vmem((layers, half, narrow), BF16), vmem((layers, half, narrow), BF16), vmem((layers, 8, n, narrow), BF16),
        vmem((4 * layers, na, 2, narrow), F32), vmem((4 * layers, slots, 2, narrow), F32),
        vmem((2 * layers, na, 2, wide), F32), vmem((2 * layers, ne, 2, wide), F32),
        pltpu.SemaphoreType.DMA((4 + len(plan),)), pltpu.SemaphoreType.DMA((n_sync, 2)), pltpu.SemaphoreType.DMA((n_sync, 2)),
        pltpu.SemaphoreType.DMA((3 * layers, 8)), pltpu.SemaphoreType.DMA((3 * layers, 8)),
        pltpu.SemaphoreType.DMA((len(plan), 6)), pltpu.SemaphoreType.DMA((len(plan), 6)),
    ]
    outs_packed = []
    for number, (_, stages, padded, _) in enumerate(plan):
        scratch.append(vmem((padded if number < 2 else 16, LANES), BF16))
        recvs, gats, left = [], [], padded
        for st in stages:
            left //= group_size[st]
            recvs.append(vmem((group_size[st], left, LANES), BF16))
            gats.append(vmem((group_size[st], left, LANES), BF16))
        scratch += recvs + gats
        outs_packed.append(jax.ShapeDtypeStruct(gats[0].shape, BF16))
    shape = jax.ShapeDtypeStruct
    outs = (
        shape((rows, wide), BF16), shape((rows, wide), BF16),
        *outs_packed,
        shape((4 * layers, narrow), F32), shape((2 * layers, wide), F32),
    )
    return pl.pallas_call(
        kernel,
        out_shape=outs,
        in_specs=[smem, smem, hbm, hbm] + [spec] * 8,
        out_specs=(hbm,) * 6 + (spec,) * 2,
        scratch_shapes=scratch,
        compiler_params=pltpu.CompilerParams(
            collective_id=0, has_side_effects=True, vmem_limit_bytes=63 * 1024 * 1024
        ),
    )(stride, order, x, cot, w_reduce, w_mix, w_depth, w_expand, gn, sn, gw, sw)


def finish_kernel(plan, layers, wide, narrow, steps, *refs):
    if not ROOT_COPY:
        y_ref, g_ref, *refs = refs
        oy, og = refs[6:8]
        refs = refs[:6] + refs[8:]
        oy[...] = y_ref[...]
        og[...] = g_ref[...]
    pa, pb, pc, pd, sn, sw, owr, owm, owd, owe, ogn, osn, ogw, osw = refs
    i = pl.program_id(0)
    packed = (pa, pb, pc, pd)
    rows_r, rows_m = wide // steps, narrow // steps
    for number, (parts, _, _, _) in enumerate(plan):
        for (kind, l), row, _ in parts:
            ref = packed[number]
            if kind == "expand":
                for k in range(wide // LANES):
                    spot = pl.ds(pl.multiple_of(row + k * narrow + i * rows_m, 16), rows_m)
                    owe[l, :, k * LANES : (k + 1) * LANES] = ref[spot, :].astype(F32)
            elif kind != "depth":
                dst, size, part = (owr, wide, rows_r) if kind == "reduce" else (owm, narrow, rows_m)
                for lb in range(narrow // LANES):
                    spot = pl.ds(pl.multiple_of(row + lb * size + i * part, 16), part)
                    dst[l, :, lb * LANES : (lb + 1) * LANES] = ref[spot, :].astype(F32)
            else:
                @pl.when(i == 0)
                def _():
                    taps = jnp.concatenate([ref[row + lb * 32 : row + lb * 32 + 32, :] for lb in range(narrow // LANES)], axis=1).astype(F32)
                    for t in range(27):
                        owd[t // 9, t // 3 % 3, t % 3, l : l + 1, :] = taps[t : t + 1]

    @pl.when(i == 0)
    def _():
        for l in range(layers):
            ogn[l] = sn[4 * l : 4 * l + 2]
            osn[l] = sn[4 * l + 2 : 4 * l + 4]
        ogw[...] = sw[0:layers]
        osw[...] = sw[layers : 2 * layers]


def finish_call(plan, layers, wide, narrow, y, g, packed, small):
    steps = FINISH_STEPS
    per = y.shape[0] // steps
    packed = [p.reshape(-1, LANES) for p in packed]
    whole = lambda a: pl.BlockSpec(a.shape, lambda i: (0,) * len(a.shape), pipeline_mode=pl.Buffered(1))
    keep = lambda shape: pl.BlockSpec(shape, lambda i: (0,) * len(shape))
    big = pl.BlockSpec((per, wide), lambda i: (i, 0))
    shape = jax.ShapeDtypeStruct
    bigs = [] if ROOT_COPY else [big, big]
    tiny = ((layers, 2, narrow), (layers, 2, narrow), (layers, wide), (layers, wide))
    outs = (() if ROOT_COPY else (shape(y.shape, BF16), shape(y.shape, BF16))) + (
        shape((layers, wide, narrow), F32), shape((layers, narrow, narrow), F32),
        shape((3, 3, 3, layers, narrow), F32), shape((layers, narrow, wide), F32),
    ) + tuple(shape(a, F32) for a in tiny)
    return pl.pallas_call(
        functools.partial(finish_kernel, plan, layers, wide, narrow, steps),
        out_shape=outs,
        grid=(steps,),
        in_specs=bigs + [whole(p) for p in packed] + [whole(a) for a in small],
        out_specs=tuple(bigs) + (
            pl.BlockSpec((layers, wide // steps, narrow), lambda i: (0, i, 0)),
            pl.BlockSpec((layers, narrow // steps, narrow), lambda i: (0, i, 0)),
            keep((3, 3, 3, layers, narrow)),
            pl.BlockSpec((layers, narrow // steps, wide), lambda i: (0, i, 0)),
        ) + tuple(keep(a) for a in tiny),
        compiler_params=pltpu.CompilerParams(vmem_limit_bytes=62 * 1024 * 1024),
    )(*(() if ROOT_COPY else (y, g)), *packed, *small)


def body(
    sizes, activations, stride, clip_order, cotangent, w_reduce, w_mix, w_depth, w_expand,
    gains_narrow, shifts_narrow, gains_wide, shifts_wide,
):
    clips, frame_len, _, _, wide = activations.shape
    layers, _, narrow = w_reduce.shape
    flat = (clips * frame_len * SPOT, wide)
    res = mega_call(
        sizes, clips, activations.reshape(flat), cotangent.reshape(flat),
        stride, clip_order, w_reduce, w_mix, jnp.transpose(w_depth, (1, 2, 3, 0, 4)), w_expand,
        gains_narrow, shifts_narrow, gains_wide, shifts_wide,
    )
    out = finish_call(pack_plan(sizes, wide, narrow), layers, wide, narrow, res[0], res[1], res[2:6], res[6:])
    if ROOT_COPY:
        out = (res[0], res[1]) + tuple(out)
    return (
        out[0].reshape(activations.shape), out[1].reshape(activations.shape), out[2], out[3],
        jnp.transpose(out[4], (3, 0, 1, 2, 4)),
    ) + tuple(out[5:])


def solution(mesh):
    sizes = tuple(mesh.shape[a] for a in AXES)
    big = P("clip", None, "ha", "wa", None)
    return jax.shard_map(
        functools.partial(body, sizes),
        mesh=mesh,
        in_specs=(big, P(), P(), big) + (P(),) * 8,
        out_specs=(big, big) + (P(),) * 8,
        check_vma=False,
    )
```

```python
import functools
import math

import jax
import jax.numpy as jnp
from jax import lax
from jax.experimental import pallas as pl
from jax.experimental.pallas import tpu as pltpu
from jax.sharding import PartitionSpec as P

EPSILON = 1e-05
AXES = ("ha", "wa", "clip")
MESH = pl.DeviceIdType.MESH
F32 = jnp.float32
BF16 = jnp.bfloat16
ROWS = 2
COLS = 8
SPOT = ROWS * COLS
LANES = 128
UNROLL_F = 2
UNROLL_B = 2
FINISH_STEPS = 4
ROOT_COPY = False
BIG_DOT = True


def dot(a, b):
    return jnp.dot(a, b, preferred_element_type=F32)


def dot_first(a, b):
    return lax.dot_general(a, b, (((0,), (0,)), ((), ())), preferred_element_type=F32)


def sigmoid(v):
    return jax.nn.sigmoid(v)


def slope_of(z):
    s = sigmoid(z)
    return s * (1.0 + z * (1.0 - s))


def get(ref, spot):
    return jnp.concatenate([ref[lb, spot, :] for lb in range(ref.shape[0])], axis=-1)


def put(ref, spot, value):
    for lb in range(ref.shape[0]):
        ref[lb, spot, :] = value[:, lb * LANES : (lb + 1) * LANES]


def fold8(v):
    return jnp.sum(v.reshape(v.shape[0] // 8, 8, v.shape[1]), axis=0)


def split_dot(v, w):
    high = v.astype(BF16)
    low = (v - high.astype(F32)).astype(BF16)
    return dot(high, w) + dot(low, w)


def mega(sizes, clips, frame_len, layers, wide, narrow, plan, *refs):
    (
        stride_ref, order_ref, x_hbm, cot_hbm, wred_ref, wmix_ref, wdep_ref, wexp_ref,
        gn_ref, sn_ref, gw_ref, sw_ref,
        y_ref, gx_ref, packed_a, packed_b, packed_c, packed_d, small_n, small_w,
        flag_ref, xc, u, x1, s0, red, mown, spat, h2, g2, gm, mtop, mbot, mside,
        vm8, vflag, wtap, hu, gram, wtr, wtb, wmt,
        row_send, col_send, top_in, bot_in, side_in, top_sp, bot_sp, side_sp,
        nar_a, nar_b, wid_a, wid_b,
        load_sem, ar_send, ar_recv, halo_send, halo_recv, wg_send, wg_recv, *pack_refs
    ) = refs
    n = clips * frame_len
    CH = n // 2
    rows = n * SPOT
    na, nw, nc = sizes
    ne = nw * nc
    me = {a: lax.axis_index(a) for a in AXES}
    my_a = me["ha"]
    my_e = me["wa"] * nc + me["clip"]
    exists = {
        (-1, 0): my_a > 0, (1, 0): my_a < na - 1,
    }
    for dw, here in ((-1, me["wa"] > 0), (1, me["wa"] < nw - 1)):
        exists[(0, dw)] = here
        for dh in (-1, 1):
            exists[(dh, dw)] = jnp.logical_and(exists[(dh, 0)], here)

    def at(ha=None, wa=None, clip=None):
        return (
            me["ha"] if ha is None else ha,
            me["wa"] if wa is None else wa,
            me["clip"] if clip is None else clip,
        )

    def a_peer(k):
        return at(ha=lax.rem(my_a + k, na))

    def e_peer(k):
        p = lax.rem(my_e + k, ne)
        return at(wa=p // nc, clip=lax.rem(p, nc))

    world = na * ne
    one_shot = world <= 64 and world & (world - 1) == 0
    my_d = (me["clip"] * nw + me["wa"]) * na + my_a

    def d_peer(k):
        k = world - k
        p = 0
        bit = 1
        while bit < world:
            p = p + bit * lax.rem(lax.rem(my_d // bit, 2) + lax.rem(k // bit, 2), 2)
            bit *= 2
        return at(ha=lax.rem(p, na), wa=lax.rem(p // na, nw), clip=p // (na * nw))

    barrier = pltpu.get_barrier_semaphore()

    load = pltpu.make_async_copy(x_hbm, xc, load_sem.at[0])
    load.start()
    load2 = pltpu.make_async_copy(cot_hbm, u, load_sem.at[1])

    def greet_a(k, c):
        pl.semaphore_signal(barrier, inc=1, device_id=a_peer(k), device_id_type=MESH)
        return c

    def greet_e(k, c):
        pl.semaphore_signal(barrier, inc=1, device_id=e_peer(k), device_id_type=MESH)
        return c

    def greet_d(k, c):
        pl.semaphore_signal(barrier, inc=1, device_id=d_peer(k), device_id_type=MESH)
        return c

    if one_shot:
        lax.fori_loop(1, world, greet_d, 0)
        expected = world - 1
    else:
        lax.fori_loop(1, na, greet_a, 0)
        lax.fori_loop(1, ne, greet_e, 0)
        expected = na - 1 + ne - 1
        for dh in (-1, 1):
            for dw in (-1, 1):
                ok = exists[(dh, dw)]
                expected = expected + ok.astype(jnp.int32)

                @pl.when(ok)
                def _():
                    pl.semaphore_signal(
                        barrier, inc=1, device_id=at(ha=my_a + dh, wa=me["wa"] + dw), device_id_type=MESH
                    )

    def live_of(slot):
        return stride_ref[order_ref[slot]]

    base_slot = me["clip"] * clips

    def list_clip(slot, c):
        pace = live_of(base_slot + slot)
        ones = [jnp.where((t + 1) * pace <= frame_len, 1.0, 0.0) for t in range(frame_len)]
        ones.append(0.0)
        for t in range(frame_len):
            k = slot * frame_len + t
            flag_ref[0, k] = ones[t]
            flag_ref[1, k] = ones[t] if t > 0 else 0.0
            flag_ref[2, k + 1] = ones[t]
            vm8[pl.ds(pl.multiple_of(k * 8, 8), 8), :] = jnp.full((8, LANES), ones[t], F32)
            for i, flag in enumerate((ones[t] if t > 0 else 0.0, ones[t], ones[t + 1])):
                vflag[i, pl.ds(k, 1), :] = jnp.full((1, LANES), flag, F32)
        return c

    lax.fori_loop(0, clips, list_clip, 0)
    flag_ref[0, n] = 0.0
    flag_ref[1, n] = 0.0
    flag_ref[2, 0] = 0.0

    def group_frames(group):
        def add(slot, total):
            pace = live_of(group * clips + slot)
            one = jnp.where(pace == 1, frame_len, jnp.where(pace == 2, frame_len // 2, frame_len // 4))
            return total + one

        return lax.fori_loop(0, clips, add, jnp.int32(0))

    group_count = [(group_frames(g) * SPOT).astype(F32) for g in range(nc)]
    total_count = sum(group_count) * float(na * nw)
    my_frames = group_count[0]
    for g in range(1, nc):
        my_frames = jnp.where(me["clip"] == g, group_count[g], my_frames)
    widths = (narrow, wide)
    total_inv = {w: 1.0 / jnp.full((1, w), total_count, F32) for w in widths}
    my_count_inv = {w: 1.0 / jnp.full((1, w), my_frames, F32) for w in widths}
    group_inv = [{w: 1.0 / jnp.full((1, w), c, F32) for w in widths} for c in group_count]

    for l in range(layers):
        for lb in range(narrow // LANES):
            mown[l, lb, 0:SPOT] = jnp.zeros((SPOT, LANES), F32)
            mown[l, lb, SPOT + rows : SPOT + rows + SPOT] = jnp.zeros((SPOT, LANES), F32)
    mtop[...] = jnp.zeros_like(mtop)
    mbot[...] = jnp.zeros_like(mbot)
    mside[...] = jnp.zeros_like(mside)

    pl.semaphore_wait(barrier, expected)

    def set_taps():
        for l in range(layers):
            for i in range(27):
                tap = wdep_ref[i // 9, i // 3 % 3, i % 3].astype(F32)[l : l + 1]
                wtap[l, i] = jnp.broadcast_to(tap, (8, narrow))

    def turn_weights():
        for l in range(layers):
            wtr[l] = wred_ref[l].T
            wmt[l] = wmix_ref[l].T

    def finish(got, moments, slots, group_of, share):
        total = jnp.sum(got, axis=0)
        if not moments:
            return total[0:1], total[1:2]
        w = got.shape[-1]
        average = total[0:1] * total_inv[w]
        extra = [jnp.zeros((1, w), F32)] * 4
        for j in range(slots):
            g = group_of(j)
            off = got[j, 0:1] * (group_inv[g][w] * (1.0 / share)) - average
            extra[j % 4] = extra[j % 4] + off * off * (group_count[g] * float(share))
        second = total[1:2] + ((extra[0] + extra[1]) + (extra[2] + extra[3]))
        return average, lax.rsqrt(second * total_inv[w] + EPSILON)

    def pair_start(number, buf_a, buf_b, slot, value, moments):
        w = value.shape[-1]
        if na > 1:
            buf_a[slot, my_a] = value

            def send_a(k, c):
                pltpu.make_async_remote_copy(
                    src_ref=buf_a.at[slot, my_a], dst_ref=buf_a.at[slot, my_a],
                    send_sem=ar_send.at[number, 0], recv_sem=ar_recv.at[number, 0],
                    device_id=a_peer(k), device_id_type=MESH,
                ).start()
                return c

            lax.fori_loop(1, na, send_a, 0)
            part = buf_a.at[slot, pl.ds(0, na - 1)]
            pltpu.make_async_copy(part, part, ar_recv.at[number, 0]).wait()
            pltpu.make_async_copy(part, part, ar_send.at[number, 0]).wait()
            got = buf_a[slot]
            total = jnp.sum(got, axis=0)
            if moments:
                off = got[:, 0:1] - (total[0:1] * (1.0 / na))[None]
                extra = jnp.sum(off * off, axis=0) * my_count_inv[w]
                total = jnp.concatenate([total[0:1], total[1:2] + extra], axis=0)
            value = total
        buf_b[slot, my_e] = value

        def send_e(k, c):
            pltpu.make_async_remote_copy(
                src_ref=buf_b.at[slot, my_e], dst_ref=buf_b.at[slot, my_e],
                send_sem=ar_send.at[number, 1], recv_sem=ar_recv.at[number, 1],
                device_id=e_peer(k), device_id_type=MESH,
            ).start()
            return c

        lax.fori_loop(1, ne, send_e, 0)

    def bulk_wait(number, buf, slot, count):
        part = buf.at[slot, pl.ds(0, count)]
        pltpu.make_async_copy(part, part, ar_recv.at[number, 1]).wait()
        pltpu.make_async_copy(part, part, ar_send.at[number, 1]).wait()

    def reduce_start(number, buf_a, buf_b, slot, value, moments):
        if not (one_shot and value.shape[-1] == narrow):
            pair_start(number, buf_a, buf_b, slot, value, moments)
            return
        buf_b[slot, my_d] = value

        def send_d(k, c):
            pltpu.make_async_remote_copy(
                src_ref=buf_b.at[slot, my_d], dst_ref=buf_b.at[slot, my_d],
                send_sem=ar_send.at[number, 1], recv_sem=ar_recv.at[number, 1],
                device_id=d_peer(k), device_id_type=MESH,
            ).start()
            return c

        lax.fori_loop(1, world, send_d, 0)

    def reduce_finish(number, buf_b, slot, moments):
        if one_shot and buf_b.shape[-1] == narrow:
            bulk_wait(number, buf_b, slot, world - 1)
            return finish(buf_b[slot], moments, world, lambda j: j // (na * nw), 1)
        bulk_wait(number, buf_b, slot, ne - 1)
        return finish(buf_b[slot], moments, ne, lambda j: j % nc, na)

    def local_moments(first, square):
        total = jnp.sum(first, axis=0, keepdims=True)
        second = jnp.sum(square, axis=0, keepdims=True) - total * total * my_count_inv[total.shape[-1]]
        return jnp.concatenate([total, second], axis=0)

    def plain_pair(first, second):
        return jnp.concatenate(
            [jnp.sum(first, axis=0, keepdims=True), jnp.sum(second, axis=0, keepdims=True)], axis=0
        )

    def rim_list(r_send, c_send, top, bot, side):
        return [
            (1, 0, r_send.at[1], top), (-1, 0, r_send.at[0], bot),
            (0, 1, c_send.at[1], side.at[pl.ds(1, 2)]), (0, -1, c_send.at[0], side.at[pl.ds(5, 2)]),
            (1, 1, c_send.at[1, 1], side.at[0]), (-1, 1, c_send.at[1, 0], side.at[3]),
            (1, -1, c_send.at[0, 1], side.at[4]), (-1, -1, c_send.at[0, 0], side.at[7]),
        ]

    def rim_copy(number, k, item):
        dh, dw, src, dst = item
        return pltpu.make_async_remote_copy(
            src_ref=src, dst_ref=dst, send_sem=halo_send.at[number, k], recv_sem=halo_recv.at[number, k],
            device_id=at(ha=my_a + dh, wa=me["wa"] + dw), device_id_type=MESH,
        )

    def rim_start(number, items):
        for k, item in enumerate(items):
            @pl.when(exists[(item[0], item[1])])
            def _():
                rim_copy(number, k, item).start()

    def rim_sent(number, items):
        for k, item in enumerate(items):
            @pl.when(exists[(item[0], item[1])])
            def _():
                rim_copy(number, k, item).wait_send()

    def rim_arrived(number, items, which):
        for k in which:
            item = items[k]

            @pl.when(exists[(-item[0], -item[1])])
            def _():
                rim_copy(number, k, item).wait_recv()

    def fill_send(source, base):
        def rows_body(c, carry):
            tile = get(source, pl.ds(pl.multiple_of(base + c * CH * SPOT, SPOT), CH * SPOT))
            tile = tile.reshape(CH, ROWS, COLS, narrow)
            spot = pl.ds(pl.multiple_of(c * CH * COLS, CH * COLS), CH * COLS)
            for h in range(ROWS):
                row_send[h, spot, :] = tile[:, h].reshape(CH * COLS, narrow).astype(BF16)
            return carry

        lax.fori_loop(0, n // CH, rows_body, 0)
        for h in range(ROWS):
            for side, col in ((0, 0), (1, COLS - 1)):
                col_send[side, h] = get(source, pl.ds(base + h * COLS + col, n, stride=SPOT)).astype(BF16)

    def over_rim(apply):
        half = CH * COLS
        for key, which in ((-1, 0), (1, 1)):
            @pl.when(exists[(key, 0)])
            def _():
                dst = (mtop, mbot)[which]

                def body(c, carry):
                    spot = pl.ds(pl.multiple_of(c * half, half), half)
                    put(dst, spot, apply(
                        lambda: (top_in, bot_in)[which][spot, :].astype(F32),
                        lambda l: (top_sp, bot_sp)[which][l, spot, :].astype(F32),
                    ))
                    return carry

                lax.fori_loop(0, n // CH, body, 0)

    def over_sides(apply):
        for dw, base in ((-1, 0), (1, 4)):
            for r in range(4):
                dh = -1 if r == 0 else (1 if r == 3 else 0)

                @pl.when(exists[(dh, dw)])
                def _():
                    put(mside.at[base + r], pl.ds(8, n), apply(
                        lambda: side_in[base + r].astype(F32), lambda l: side_sp[l, base + r].astype(F32)
                    ))

    def side_sums(l, flip, target, base):
        stats = []
        for lb in range(narrow // LANES):
            lanes = pl.ds(lb * LANES, LANES)
            first = jnp.zeros((8, LANES), F32)
            square = jnp.zeros((8, LANES), F32)
            for side, e, col in ((0, 0, 0), (4, 2, COLS - 1)):
                for h in range(ROWS):
                    total = None
                    for a in range(3):
                        part = None
                        for b in range(3):
                            i = (a * 3 + b) * 3 + e
                            weight = wtap[l, 26 - i if flip else i, 0:1, lanes]
                            term = mside[side + h + b, lb, 7 + a : 7 + a + n, :] * weight
                            part = term if part is None else part + term
                        part = part * vflag[a] if a != 1 else part
                        total = part if total is None else total + part
                    total = total * vflag[1]
                    spot = pl.ds(base + 8 * h + col, n, stride=SPOT)
                    old = target[lb, spot, :]
                    new = old + total
                    target[lb, spot, :] = new
                    first = first + fold8(total)
                    square = square + fold8((new - old) * (new + old))
            stats.append((first, square))
        return stats

    row_id = lax.broadcasted_iota(jnp.int32, (8, LANES), 0)

    def shifted(own, own_base, f, lb):
        start = own_base + f * SPOT
        lines = [
            mtop[lb, pl.ds(pl.multiple_of(f * 8, 8), 8), :],
            own[lb, pl.ds(pl.multiple_of(start, 8), 8), :],
            own[lb, pl.ds(pl.multiple_of(start + 8, 8), 8), :],
            mbot[lb, pl.ds(pl.multiple_of(f * 8, 8), 8), :],
        ]
        out = []
        for v in lines:
            left = jnp.where(row_id == 0, 0.0, pltpu.roll(v, 1, 0))
            right = jnp.where(row_id == 7, 0.0, pltpu.roll(v, 7, 0))
            out.append((left, v, right))
        return out

    def tap_sum(grid, l, lanes, a, flip):
        res = []
        for h in range(ROWS):
            total = None
            for b in range(3):
                for e in range(3):
                    i = (a * 3 + b) * 3 + e
                    term = grid[h + b][e] * wtap[l, 26 - i if flip else i, :, lanes]
                    total = term if total is None else total + term
            res.append(total)
        return res

    def vmask(c):
        m = vm8[pl.ds(pl.multiple_of(c * CH * 8, CH * 8), CH * 8), :]
        m = jnp.broadcast_to(m.reshape(CH, 1, 8, LANES), (CH, ROWS, 8, LANES)).reshape(CH * SPOT, LANES)
        return jnp.concatenate([m] * (narrow // LANES), axis=1)

    def chunk(c):
        return pl.ds(pl.multiple_of(c * CH * SPOT, CH * SPOT), CH * SPOT)

    def chunk_off(c, base):
        return pl.ds(pl.multiple_of(base + c * CH * SPOT, SPOT), CH * SPOT)

    zero8 = jnp.zeros((8, narrow), F32)
    blocks = [pl.ds(k * narrow, narrow) for k in range(wide // narrow)]
    steps = n // CH
    scal = {}

    def reduce_phase(l):
        source = xc if l == 0 else x1

        def body(c, carry):
            first, square = carry
            r = dot(source[chunk(c), :], wred_ref[l])
            put(red.at[l], chunk(c), r)
            kept = r * vmask(c) if l == 0 else r
            return first + fold8(kept), square + fold8(kept * r)

        first, square = lax.fori_loop(0, steps, body, (zero8, zero8))
        reduce_start(3 * l, nar_a, nar_b, 2 * l, local_moments(first, square), True)
        fill_send(red.at[l], 0)
        rim_start(l, rims)
        if l == 0:
            set_taps()

    def mix_phase(l):
        average, inv = reduce_finish(3 * l, nar_b, 2 * l, True)
        scale = gn_ref[l, 0:1] * inv
        shift = sn_ref[l, 0:1] - average * scale
        scal["one", l] = (average, inv, scale, shift)

        def body(c, carry):
            z = get(red.at[l], chunk(c)) * scale + shift
            h = (z * sigmoid(z)).astype(BF16)
            put(mown.at[l], chunk_off(c, SPOT), dot(h, wmix_ref[l]))
            return carry

        lax.fori_loop(0, steps, body, 0)
        rim_arrived(l, rims, range(2))

        def apply(arrived, second):
            z = arrived() * scale + shift
            return dot((z * sigmoid(z)).astype(BF16), wmix_ref[l])

        over_rim(apply)
        return apply

    def spatial_phase(l, apply):
        stats = []
        for lb in range(narrow // LANES):
            lanes = pl.ds(lb * LANES, LANES)

            def body(f, carry):
                cur, nxt, first, square = carry
                grid = shifted(mown.at[l], SPOT, f, lb)
                here = flag_ref[1, f]
                t2 = tap_sum(grid, l, lanes, 2, False)
                t1 = tap_sum(grid, l, lanes, 1, False)
                t0 = tap_sum(grid, l, lanes, 0, False)
                alive = flag_ref[2, f]
                for h in range(ROWS):
                    done = (cur[h] + here * t2[h]) * alive
                    spat[l, lb, pl.ds(pl.multiple_of(f * SPOT + 8 * h, 8), 8), :] = done
                    first = first + done
                    square = square + done * done
                cur = tuple(t1[h] + here * nxt[h] for h in range(ROWS))
                return cur, tuple(t0), first, square

            z = jnp.zeros((8, LANES), F32)
            cur, nxt, first, square = lax.fori_loop(0, n, body, ((z, z), (z, z), z, z), unroll=UNROLL_F)
            for h in range(ROWS):
                done = cur[h] * flag_ref[2, n]
                spat[l, lb, rows + 8 * h : rows + 8 * h + 8, :] = done
                first = first + done
                square = square + done * done
            stats.append((first, square))
        rim_arrived(l, rims, range(2, 8))
        over_sides(apply)
        more = side_sums(l, False, spat.at[l], SPOT)
        rim_sent(l, rims)
        first = jnp.concatenate([s[0] + m[0] for s, m in zip(stats, more)], axis=1)
        square = jnp.concatenate([s[1] + m[1] for s, m in zip(stats, more)], axis=1)
        reduce_start(3 * l + 1, nar_a, nar_b, 2 * l + 1, local_moments(first, square), True)
        fill_send(spat.at[l], SPOT)
        rim_start(layers + l, rims_sp[l])
        if l == 0:
            turn_weights()

    def hidden_phase(l):
        average, inv = reduce_finish(3 * l + 1, nar_b, 2 * l + 1, True)
        scale = gn_ref[l, 1:2] * inv
        shift = sn_ref[l, 1:2] - average * scale
        scal["two", l] = (average, inv, scale, shift)

        def body(c, first):
            z = get(spat.at[l], chunk_off(c, SPOT)) * scale + shift
            h = z * sigmoid(z) * vmask(c)
            low = h.astype(BF16)
            h2[l, chunk(c), :] = low
            return first + fold8(low.astype(F32))

        first = lax.fori_loop(0, steps, body, zero8)
        g = dot_first(h2[l], h2[l])
        gram[l] = g
        t = split_dot(g, wexp_ref[l])
        square = jnp.sum(t * wexp_ref[l].astype(F32), axis=0, keepdims=True)
        hsum = jnp.sum(first, axis=0, keepdims=True)
        scal["hsum", l] = hsum
        both = split_dot(jnp.broadcast_to(hsum, (8, narrow)), wexp_ref[l])[0:1]
        second = square - both * both * my_count_inv[wide]
        reduce_start(3 * l + 2, wid_a, wid_b, l, jnp.concatenate([both, second], axis=0), True)
        rim_sent(layers + l, rims_sp[l])

    def widen_phase(l):
        average, inv = reduce_finish(3 * l + 2, wid_b, l, True)
        scale = gw_ref[l : l + 1] * inv
        shift = sw_ref[l : l + 1] - average * scale
        scal["wide", l] = (average, inv, scale, shift)
        source = xc if l == 0 else x1
        last = l == layers - 1

        def body(c, sums):
            out = []
            hid = h2[l, chunk(c), :]
            mask = vmask(c)
            for k, blk in enumerate(blocks):
                cut = slice(k * narrow, (k + 1) * narrow)
                w = dot(hid, wexp_ref[l, :, blk])
                summed = source[chunk(c), blk].astype(F32) + (w * scale[:, cut] + shift[:, cut])
                s = sigmoid(summed)
                y = summed * s
                if not last:
                    x1[chunk(c), blk] = (y * mask).astype(BF16)
                    s0[chunk(c), blk] = summed.astype(BF16)
                else:
                    xc[chunk(c), blk] = (y * mask).astype(BF16)
                    up = u[chunk(c), blk].astype(F32) * (s * (1.0 + summed * (1.0 - s))) * mask
                    low = up.astype(BF16)
                    u[chunk(c), blk] = low
                    out.append(sums[k] + fold8(low.astype(F32)))
            return tuple(out)

        return lax.fori_loop(0, steps, body, tuple(zero8 for _ in blocks) if last else ())

    def back_wide(l, sums):
        total = jnp.concatenate([jnp.sum(s, axis=0, keepdims=True) for s in sums], axis=1)
        second = []
        if BIG_DOT:
            hu[...] = dot_first(h2[l], u[...])
        for blk in blocks:
            if not BIG_DOT:
                hu[:, blk] = dot_first(h2[l], u[:, blk])
            second.append(jnp.sum(hu[:, blk] * wexp_ref[l, :, blk].astype(F32), axis=0, keepdims=True))
        second = jnp.concatenate(second, axis=1)
        reduce_start(
            3 * layers + 3 * l, wid_a, wid_b, layers + l, jnp.concatenate([total, second], axis=0), False
        )
        wtb[...] = (wexp_ref[l].astype(F32) * scal["wide", l][2]).T.astype(BF16)

        def body(c, carry):
            put(g2, chunk(c), dot(u[chunk(c), :], wtb[...]))
            return carry

        lax.fori_loop(0, steps, body, 0)

    def back_expand(l):
        gshift, gsec = reduce_finish(3 * layers + 3 * l, wid_b, layers + l, False)
        average, inv, scale, _ = scal["wide", l]
        ggain = inv * (gsec - average * gshift)
        small_w[l : l + 1] = ggain
        small_w[layers + l : layers + l + 1] = gshift
        drift = inv * ggain * total_inv[wide]
        mx = dot((wexp_ref[l].astype(F32) * drift).astype(BF16), wtb[...]).astype(BF16)
        base = gshift * total_inv[wide] - average * drift
        const = split_dot(jnp.broadcast_to(base, (8, wide)), wtb[...])[0:1]
        _, _, scale2, shift2 = scal["two", l]
        avg2, inv2, _, _ = scal["two", l]

        def body(c, carry):
            first, square = carry
            p = get(g2, chunk(c)) - dot(h2[l, chunk(c), :], mx) - const
            sp = get(spat.at[l], chunk_off(c, SPOT))
            g = p * slope_of(sp * scale2 + shift2) * vmask(c)
            put(g2, chunk(c), g)
            normed = (sp - avg2) * inv2
            return first + fold8(g), square + fold8(g * normed)

        first, square = lax.fori_loop(0, steps, body, (zero8, zero8))
        reduce_start(
            3 * layers + 3 * l + 1, nar_a, nar_b, 2 * layers + 2 * l, plain_pair(first, square), False
        )
        fill_send(g2, 0)
        rim_start(2 * layers + l, rims)
        hcol = jnp.broadcast_to(scal["hsum", l], (8, narrow)).T[:, 0:1]
        grad = scale * (
            hu[...] - hcol * (gshift * total_inv[wide] - average * drift) - split_dot(gram[l], wexp_ref[l]) * drift
        )
        buf, row = place[("expand", l)]
        for k in range(wide // LANES):
            buf[row + k * narrow : row + (k + 1) * narrow, :] = grad[:, k * LANES : (k + 1) * LANES].astype(BF16)

    def back_spatial(l):
        gshift, ggain = reduce_finish(3 * layers + 3 * l + 1, nar_b, 2 * layers + 2 * l, False)
        small_n[4 * l + 1 : 4 * l + 2] = ggain
        small_n[4 * l + 3 : 4 * l + 4] = gshift
        avg2, inv2, scale2, _ = scal["two", l]
        a_u = scale2
        a_s = scale2 * inv2 * ggain * total_inv[narrow]
        a_c = scale2 * gshift * total_inv[narrow] - a_s * avg2

        def body(c, carry):
            put(g2, chunk(c), a_u * get(g2, chunk(c)) - a_s * get(spat.at[l], chunk_off(c, SPOT)) - a_c)
            return carry

        lax.fori_loop(0, steps, body, 0)
        rim_arrived(2 * layers + l, rims, range(2))
        rim_arrived(layers + l, rims_sp[l], range(8))
        apply = lambda arrived, second: a_u * arrived() - a_s * second(l) - a_c
        over_rim(apply)
        tap_grads = []

        for lb in range(narrow // LANES):
            lanes = pl.ds(lb * LANES, LANES)
            if l == 0 and lb == 0:
                step_b(1)
            if l == 0 and lb == 1:
                step_a(4)
                step_b(2)

            def body(f, carry):
                cur, nxt, grads = carry
                grid = shifted(g2, 0, f, lb)
                here = flag_ref[1, f]
                after = flag_ref[1, f + 1]
                live = flag_ref[0, f]
                t2 = tap_sum(grid, l, lanes, 2, True)
                t1 = tap_sum(grid, l, lanes, 1, True)
                t0 = tap_sum(grid, l, lanes, 0, True)
                alive = flag_ref[2, f]
                done = [(cur[h] + here * t2[h]) * alive for h in range(ROWS)]
                spat[l, lb, pl.ds(pl.multiple_of(f * SPOT, SPOT), SPOT), :] = jnp.concatenate(done, axis=0)
                grads = list(grads)
                for a, flag in ((0, here), (1, live), (2, after)):
                    for h in range(ROWS):
                        m = flag * mown[l, lb, pl.ds(pl.multiple_of((f + a) * SPOT + 8 * h, 8), 8), :]
                        for b in range(3):
                            for e in range(3):
                                i = (a * 3 + b) * 3 + e
                                grads[i] = grads[i] + m * grid[h + 2 - b][2 - e]
                cur = tuple(t1[h] + here * nxt[h] for h in range(ROWS))
                return cur, tuple(t0), tuple(grads)

            z = jnp.zeros((8, LANES), F32)
            cur, nxt, grads = lax.fori_loop(0, n, body, ((z, z), (z, z), tuple(z for _ in range(27))), unroll=UNROLL_B)
            spat[l, lb, rows : rows + SPOT, :] = jnp.concatenate(
                [cur[h] * flag_ref[2, n] for h in range(ROWS)], axis=0
            )
            tap_grads.append(list(grads))

        rim_arrived(2 * layers + l, rims, range(2, 8))
        over_sides(apply)
        side_sums(l, True, spat.at[l], SPOT)
        rim_sent(2 * layers + l, rims)
        for lb in range(narrow // LANES):
            grads = tap_grads[lb]
            for side, e, col in ((0, 2, 0), (4, 0, COLS - 1)):
                for a in range(3):
                    for h in range(ROWS):
                        m = mown[l, lb, pl.ds(a * SPOT + 8 * h + col, n, stride=SPOT), :] * vflag[a]
                        for b in range(3):
                            i = (a * 3 + b) * 3 + e
                            grads[i] = grads[i] + fold8(m * mside[side + h + 2 - b, lb, 8 : 8 + n, :])
            folded = [jnp.sum(g, axis=0, keepdims=True) for g in grads]
            folded += [jnp.zeros((1, LANES), F32)] * 5
            buf, row = place[("depth", l)]
            buf[row + lb * 32 : row + lb * 32 + 32, :] = jnp.concatenate(folded, axis=0).astype(BF16)

        avg1, inv1, scale1, shift1 = scal["one", l]

        def body2(c, carry):
            first, square = carry
            low = get(spat.at[l], chunk_off(c, SPOT)).astype(BF16)
            gm[chunk(c), :] = low
            r = get(red.at[l], chunk(c))
            z = r * scale1 + shift1
            sig = sigmoid(z)
            h2[l, chunk(c), :] = (z * sig).astype(BF16)
            g = dot(low, wmt[l]) * (sig * (1.0 + z * (1.0 - sig)))
            put(g2, chunk(c), g)
            return first + fold8(g), square + fold8(g * ((r - avg1) * inv1))

        first, square = lax.fori_loop(0, steps, body2, (zero8, zero8))
        reduce_start(
            3 * layers + 3 * l + 2, nar_a, nar_b, 2 * layers + 2 * l + 1, plain_pair(first, square), False
        )
        buf, row = place[("mix", l)]
        grad = dot_first(h2[l], gm[...]).astype(BF16)
        for k in range(narrow // LANES):
            buf[row + k * narrow : row + (k + 1) * narrow, :] = grad[:, k * LANES : (k + 1) * LANES]

    def back_reduce(l):
        gshift, ggain = reduce_finish(3 * layers + 3 * l + 2, nar_b, 2 * layers + 2 * l + 1, False)
        small_n[4 * l : 4 * l + 1] = ggain
        small_n[4 * l + 2 : 4 * l + 3] = gshift
        avg1, inv1, scale1, _ = scal["one", l]
        a_u = scale1
        a_s = scale1 * inv1 * ggain * total_inv[narrow]
        a_c = scale1 * gshift * total_inv[narrow] - a_s * avg1

        def body(c, sums):
            gr = (a_u * get(g2, chunk(c)) - a_s * get(red.at[l], chunk(c)) - a_c) * vmask(c)
            gr = gr.astype(BF16)
            gm[chunk(c), :] = gr
            if l == 0:
                return ()
            out = []
            for k, blk in enumerate(blocks):
                g = u[chunk(c), blk].astype(F32) + dot(gr, wtr[l, :, blk])
                up = g * slope_of(s0[chunk(c), blk].astype(F32))
                low = up.astype(BF16)
                u[chunk(c), blk] = low
                out.append(sums[k] + fold8(low.astype(F32)))
            return tuple(out)

        sums = lax.fori_loop(0, steps, body, tuple(zero8 for _ in blocks) if l > 0 else ())
        return sums

    def input_grads(c):
        for blk in blocks:
            g = u[chunk(c), blk].astype(F32) + dot(gm[chunk(c), :], wtr[0, :, blk])
            u[chunk(c), blk] = g.astype(BF16)
        pltpu.make_async_copy(u.at[chunk(c)], gx_ref.at[chunk(c)], load_sem.at[3]).start()

    def back_reduce_weight(l):
        source = xc if l == 0 else x1
        buf, row = place[("reduce", l)]
        if BIG_DOT:
            whole = dot_first(gm[...], source[...])
        for k, blk in enumerate(blocks):
            if BIG_DOT:
                grad = whole[:, k * narrow : (k + 1) * narrow].T.astype(BF16)
            else:
                grad = dot_first(gm[...], source[:, blk]).T.astype(BF16)
            for lb in range(narrow // LANES):
                first = row + lb * wide + k * narrow
                buf[first : first + narrow, :] = grad[:, lb * LANES : (lb + 1) * LANES]

    groups = {
        "ha": (na, my_a, a_peer),
        "wa": (nw, me["wa"], lambda k: at(wa=lax.rem(me["wa"] + k, nw))),
        "clip": (nc, me["clip"], lambda k: at(clip=lax.rem(me["clip"] + k, nc))),
        "all": (ne, my_e, e_peer),
    }

    def bytes_wait(ref, count, sem):
        part = ref.at[pl.ds(0, count)]
        pltpu.make_async_copy(part, part, sem).wait()

    def pack_step(number, stages, padded, bufs, out_hbm):
        wb, recvs, gats = bufs
        sizes_of = []
        left = padded
        for st in stages:
            sizes_of.append((left, left // groups[st][0]))
            left //= groups[st][0]
        last = len(stages) - 1

        def send_seg(i):
            size, mine, peer = groups[stages[i]]
            seg = sizes_of[i][1]
            src = wb if i == 0 else gats[i - 1].at[groups[stages[i - 1]][1]]

            def send(k, c):
                target = lax.rem(mine + k, size)
                pltpu.make_async_remote_copy(
                    src_ref=src.at[pl.ds(pl.multiple_of(target * seg, 16), seg)], dst_ref=recvs[i].at[mine],
                    send_sem=wg_send.at[number, i], recv_sem=wg_recv.at[number, i],
                    device_id=peer(k), device_id_type=MESH,
                ).start()
                return c

            lax.fori_loop(1, size, send, 0)
            recvs[i][mine] = src[pl.ds(pl.multiple_of(mine * seg, 16), seg), :]

        def add_up(i):
            size, mine, _ = groups[stages[i]]
            seg = sizes_of[i][1]
            if size > 1:
                bytes_wait(recvs[i], size - 1, wg_recv.at[number, i])
                bytes_wait(recvs[i], size - 1, wg_send.at[number, i])

            def add(c, carry):
                spot = pl.ds(pl.multiple_of(c * 16, 16), 16)
                total = recvs[i][0, spot, :].astype(F32)
                for j in range(1, size):
                    total = total + recvs[i][j, spot, :].astype(F32)
                gats[i][mine, spot, :] = total.astype(BF16)
                return carry

            lax.fori_loop(0, seg // 16, add, 0)

        def send_back(i):
            size, mine, peer = groups[stages[i]]
            k_sem = 2 * len(stages) - 1 - i

            def send(k, c):
                pltpu.make_async_remote_copy(
                    src_ref=gats[i].at[mine], dst_ref=gats[i].at[mine],
                    send_sem=wg_send.at[number, k_sem], recv_sem=wg_recv.at[number, k_sem],
                    device_id=peer(k), device_id_type=MESH,
                ).start()
                return c

            lax.fori_loop(1, size, send, 0)

        def got_back(i):
            size = groups[stages[i]][0]
            k_sem = 2 * len(stages) - 1 - i
            if size > 1:
                bytes_wait(gats[i], size - 1, wg_recv.at[number, k_sem])
                bytes_wait(gats[i], size - 1, wg_send.at[number, k_sem])

        def down(i):
            mine = groups[stages[i]][1]
            seg = sizes_of[i + 1][1]

            def keep(j, c):
                gats[i][mine, pl.ds(pl.multiple_of(j * seg, 16), seg), :] = gats[i + 1][j]
                return c

            lax.fori_loop(0, groups[stages[i + 1]][0], keep, 0)

        def step(k):
            if k <= last:
                if k > 0:
                    add_up(k - 1)
                send_seg(k)
            elif k == last + 1:
                add_up(last)
                send_back(last)
            elif k <= 2 * last + 1:
                i = 2 * last + 1 - k
                got_back(i + 1)
                down(i)
                send_back(i)
            else:
                got_back(0)
                copy = pltpu.make_async_copy(gats[0], out_hbm, load_sem.at[4 + number])
                copy.start()

        def stored():
            pltpu.make_async_copy(gats[0], out_hbm, load_sem.at[4 + number]).wait()

        return step, stored

    rims = rim_list(row_send, col_send, top_in, bot_in, side_in)
    rims_sp = [rim_list(row_send, col_send, top_sp.at[l], bot_sp.at[l], side_sp.at[l]) for l in range(layers)]

    place = {}
    packs = []
    first_bufs = []
    at_ref = 0
    for number, (parts, stages, padded, used) in enumerate(plan):
        m = len(stages)
        bufs = (pack_refs[at_ref] if number < 2 else first_bufs[number - 2], pack_refs[at_ref + 1 : at_ref + 1 + m], pack_refs[at_ref + 1 + m : at_ref + 1 + 2 * m])
        first_bufs.append(pack_refs[at_ref])
        at_ref += 1 + 2 * m
        for key, row, _ in parts:
            place[key] = (bufs[0], row)
        if padded > used and number < 2:
            bufs[0][used:padded, :] = jnp.zeros((padded - used, LANES), BF16)
        packs.append(pack_step(number, stages, padded, bufs, (packed_a, packed_b, packed_c, packed_d)[number]))
    (step_a, stored_a), (step_b, stored_b), (step_c, stored_c), (step_d, stored_d) = packs

    load.wait()
    load2.start()
    for l in range(layers):
        reduce_phase(l)
        spatial_phase(l, mix_phase(l))
        hidden_phase(l)
        if l == layers - 1:
            load2.wait()
        sums = widen_phase(l)
    store_y = pltpu.make_async_copy(xc, y_ref, load_sem.at[2])
    store_y.start()
    load_again = pltpu.make_async_copy(x_hbm, xc, load_sem.at[0])
    for l in reversed(range(layers)):
        back_wide(l, sums)
        if l == 0:
            store_y.wait()
            load_again.start()
            back_reduce_weight(1)
            step_a(2)
        back_expand(l)
        if l == 0:
            step_a(3)
            step_b(0)
        back_spatial(l)
        if l == 0:
            step_a(5)
            step_b(3)
            step_d(0)
        else:
            step_a(0)
        sums = back_reduce(l)
        if l == 0:
            step_a(6)
            step_b(4)
        else:
            step_a(1)
    load_again.wait()
    back_reduce_weight(0)
    step_c(0)
    step_d(1)
    input_grads(0)
    step_c(1)
    step_b(5)
    input_grads(1)
    step_d(2)
    step_b(6)
    step_d(3)
    step_c(2)
    step_d(4)
    step_c(3)
    step_c(4)
    pltpu.make_async_copy(u, gx_ref, load_sem.at[3]).wait()
    stored_a()
    stored_b()
    stored_c()
    stored_d()


def pack_plan(sizes, wide, narrow):
    world = sizes[0] * sizes[1] * sizes[2]
    plan = []
    for names, stages in (
        ((("expand", 1), ("mix", 1), ("depth", 1)), ("ha", "wa", "clip")),
        ((("reduce", 1), ("expand", 0)), ("ha", "wa", "clip")),
        ((("reduce", 0),), ("ha", "all")),
        ((("mix", 0), ("depth", 0)), ("ha", "all")),
    ):
        nb = narrow // LANES
        rows = {"reduce": nb * wide, "expand": nb * wide, "mix": nb * narrow, "depth": nb * 32}
        used = 0
        parts = []
        for key in names:
            parts.append((key, used, rows[key[0]]))
            used += rows[key[0]]
        padded = -(-used // (16 * world)) * 16 * world
        plan.append((parts, stages, padded, used))
    return plan


def mega_call(sizes, clips, x, cot, stride, order, w_reduce, w_mix, w_depth, w_expand, gn, sn, gw, sw):
    na, nw, nc = sizes
    ne = nw * nc
    layers, wide, narrow = w_reduce.shape
    n = x.shape[0] // SPOT
    rows = n * SPOT
    plan = pack_plan(sizes, wide, narrow)
    group_size = {"ha": na, "wa": nw, "clip": nc, "all": ne}
    vmem = lambda shape, kind: pltpu.VMEM(shape, kind)
    half = n * COLS
    kernel = functools.partial(mega, sizes, clips, n // clips, layers, wide, narrow, plan)
    spec = pl.BlockSpec(memory_space=pltpu.VMEM)
    smem = pl.BlockSpec(memory_space=pltpu.SMEM)
    hbm = pl.BlockSpec(memory_space=pl.ANY)
    n_sync = 6 * layers
    nb = narrow // LANES
    world = na * ne
    slots = world if world <= 64 and world & (world - 1) == 0 else ne
    scratch = [
        pltpu.SMEM((3, n + 1), F32),
        vmem((rows, wide), BF16), vmem((rows, wide), BF16), vmem((rows, wide), BF16), vmem((rows, wide), BF16),
        vmem((layers, nb, rows, LANES), F32),
        vmem((layers, nb, rows + 2 * SPOT, LANES), F32), vmem((layers, nb, rows + SPOT, LANES), F32),
        vmem((layers, rows, narrow), BF16), vmem((nb, rows, LANES), F32), vmem((rows, narrow), BF16),
        vmem((nb, half, LANES), F32), vmem((nb, half, LANES), F32), vmem((8, nb, n + 16, LANES), F32),
        vmem((half, LANES), F32), vmem((3, n, LANES), F32), vmem((layers, 27, 8, narrow), F32), vmem((narrow, wide), F32),
        vmem((layers, narrow, narrow), F32),
        vmem((layers, narrow, wide), BF16), vmem((wide, narrow), BF16), vmem((layers, narrow, narrow), BF16),
        vmem((2, half, narrow), BF16), vmem((2, 2, n, narrow), BF16),
        vmem((half, narrow), BF16), vmem((half, narrow), BF16), vmem((8, n, narrow), BF16),
        vmem((layers, half, narrow), BF16), vmem((layers, half, narrow), BF16), vmem((layers, 8, n, narrow), BF16),
        vmem((4 * layers, na, 2, narrow), F32), vmem((4 * layers, slots, 2, narrow), F32),
        vmem((2 * layers, na, 2, wide), F32), vmem((2 * layers, ne, 2, wide), F32),
        pltpu.SemaphoreType.DMA((4 + len(plan),)), pltpu.SemaphoreType.DMA((n_sync, 2)), pltpu.SemaphoreType.DMA((n_sync, 2)),
        pltpu.SemaphoreType.DMA((3 * layers, 8)), pltpu.SemaphoreType.DMA((3 * layers, 8)),
        pltpu.SemaphoreType.DMA((len(plan), 6)), pltpu.SemaphoreType.DMA((len(plan), 6)),
    ]
    outs_packed = []
    for number, (_, stages, padded, _) in enumerate(plan):
        scratch.append(vmem((padded if number < 2 else 16, LANES), BF16))
        recvs, gats, left = [], [], padded
        for st in stages:
            left //= group_size[st]
            recvs.append(vmem((group_size[st], left, LANES), BF16))
            gats.append(vmem((group_size[st], left, LANES), BF16))
        scratch += recvs + gats
        outs_packed.append(jax.ShapeDtypeStruct(gats[0].shape, BF16))
    shape = jax.ShapeDtypeStruct
    outs = (
        shape((rows, wide), BF16), shape((rows, wide), BF16),
        *outs_packed,
        shape((4 * layers, narrow), F32), shape((2 * layers, wide), F32),
    )
    return pl.pallas_call(
        kernel,
        out_shape=outs,
        in_specs=[smem, smem, hbm, hbm] + [spec] * 8,
        out_specs=(hbm,) * 6 + (spec,) * 2,
        scratch_shapes=scratch,
        compiler_params=pltpu.CompilerParams(
            collective_id=0, has_side_effects=True, vmem_limit_bytes=63 * 1024 * 1024
        ),
    )(stride, order, x, cot, w_reduce, w_mix, w_depth, w_expand, gn, sn, gw, sw)


def finish_kernel(plan, layers, wide, narrow, steps, *refs):
    if not ROOT_COPY:
        y_ref, g_ref, *refs = refs
        oy, og = refs[6:8]
        refs = refs[:6] + refs[8:]
        oy[...] = y_ref[...]
        og[...] = g_ref[...]
    pa, pb, pc, pd, sn, sw, owr, owm, owd, owe, ogn, osn, ogw, osw = refs
    i = pl.program_id(0)
    packed = (pa, pb, pc, pd)
    rows_r, rows_m = wide // steps, narrow // steps
    for number, (parts, _, _, _) in enumerate(plan):
        for (kind, l), row, _ in parts:
            ref = packed[number]
            if kind == "expand":
                for k in range(wide // LANES):
                    spot = pl.ds(pl.multiple_of(row + k * narrow + i * rows_m, 16), rows_m)
                    owe[l, :, k * LANES : (k + 1) * LANES] = ref[spot, :].astype(F32)
            elif kind != "depth":
                dst, size, part = (owr, wide, rows_r) if kind == "reduce" else (owm, narrow, rows_m)
                for lb in range(narrow // LANES):
                    spot = pl.ds(pl.multiple_of(row + lb * size + i * part, 16), part)
                    dst[l, :, lb * LANES : (lb + 1) * LANES] = ref[spot, :].astype(F32)
            else:
                @pl.when(i == 0)
                def _():
                    taps = jnp.concatenate([ref[row + lb * 32 : row + lb * 32 + 32, :] for lb in range(narrow // LANES)], axis=1).astype(F32)
                    for t in range(27):
                        owd[t // 9, t // 3 % 3, t % 3, l : l + 1, :] = taps[t : t + 1]

    @pl.when(i == 0)
    def _():
        for l in range(layers):
            ogn[l] = sn[4 * l : 4 * l + 2]
            osn[l] = sn[4 * l + 2 : 4 * l + 4]
        ogw[...] = sw[0:layers]
        osw[...] = sw[layers : 2 * layers]


def finish_call(plan, layers, wide, narrow, y, g, packed, small):
    steps = FINISH_STEPS
    per = y.shape[0] // steps
    packed = [p.reshape(-1, LANES) for p in packed]
    whole = lambda a: pl.BlockSpec(a.shape, lambda i: (0,) * len(a.shape), pipeline_mode=pl.Buffered(1))
    keep = lambda shape: pl.BlockSpec(shape, lambda i: (0,) * len(shape))
    big = pl.BlockSpec((per, wide), lambda i: (i, 0))
    shape = jax.ShapeDtypeStruct
    bigs = [] if ROOT_COPY else [big, big]
    tiny = ((layers, 2, narrow), (layers, 2, narrow), (layers, wide), (layers, wide))
    outs = (() if ROOT_COPY else (shape(y.shape, BF16), shape(y.shape, BF16))) + (
        shape((layers, wide, narrow), F32), shape((layers, narrow, narrow), F32),
        shape((3, 3, 3, layers, narrow), F32), shape((layers, narrow, wide), F32),
    ) + tuple(shape(a, F32) for a in tiny)
    return pl.pallas_call(
        functools.partial(finish_kernel, plan, layers, wide, narrow, steps),
        out_shape=outs,
        grid=(steps,),
        in_specs=bigs + [whole(p) for p in packed] + [whole(a) for a in small],
        out_specs=tuple(bigs) + (
            pl.BlockSpec((layers, wide // steps, narrow), lambda i: (0, i, 0)),
            pl.BlockSpec((layers, narrow // steps, narrow), lambda i: (0, i, 0)),
            keep((3, 3, 3, layers, narrow)),
            pl.BlockSpec((layers, narrow // steps, wide), lambda i: (0, i, 0)),
        ) + tuple(keep(a) for a in tiny),
        compiler_params=pltpu.CompilerParams(vmem_limit_bytes=62 * 1024 * 1024),
    )(*(() if ROOT_COPY else (y, g)), *packed, *small)


def body(
    sizes, activations, stride, clip_order, cotangent, w_reduce, w_mix, w_depth, w_expand,
    gains_narrow, shifts_narrow, gains_wide, shifts_wide,
):
    clips, frame_len, _, _, wide = activations.shape
    layers, _, narrow = w_reduce.shape
    flat = (clips * frame_len * SPOT, wide)
    res = mega_call(
        sizes, clips, activations.reshape(flat), cotangent.reshape(flat),
        stride, clip_order, w_reduce, w_mix, jnp.transpose(w_depth, (1, 2, 3, 0, 4)), w_expand,
        gains_narrow, shifts_narrow, gains_wide, shifts_wide,
    )
    out = finish_call(pack_plan(sizes, wide, narrow), layers, wide, narrow, res[0], res[1], res[2:6], res[6:])
    if ROOT_COPY:
        out = (res[0], res[1]) + tuple(out)
    return (
        out[0].reshape(activations.shape), out[1].reshape(activations.shape), out[2], out[3],
        jnp.transpose(out[4], (3, 0, 1, 2, 4)),
    ) + tuple(out[5:])


def solution(mesh):
    sizes = tuple(mesh.shape[a] for a in AXES)
    big = P("clip", None, "ha", "wa", None)
    return jax.shard_map(
        functools.partial(body, sizes),
        mesh=mesh,
        in_specs=(big, P(), P(), big) + (P(),) * 8,
        out_specs=(big, big) + (P(),) * 8,
        check_vma=False,
    )
```

```python
import functools
import math

import jax
import jax.numpy as jnp
from jax import lax
from jax.experimental import pallas as pl
from jax.experimental.pallas import tpu as pltpu
from jax.sharding import PartitionSpec as P

EPSILON = 1e-05
AXES = ("ha", "wa", "clip")
MESH = pl.DeviceIdType.MESH
F32 = jnp.float32
BF16 = jnp.bfloat16
ROWS = 2
COLS = 8
SPOT = ROWS * COLS
LANES = 128
UNROLL_F = 2
UNROLL_B = 4
FINISH_STEPS = 2
ROOT_COPY = False
BIG_DOT = True


def dot(a, b):
    return jnp.dot(a, b, preferred_element_type=F32)


def dot_first(a, b):
    return lax.dot_general(a, b, (((0,), (0,)), ((), ())), preferred_element_type=F32)


def sigmoid(v):
    return jax.nn.sigmoid(v)


def slope_of(z):
    s = sigmoid(z)
    return s * (1.0 + z * (1.0 - s))


def get(ref, spot):
    return jnp.concatenate([ref[lb, spot, :] for lb in range(ref.shape[0])], axis=-1)


def put(ref, spot, value):
    for lb in range(ref.shape[0]):
        ref[lb, spot, :] = value[:, lb * LANES : (lb + 1) * LANES]


def fold8(v):
    return jnp.sum(v.reshape(v.shape[0] // 8, 8, v.shape[1]), axis=0)


def split_dot(v, w):
    high = v.astype(BF16)
    low = (v - high.astype(F32)).astype(BF16)
    return dot(high, w) + dot(low, w)


def mega(sizes, clips, frame_len, layers, wide, narrow, plan, *refs):
    (
        stride_ref, order_ref, x_hbm, cot_hbm, wred_ref, wmix_ref, wdep_ref, wexp_ref,
        gn_ref, sn_ref, gw_ref, sw_ref,
        y_ref, gx_ref, packed_a, packed_b, packed_c, packed_d, small_n, small_w,
        flag_ref, xc, u, x1, s0, red, mown, spat, h2, g2, gm, mtop, mbot, mside,
        vm8, vflag, wtap, hu, gram, wtr, wtb, wmt,
        row_send, col_send, top_in, bot_in, side_in, top_sp, bot_sp, side_sp,
        nar_a, nar_b, wid_a, wid_b,
        load_sem, ar_send, ar_recv, halo_send, halo_recv, wg_send, wg_recv, *pack_refs
    ) = refs
    n = clips * frame_len
    CH = n // 2
    rows = n * SPOT
    na, nw, nc = sizes
    ne = nw * nc
    me = {a: lax.axis_index(a) for a in AXES}
    my_a = me["ha"]
    my_e = me["wa"] * nc + me["clip"]
    exists = {
        (-1, 0): my_a > 0, (1, 0): my_a < na - 1,
    }
    for dw, here in ((-1, me["wa"] > 0), (1, me["wa"] < nw - 1)):
        exists[(0, dw)] = here
        for dh in (-1, 1):
            exists[(dh, dw)] = jnp.logical_and(exists[(dh, 0)], here)

    def at(ha=None, wa=None, clip=None):
        return (
            me["ha"] if ha is None else ha,
            me["wa"] if wa is None else wa,
            me["clip"] if clip is None else clip,
        )

    def a_peer(k):
        return at(ha=lax.rem(my_a + k, na))

    def e_peer(k):
        p = lax.rem(my_e + k, ne)
        return at(wa=p // nc, clip=lax.rem(p, nc))

    world = na * ne
    one_shot = world <= 64 and world & (world - 1) == 0
    my_d = (me["clip"] * nw + me["wa"]) * na + my_a

    def d_peer(k):
        k = world - k
        p = 0
        bit = 1
        while bit < world:
            p = p + bit * lax.rem(lax.rem(my_d // bit, 2) + lax.rem(k // bit, 2), 2)
            bit *= 2
        return at(ha=lax.rem(p, na), wa=lax.rem(p // na, nw), clip=p // (na * nw))

    barrier = pltpu.get_barrier_semaphore()

    load = pltpu.make_async_copy(x_hbm, xc, load_sem.at[0])
    load.start()
    load2 = pltpu.make_async_copy(cot_hbm, u, load_sem.at[1])

    def greet_a(k, c):
        pl.semaphore_signal(barrier, inc=1, device_id=a_peer(k), device_id_type=MESH)
        return c

    def greet_e(k, c):
        pl.semaphore_signal(barrier, inc=1, device_id=e_peer(k), device_id_type=MESH)
        return c

    def greet_d(k, c):
        pl.semaphore_signal(barrier, inc=1, device_id=d_peer(k), device_id_type=MESH)
        return c

    if one_shot:
        lax.fori_loop(1, world, greet_d, 0)
        expected = world - 1
    else:
        lax.fori_loop(1, na, greet_a, 0)
        lax.fori_loop(1, ne, greet_e, 0)
        expected = na - 1 + ne - 1
        for dh in (-1, 1):
            for dw in (-1, 1):
                ok = exists[(dh, dw)]
                expected = expected + ok.astype(jnp.int32)

                @pl.when(ok)
                def _():
                    pl.semaphore_signal(
                        barrier, inc=1, device_id=at(ha=my_a + dh, wa=me["wa"] + dw), device_id_type=MESH
                    )

    def live_of(slot):
        return stride_ref[order_ref[slot]]

    base_slot = me["clip"] * clips

    def list_clip(slot, c):
        pace = live_of(base_slot + slot)
        ones = [jnp.where((t + 1) * pace <= frame_len, 1.0, 0.0) for t in range(frame_len)]
        ones.append(0.0)
        for t in range(frame_len):
            k = slot * frame_len + t
            flag_ref[0, k] = ones[t]
            flag_ref[1, k] = ones[t] if t > 0 else 0.0
            flag_ref[2, k + 1] = ones[t]
            vm8[pl.ds(pl.multiple_of(k * 8, 8), 8), :] = jnp.full((8, LANES), ones[t], F32)
            for i, flag in enumerate((ones[t] if t > 0 else 0.0, ones[t], ones[t + 1])):
                vflag[i, pl.ds(k, 1), :] = jnp.full((1, LANES), flag, F32)
        return c

    lax.fori_loop(0, clips, list_clip, 0)
    flag_ref[0, n] = 0.0
    flag_ref[1, n] = 0.0
    flag_ref[2, 0] = 0.0

    def group_frames(group):
        def add(slot, total):
            pace = live_of(group * clips + slot)
            one = jnp.where(pace == 1, frame_len, jnp.where(pace == 2, frame_len // 2, frame_len // 4))
            return total + one

        return lax.fori_loop(0, clips, add, jnp.int32(0))

    group_count = [(group_frames(g) * SPOT).astype(F32) for g in range(nc)]
    total_count = sum(group_count) * float(na * nw)
    my_frames = group_count[0]
    for g in range(1, nc):
        my_frames = jnp.where(me["clip"] == g, group_count[g], my_frames)
    widths = (narrow, wide)
    total_inv = {w: 1.0 / jnp.full((1, w), total_count, F32) for w in widths}
    my_count_inv = {w: 1.0 / jnp.full((1, w), my_frames, F32) for w in widths}
    group_inv = [{w: 1.0 / jnp.full((1, w), c, F32) for w in widths} for c in group_count]

    for l in range(layers):
        for lb in range(narrow // LANES):
            mown[l, lb, 0:SPOT] = jnp.zeros((SPOT, LANES), F32)
            mown[l, lb, SPOT + rows : SPOT + rows + SPOT] = jnp.zeros((SPOT, LANES), F32)
    mtop[...] = jnp.zeros_like(mtop)
    mbot[...] = jnp.zeros_like(mbot)
    mside[...] = jnp.zeros_like(mside)

    pl.semaphore_wait(barrier, expected)

    def set_taps():
        for l in range(layers):
            for i in range(27):
                tap = wdep_ref[i // 9, i // 3 % 3, i % 3].astype(F32)[l : l + 1]
                wtap[l, i] = jnp.broadcast_to(tap, (8, narrow))

    def turn_weights():
        for l in range(layers):
            wtr[l] = wred_ref[l].T
            wmt[l] = wmix_ref[l].T

    def finish(got, moments, slots, group_of, share):
        total = jnp.sum(got, axis=0)
        if not moments:
            return total[0:1], total[1:2]
        w = got.shape[-1]
        average = total[0:1] * total_inv[w]
        extra = [jnp.zeros((1, w), F32)] * 4
        for j in range(slots):
            g = group_of(j)
            off = got[j, 0:1] * (group_inv[g][w] * (1.0 / share)) - average
            extra[j % 4] = extra[j % 4] + off * off * (group_count[g] * float(share))
        second = total[1:2] + ((extra[0] + extra[1]) + (extra[2] + extra[3]))
        return average, lax.rsqrt(second * total_inv[w] + EPSILON)

    def pair_start(number, buf_a, buf_b, slot, value, moments):
        w = value.shape[-1]
        if na > 1:
            buf_a[slot, my_a] = value

            def send_a(k, c):
                pltpu.make_async_remote_copy(
                    src_ref=buf_a.at[slot, my_a], dst_ref=buf_a.at[slot, my_a],
                    send_sem=ar_send.at[number, 0], recv_sem=ar_recv.at[number, 0],
                    device_id=a_peer(k), device_id_type=MESH,
                ).start()
                return c

            lax.fori_loop(1, na, send_a, 0)
            part = buf_a.at[slot, pl.ds(0, na - 1)]
            pltpu.make_async_copy(part, part, ar_recv.at[number, 0]).wait()
            pltpu.make_async_copy(part, part, ar_send.at[number, 0]).wait()
            got = buf_a[slot]
            total = jnp.sum(got, axis=0)
            if moments:
                off = got[:, 0:1] - (total[0:1] * (1.0 / na))[None]
                extra = jnp.sum(off * off, axis=0) * my_count_inv[w]
                total = jnp.concatenate([total[0:1], total[1:2] + extra], axis=0)
            value = total
        buf_b[slot, my_e] = value

        def send_e(k, c):
            pltpu.make_async_remote_copy(
                src_ref=buf_b.at[slot, my_e], dst_ref=buf_b.at[slot, my_e],
                send_sem=ar_send.at[number, 1], recv_sem=ar_recv.at[number, 1],
                device_id=e_peer(k), device_id_type=MESH,
            ).start()
            return c

        lax.fori_loop(1, ne, send_e, 0)

    def bulk_wait(number, buf, slot, count):
        part = buf.at[slot, pl.ds(0, count)]
        pltpu.make_async_copy(part, part, ar_recv.at[number, 1]).wait()
        pltpu.make_async_copy(part, part, ar_send.at[number, 1]).wait()

    def reduce_start(number, buf_a, buf_b, slot, value, moments):
        if not (one_shot and value.shape[-1] == narrow):
            pair_start(number, buf_a, buf_b, slot, value, moments)
            return
        buf_b[slot, my_d] = value

        def send_d(k, c):
            pltpu.make_async_remote_copy(
                src_ref=buf_b.at[slot, my_d], dst_ref=buf_b.at[slot, my_d],
                send_sem=ar_send.at[number, 1], recv_sem=ar_recv.at[number, 1],
                device_id=d_peer(k), device_id_type=MESH,
            ).start()
            return c

        lax.fori_loop(1, world, send_d, 0)

    def reduce_finish(number, buf_b, slot, moments):
        if one_shot and buf_b.shape[-1] == narrow:
            bulk_wait(number, buf_b, slot, world - 1)
            return finish(buf_b[slot], moments, world, lambda j: j // (na * nw), 1)
        bulk_wait(number, buf_b, slot, ne - 1)
        return finish(buf_b[slot], moments, ne, lambda j: j % nc, na)

    def local_moments(first, square):
        total = jnp.sum(first, axis=0, keepdims=True)
        second = jnp.sum(square, axis=0, keepdims=True) - total * total * my_count_inv[total.shape[-1]]
        return jnp.concatenate([total, second], axis=0)

    def plain_pair(first, second):
        return jnp.concatenate(
            [jnp.sum(first, axis=0, keepdims=True), jnp.sum(second, axis=0, keepdims=True)], axis=0
        )

    def rim_list(r_send, c_send, top, bot, side):
        return [
            (1, 0, r_send.at[1], top), (-1, 0, r_send.at[0], bot),
            (0, 1, c_send.at[1], side.at[pl.ds(1, 2)]), (0, -1, c_send.at[0], side.at[pl.ds(5, 2)]),
            (1, 1, c_send.at[1, 1], side.at[0]), (-1, 1, c_send.at[1, 0], side.at[3]),
            (1, -1, c_send.at[0, 1], side.at[4]), (-1, -1, c_send.at[0, 0], side.at[7]),
        ]

    def rim_copy(number, k, item):
        dh, dw, src, dst = item
        return pltpu.make_async_remote_copy(
            src_ref=src, dst_ref=dst, send_sem=halo_send.at[number, k], recv_sem=halo_recv.at[number, k],
            device_id=at(ha=my_a + dh, wa=me["wa"] + dw), device_id_type=MESH,
        )

    def rim_start(number, items):
        for k, item in enumerate(items):
            @pl.when(exists[(item[0], item[1])])
            def _():
                rim_copy(number, k, item).start()

    def rim_sent(number, items):
        for k, item in enumerate(items):
            @pl.when(exists[(item[0], item[1])])
            def _():
                rim_copy(number, k, item).wait_send()

    def rim_arrived(number, items, which):
        for k in which:
            item = items[k]

            @pl.when(exists[(-item[0], -item[1])])
            def _():
                rim_copy(number, k, item).wait_recv()

    def fill_send(source, base):
        def rows_body(c, carry):
            tile = get(source, pl.ds(pl.multiple_of(base + c * CH * SPOT, SPOT), CH * SPOT))
            tile = tile.reshape(CH, ROWS, COLS, narrow)
            spot = pl.ds(pl.multiple_of(c * CH * COLS, CH * COLS), CH * COLS)
            for h in range(ROWS):
                row_send[h, spot, :] = tile[:, h].reshape(CH * COLS, narrow).astype(BF16)
            return carry

        lax.fori_loop(0, n // CH, rows_body, 0)
        for h in range(ROWS):
            for side, col in ((0, 0), (1, COLS - 1)):
                col_send[side, h] = get(source, pl.ds(base + h * COLS + col, n, stride=SPOT)).astype(BF16)

    def over_rim(apply):
        half = CH * COLS
        for key, which in ((-1, 0), (1, 1)):
            @pl.when(exists[(key, 0)])
            def _():
                dst = (mtop, mbot)[which]

                def body(c, carry):
                    spot = pl.ds(pl.multiple_of(c * half, half), half)
                    put(dst, spot, apply(
                        lambda: (top_in, bot_in)[which][spot, :].astype(F32),
                        lambda l: (top_sp, bot_sp)[which][l, spot, :].astype(F32),
                    ))
                    return carry

                lax.fori_loop(0, n // CH, body, 0)

    def over_sides(apply):
        for dw, base in ((-1, 0), (1, 4)):
            for r in range(4):
                dh = -1 if r == 0 else (1 if r == 3 else 0)

                @pl.when(exists[(dh, dw)])
                def _():
                    put(mside.at[base + r], pl.ds(8, n), apply(
                        lambda: side_in[base + r].astype(F32), lambda l: side_sp[l, base + r].astype(F32)
                    ))

    def side_sums(l, flip, target, base):
        stats = []
        for lb in range(narrow // LANES):
            lanes = pl.ds(lb * LANES, LANES)
            first = jnp.zeros((8, LANES), F32)
            square = jnp.zeros((8, LANES), F32)
            for side, e, col in ((0, 0, 0), (4, 2, COLS - 1)):
                for h in range(ROWS):
                    total = None
                    for a in range(3):
                        part = None
                        for b in range(3):
                            i = (a * 3 + b) * 3 + e
                            weight = wtap[l, 26 - i if flip else i, 0:1, lanes]
                            term = mside[side + h + b, lb, 7 + a : 7 + a + n, :] * weight
                            part = term if part is None else part + term
                        part = part * vflag[a] if a != 1 else part
                        total = part if total is None else total + part
                    total = total * vflag[1]
                    spot = pl.ds(base + 8 * h + col, n, stride=SPOT)
                    old = target[lb, spot, :]
                    new = old + total
                    target[lb, spot, :] = new
                    first = first + fold8(total)
                    square = square + fold8((new - old) * (new + old))
            stats.append((first, square))
        return stats

    row_id = lax.broadcasted_iota(jnp.int32, (8, LANES), 0)

    def shifted(own, own_base, f, lb):
        start = own_base + f * SPOT
        lines = [
            mtop[lb, pl.ds(pl.multiple_of(f * 8, 8), 8), :],
            own[lb, pl.ds(pl.multiple_of(start, 8), 8), :],
            own[lb, pl.ds(pl.multiple_of(start + 8, 8), 8), :],
            mbot[lb, pl.ds(pl.multiple_of(f * 8, 8), 8), :],
        ]
        out = []
        for v in lines:
            left = jnp.where(row_id == 0, 0.0, pltpu.roll(v, 1, 0))
            right = jnp.where(row_id == 7, 0.0, pltpu.roll(v, 7, 0))
            out.append((left, v, right))
        return out

    def tap_sum(grid, l, lanes, a, flip):
        res = []
        for h in range(ROWS):
            total = None
            for b in range(3):
                for e in range(3):
                    i = (a * 3 + b) * 3 + e
                    term = grid[h + b][e] * wtap[l, 26 - i if flip else i, :, lanes]
                    total = term if total is None else total + term
            res.append(total)
        return res

    def vmask(c):
        m = vm8[pl.ds(pl.multiple_of(c * CH * 8, CH * 8), CH * 8), :]
        m = jnp.broadcast_to(m.reshape(CH, 1, 8, LANES), (CH, ROWS, 8, LANES)).reshape(CH * SPOT, LANES)
        return jnp.concatenate([m] * (narrow // LANES), axis=1)

    def chunk(c):
        return pl.ds(pl.multiple_of(c * CH * SPOT, CH * SPOT), CH * SPOT)

    def chunk_off(c, base):
        return pl.ds(pl.multiple_of(base + c * CH * SPOT, SPOT), CH * SPOT)

    zero8 = jnp.zeros((8, narrow), F32)
    blocks = [pl.ds(k * narrow, narrow) for k in range(wide // narrow)]
    steps = n // CH
    scal = {}

    def reduce_phase(l):
        source = xc if l == 0 else x1

        def body(c, carry):
            first, square = carry
            r = dot(source[chunk(c), :], wred_ref[l])
            put(red.at[l], chunk(c), r)
            kept = r * vmask(c) if l == 0 else r
            return first + fold8(kept), square + fold8(kept * r)

        first, square = lax.fori_loop(0, steps, body, (zero8, zero8))
        reduce_start(3 * l, nar_a, nar_b, 2 * l, local_moments(first, square), True)
        fill_send(red.at[l], 0)
        rim_start(l, rims)
        if l == 0:
            set_taps()

    def mix_phase(l):
        average, inv = reduce_finish(3 * l, nar_b, 2 * l, True)
        scale = gn_ref[l, 0:1] * inv
        shift = sn_ref[l, 0:1] - average * scale
        scal["one", l] = (average, inv, scale, shift)

        def body(c, carry):
            z = get(red.at[l], chunk(c)) * scale + shift
            h = (z * sigmoid(z)).astype(BF16)
            put(mown.at[l], chunk_off(c, SPOT), dot(h, wmix_ref[l]))
            return carry

        lax.fori_loop(0, steps, body, 0)
        rim_arrived(l, rims, range(2))

        def apply(arrived, second):
            z = arrived() * scale + shift
            return dot((z * sigmoid(z)).astype(BF16), wmix_ref[l])

        over_rim(apply)
        return apply

    def spatial_phase(l, apply):
        stats = []
        for lb in range(narrow // LANES):
            lanes = pl.ds(lb * LANES, LANES)

            def body(f, carry):
                cur, nxt, first, square = carry
                grid = shifted(mown.at[l], SPOT, f, lb)
                here = flag_ref[1, f]
                t2 = tap_sum(grid, l, lanes, 2, False)
                t1 = tap_sum(grid, l, lanes, 1, False)
                t0 = tap_sum(grid, l, lanes, 0, False)
                alive = flag_ref[2, f]
                for h in range(ROWS):
                    done = (cur[h] + here * t2[h]) * alive
                    spat[l, lb, pl.ds(pl.multiple_of(f * SPOT + 8 * h, 8), 8), :] = done
                    first = first + done
                    square = square + done * done
                cur = tuple(t1[h] + here * nxt[h] for h in range(ROWS))
                return cur, tuple(t0), first, square

            z = jnp.zeros((8, LANES), F32)
            cur, nxt, first, square = lax.fori_loop(0, n, body, ((z, z), (z, z), z, z), unroll=UNROLL_F)
            for h in range(ROWS):
                done = cur[h] * flag_ref[2, n]
                spat[l, lb, rows + 8 * h : rows + 8 * h + 8, :] = done
                first = first + done
                square = square + done * done
            stats.append((first, square))
        rim_arrived(l, rims, range(2, 8))
        over_sides(apply)
        more = side_sums(l, False, spat.at[l], SPOT)
        rim_sent(l, rims)
        first = jnp.concatenate([s[0] + m[0] for s, m in zip(stats, more)], axis=1)
        square = jnp.concatenate([s[1] + m[1] for s, m in zip(stats, more)], axis=1)
        reduce_start(3 * l + 1, nar_a, nar_b, 2 * l + 1, local_moments(first, square), True)
        fill_send(spat.at[l], SPOT)
        rim_start(layers + l, rims_sp[l])
        if l == 0:
            turn_weights()

    def hidden_phase(l):
        average, inv = reduce_finish(3 * l + 1, nar_b, 2 * l + 1, True)
        scale = gn_ref[l, 1:2] * inv
        shift = sn_ref[l, 1:2] - average * scale
        scal["two", l] = (average, inv, scale, shift)

        def body(c, first):
            z = get(spat.at[l], chunk_off(c, SPOT)) * scale + shift
            h = z * sigmoid(z) * vmask(c)
            low = h.astype(BF16)
            h2[l, chunk(c), :] = low
            return first + fold8(low.astype(F32))

        first = lax.fori_loop(0, steps, body, zero8)
        g = dot_first(h2[l], h2[l])
        gram[l] = g
        t = split_dot(g, wexp_ref[l])
        square = jnp.sum(t * wexp_ref[l].astype(F32), axis=0, keepdims=True)
        hsum = jnp.sum(first, axis=0, keepdims=True)
        scal["hsum", l] = hsum
        both = split_dot(jnp.broadcast_to(hsum, (8, narrow)), wexp_ref[l])[0:1]
        second = square - both * both * my_count_inv[wide]
        reduce_start(3 * l + 2, wid_a, wid_b, l, jnp.concatenate([both, second], axis=0), True)
        rim_sent(layers + l, rims_sp[l])

    def widen_phase(l):
        average, inv = reduce_finish(3 * l + 2, wid_b, l, True)
        scale = gw_ref[l : l + 1] * inv
        shift = sw_ref[l : l + 1] - average * scale
        scal["wide", l] = (average, inv, scale, shift)
        source = xc if l == 0 else x1
        last = l == layers - 1

        def body(c, sums):
            out = []
            hid = h2[l, chunk(c), :]
            mask = vmask(c)
            for k, blk in enumerate(blocks):
                cut = slice(k * narrow, (k + 1) * narrow)
                w = dot(hid, wexp_ref[l, :, blk])
                summed = source[chunk(c), blk].astype(F32) + (w * scale[:, cut] + shift[:, cut])
                s = sigmoid(summed)
                y = summed * s
                if not last:
                    x1[chunk(c), blk] = (y * mask).astype(BF16)
                    s0[chunk(c), blk] = summed.astype(BF16)
                else:
                    xc[chunk(c), blk] = (y * mask).astype(BF16)
                    up = u[chunk(c), blk].astype(F32) * (s * (1.0 + summed * (1.0 - s))) * mask
                    low = up.astype(BF16)
                    u[chunk(c), blk] = low
                    out.append(sums[k] + fold8(low.astype(F32)))
            return tuple(out)

        return lax.fori_loop(0, steps, body, tuple(zero8 for _ in blocks) if last else ())

    def back_wide(l, sums):
        total = jnp.concatenate([jnp.sum(s, axis=0, keepdims=True) for s in sums], axis=1)
        second = []
        if BIG_DOT:
            hu[...] = dot_first(h2[l], u[...])
        for blk in blocks:
            if not BIG_DOT:
                hu[:, blk] = dot_first(h2[l], u[:, blk])
            second.append(jnp.sum(hu[:, blk] * wexp_ref[l, :, blk].astype(F32), axis=0, keepdims=True))
        second = jnp.concatenate(second, axis=1)
        reduce_start(
            3 * layers + 3 * l, wid_a, wid_b, layers + l, jnp.concatenate([total, second], axis=0), False
        )
        wtb[...] = (wexp_ref[l].astype(F32) * scal["wide", l][2]).T.astype(BF16)

        def body(c, carry):
            put(g2, chunk(c), dot(u[chunk(c), :], wtb[...]))
            return carry

        lax.fori_loop(0, steps, body, 0)

    def back_expand(l):
        gshift, gsec = reduce_finish(3 * layers + 3 * l, wid_b, layers + l, False)
        average, inv, scale, _ = scal["wide", l]
        ggain = inv * (gsec - average * gshift)
        small_w[l : l + 1] = ggain
        small_w[layers + l : layers + l + 1] = gshift
        drift = inv * ggain * total_inv[wide]
        mx = dot((wexp_ref[l].astype(F32) * drift).astype(BF16), wtb[...]).astype(BF16)
        base = gshift * total_inv[wide] - average * drift
        const = split_dot(jnp.broadcast_to(base, (8, wide)), wtb[...])[0:1]
        _, _, scale2, shift2 = scal["two", l]
        avg2, inv2, _, _ = scal["two", l]

        def body(c, carry):
            first, square = carry
            p = get(g2, chunk(c)) - dot(h2[l, chunk(c), :], mx) - const
            sp = get(spat.at[l], chunk_off(c, SPOT))
            g = p * slope_of(sp * scale2 + shift2) * vmask(c)
            put(g2, chunk(c), g)
            normed = (sp - avg2) * inv2
            return first + fold8(g), square + fold8(g * normed)

        first, square = lax.fori_loop(0, steps, body, (zero8, zero8))
        reduce_start(
            3 * layers + 3 * l + 1, nar_a, nar_b, 2 * layers + 2 * l, plain_pair(first, square), False
        )
        fill_send(g2, 0)
        rim_start(2 * layers + l, rims)
        hcol = jnp.broadcast_to(scal["hsum", l], (8, narrow)).T[:, 0:1]
        grad = scale * (
            hu[...] - hcol * (gshift * total_inv[wide] - average * drift) - split_dot(gram[l], wexp_ref[l]) * drift
        )
        buf, row = place[("expand", l)]
        for k in range(wide // LANES):
            buf[row + k * narrow : row + (k + 1) * narrow, :] = grad[:, k * LANES : (k + 1) * LANES].astype(BF16)

    def back_spatial(l):
        gshift, ggain = reduce_finish(3 * layers + 3 * l + 1, nar_b, 2 * layers + 2 * l, False)
        small_n[4 * l + 1 : 4 * l + 2] = ggain
        small_n[4 * l + 3 : 4 * l + 4] = gshift
        avg2, inv2, scale2, _ = scal["two", l]
        a_u = scale2
        a_s = scale2 * inv2 * ggain * total_inv[narrow]
        a_c = scale2 * gshift * total_inv[narrow] - a_s * avg2

        def body(c, carry):
            put(g2, chunk(c), a_u * get(g2, chunk(c)) - a_s * get(spat.at[l], chunk_off(c, SPOT)) - a_c)
            return carry

        lax.fori_loop(0, steps, body, 0)
        rim_arrived(2 * layers + l, rims, range(2))
        rim_arrived(layers + l, rims_sp[l], range(8))
        apply = lambda arrived, second: a_u * arrived() - a_s * second(l) - a_c
        over_rim(apply)
        tap_grads = []

        for lb in range(narrow // LANES):
            lanes = pl.ds(lb * LANES, LANES)
            if l == 0 and lb == 0:
                step_b(1)
            if l == 0 and lb == 1:
                step_a(4)
                step_b(2)

            def body(f, carry):
                cur, nxt, grads = carry
                grid = shifted(g2, 0, f, lb)
                here = flag_ref[1, f]
                after = flag_ref[1, f + 1]
                live = flag_ref[0, f]
                t2 = tap_sum(grid, l, lanes, 2, True)
                t1 = tap_sum(grid, l, lanes, 1, True)
                t0 = tap_sum(grid, l, lanes, 0, True)
                alive = flag_ref[2, f]
                done = [(cur[h] + here * t2[h]) * alive for h in range(ROWS)]
                spat[l, lb, pl.ds(pl.multiple_of(f * SPOT, SPOT), SPOT), :] = jnp.concatenate(done, axis=0)
                grads = list(grads)
                for a, flag in ((0, here), (1, live), (2, after)):
                    for h in range(ROWS):
                        m = flag * mown[l, lb, pl.ds(pl.multiple_of((f + a) * SPOT + 8 * h, 8), 8), :]
                        for b in range(3):
                            for e in range(3):
                                i = (a * 3 + b) * 3 + e
                                grads[i] = grads[i] + m * grid[h + 2 - b][2 - e]
                cur = tuple(t1[h] + here * nxt[h] for h in range(ROWS))
                return cur, tuple(t0), tuple(grads)

            z = jnp.zeros((8, LANES), F32)
            cur, nxt, grads = lax.fori_loop(0, n, body, ((z, z), (z, z), tuple(z for _ in range(27))), unroll=UNROLL_B)
            spat[l, lb, rows : rows + SPOT, :] = jnp.concatenate(
                [cur[h] * flag_ref[2, n] for h in range(ROWS)], axis=0
            )
            tap_grads.append(list(grads))

        rim_arrived(2 * layers + l, rims, range(2, 8))
        over_sides(apply)
        side_sums(l, True, spat.at[l], SPOT)
        rim_sent(2 * layers + l, rims)
        for lb in range(narrow // LANES):
            grads = tap_grads[lb]
            for side, e, col in ((0, 2, 0), (4, 0, COLS - 1)):
                for a in range(3):
                    for h in range(ROWS):
                        m = mown[l, lb, pl.ds(a * SPOT + 8 * h + col, n, stride=SPOT), :] * vflag[a]
                        for b in range(3):
                            i = (a * 3 + b) * 3 + e
                            grads[i] = grads[i] + fold8(m * mside[side + h + 2 - b, lb, 8 : 8 + n, :])
            folded = [jnp.sum(g, axis=0, keepdims=True) for g in grads]
            folded += [jnp.zeros((1, LANES), F32)] * 5
            buf, row = place[("depth", l)]
            buf[row + lb * 32 : row + lb * 32 + 32, :] = jnp.concatenate(folded, axis=0).astype(BF16)

        avg1, inv1, scale1, shift1 = scal["one", l]

        def body2(c, carry):
            first, square = carry
            low = get(spat.at[l], chunk_off(c, SPOT)).astype(BF16)
            gm[chunk(c), :] = low
            r = get(red.at[l], chunk(c))
            z = r * scale1 + shift1
            sig = sigmoid(z)
            h2[l, chunk(c), :] = (z * sig).astype(BF16)
            g = dot(low, wmt[l]) * (sig * (1.0 + z * (1.0 - sig)))
            put(g2, chunk(c), g)
            return first + fold8(g), square + fold8(g * ((r - avg1) * inv1))

        first, square = lax.fori_loop(0, steps, body2, (zero8, zero8))
        reduce_start(
            3 * layers + 3 * l + 2, nar_a, nar_b, 2 * layers + 2 * l + 1, plain_pair(first, square), False
        )
        buf, row = place[("mix", l)]
        grad = dot_first(h2[l], gm[...]).astype(BF16)
        for k in range(narrow // LANES):
            buf[row + k * narrow : row + (k + 1) * narrow, :] = grad[:, k * LANES : (k + 1) * LANES]

    def back_reduce(l):
        gshift, ggain = reduce_finish(3 * layers + 3 * l + 2, nar_b, 2 * layers + 2 * l + 1, False)
        small_n[4 * l : 4 * l + 1] = ggain
        small_n[4 * l + 2 : 4 * l + 3] = gshift
        avg1, inv1, scale1, _ = scal["one", l]
        a_u = scale1
        a_s = scale1 * inv1 * ggain * total_inv[narrow]
        a_c = scale1 * gshift * total_inv[narrow] - a_s * avg1

        def body(c, sums):
            gr = (a_u * get(g2, chunk(c)) - a_s * get(red.at[l], chunk(c)) - a_c) * vmask(c)
            gr = gr.astype(BF16)
            gm[chunk(c), :] = gr
            if l == 0:
                return ()
            out = []
            for k, blk in enumerate(blocks):
                g = u[chunk(c), blk].astype(F32) + dot(gr, wtr[l, :, blk])
                up = g * slope_of(s0[chunk(c), blk].astype(F32))
                low = up.astype(BF16)
                u[chunk(c), blk] = low
                out.append(sums[k] + fold8(low.astype(F32)))
            return tuple(out)

        sums = lax.fori_loop(0, steps, body, tuple(zero8 for _ in blocks) if l > 0 else ())
        return sums

    def input_grads(c):
        for blk in blocks:
            g = u[chunk(c), blk].astype(F32) + dot(gm[chunk(c), :], wtr[0, :, blk])
            u[chunk(c), blk] = g.astype(BF16)
        pltpu.make_async_copy(u.at[chunk(c)], gx_ref.at[chunk(c)], load_sem.at[3]).start()

    def back_reduce_weight(l):
        source = xc if l == 0 else x1
        buf, row = place[("reduce", l)]
        if BIG_DOT:
            whole = dot_first(gm[...], source[...])
        for k, blk in enumerate(blocks):
            if BIG_DOT:
                grad = whole[:, k * narrow : (k + 1) * narrow].T.astype(BF16)
            else:
                grad = dot_first(gm[...], source[:, blk]).T.astype(BF16)
            for lb in range(narrow // LANES):
                first = row + lb * wide + k * narrow
                buf[first : first + narrow, :] = grad[:, lb * LANES : (lb + 1) * LANES]

    groups = {
        "ha": (na, my_a, a_peer),
        "wa": (nw, me["wa"], lambda k: at(wa=lax.rem(me["wa"] + k, nw))),
        "clip": (nc, me["clip"], lambda k: at(clip=lax.rem(me["clip"] + k, nc))),
        "all": (ne, my_e, e_peer),
    }

    def bytes_wait(ref, count, sem):
        part = ref.at[pl.ds(0, count)]
        pltpu.make_async_copy(part, part, sem).wait()

    def pack_step(number, stages, padded, bufs, out_hbm):
        wb, recvs, gats = bufs
        sizes_of = []
        left = padded
        for st in stages:
            sizes_of.append((left, left // groups[st][0]))
            left //= groups[st][0]
        last = len(stages) - 1

        def send_seg(i):
            size, mine, peer = groups[stages[i]]
            seg = sizes_of[i][1]
            src = wb if i == 0 else gats[i - 1].at[groups[stages[i - 1]][1]]

            def send(k, c):
                target = lax.rem(mine + k, size)
                pltpu.make_async_remote_copy(
                    src_ref=src.at[pl.ds(pl.multiple_of(target * seg, 16), seg)], dst_ref=recvs[i].at[mine],
                    send_sem=wg_send.at[number, i], recv_sem=wg_recv.at[number, i],
                    device_id=peer(k), device_id_type=MESH,
                ).start()
                return c

            lax.fori_loop(1, size, send, 0)
            recvs[i][mine] = src[pl.ds(pl.multiple_of(mine * seg, 16), seg), :]

        def add_up(i):
            size, mine, _ = groups[stages[i]]
            seg = sizes_of[i][1]
            if size > 1:
                bytes_wait(recvs[i], size - 1, wg_recv.at[number, i])
                bytes_wait(recvs[i], size - 1, wg_send.at[number, i])

            def add(c, carry):
                spot = pl.ds(pl.multiple_of(c * 16, 16), 16)
                total = recvs[i][0, spot, :].astype(F32)
                for j in range(1, size):
                    total = total + recvs[i][j, spot, :].astype(F32)
                gats[i][mine, spot, :] = total.astype(BF16)
                return carry

            lax.fori_loop(0, seg // 16, add, 0)

        def send_back(i):
            size, mine, peer = groups[stages[i]]
            k_sem = 2 * len(stages) - 1 - i

            def send(k, c):
                pltpu.make_async_remote_copy(
                    src_ref=gats[i].at[mine], dst_ref=gats[i].at[mine],
                    send_sem=wg_send.at[number, k_sem], recv_sem=wg_recv.at[number, k_sem],
                    device_id=peer(k), device_id_type=MESH,
                ).start()
                return c

            lax.fori_loop(1, size, send, 0)

        def got_back(i):
            size = groups[stages[i]][0]
            k_sem = 2 * len(stages) - 1 - i
            if size > 1:
                bytes_wait(gats[i], size - 1, wg_recv.at[number, k_sem])
                bytes_wait(gats[i], size - 1, wg_send.at[number, k_sem])

        def down(i):
            mine = groups[stages[i]][1]
            seg = sizes_of[i + 1][1]

            def keep(j, c):
                gats[i][mine, pl.ds(pl.multiple_of(j * seg, 16), seg), :] = gats[i + 1][j]
                return c

            lax.fori_loop(0, groups[stages[i + 1]][0], keep, 0)

        def step(k):
            if k <= last:
                if k > 0:
                    add_up(k - 1)
                send_seg(k)
            elif k == last + 1:
                add_up(last)
                send_back(last)
            elif k <= 2 * last + 1:
                i = 2 * last + 1 - k
                got_back(i + 1)
                down(i)
                send_back(i)
            else:
                got_back(0)
                copy = pltpu.make_async_copy(gats[0], out_hbm, load_sem.at[4 + number])
                copy.start()

        def stored():
            pltpu.make_async_copy(gats[0], out_hbm, load_sem.at[4 + number]).wait()

        return step, stored

    rims = rim_list(row_send, col_send, top_in, bot_in, side_in)
    rims_sp = [rim_list(row_send, col_send, top_sp.at[l], bot_sp.at[l], side_sp.at[l]) for l in range(layers)]

    place = {}
    packs = []
    first_bufs = []
    at_ref = 0
    for number, (parts, stages, padded, used) in enumerate(plan):
        m = len(stages)
        bufs = (pack_refs[at_ref] if number < 2 else first_bufs[number - 2], pack_refs[at_ref + 1 : at_ref + 1 + m], pack_refs[at_ref + 1 + m : at_ref + 1 + 2 * m])
        first_bufs.append(pack_refs[at_ref])
        at_ref += 1 + 2 * m
        for key, row, _ in parts:
            place[key] = (bufs[0], row)
        if padded > used and number < 2:
            bufs[0][used:padded, :] = jnp.zeros((padded - used, LANES), BF16)
        packs.append(pack_step(number, stages, padded, bufs, (packed_a, packed_b, packed_c, packed_d)[number]))
    (step_a, stored_a), (step_b, stored_b), (step_c, stored_c), (step_d, stored_d) = packs

    load.wait()
    load2.start()
    for l in range(layers):
        reduce_phase(l)
        spatial_phase(l, mix_phase(l))
        hidden_phase(l)
        if l == layers - 1:
            load2.wait()
        sums = widen_phase(l)
    store_y = pltpu.make_async_copy(xc, y_ref, load_sem.at[2])
    store_y.start()
    load_again = pltpu.make_async_copy(x_hbm, xc, load_sem.at[0])
    for l in reversed(range(layers)):
        back_wide(l, sums)
        if l == 0:
            store_y.wait()
            load_again.start()
            back_reduce_weight(1)
            step_a(2)
        back_expand(l)
        if l == 0:
            step_a(3)
            step_b(0)
        back_spatial(l)
        if l == 0:
            step_a(5)
            step_b(3)
            step_d(0)
        else:
            step_a(0)
        sums = back_reduce(l)
        if l == 0:
            step_a(6)
            step_b(4)
        else:
            step_a(1)
    load_again.wait()
    back_reduce_weight(0)
    step_c(0)
    step_d(1)
    input_grads(0)
    step_c(1)
    step_b(5)
    input_grads(1)
    step_d(2)
    step_b(6)
    step_d(3)
    step_c(2)
    step_d(4)
    step_c(3)
    step_c(4)
    pltpu.make_async_copy(u, gx_ref, load_sem.at[3]).wait()
    stored_a()
    stored_b()
    stored_c()
    stored_d()


def pack_plan(sizes, wide, narrow):
    world = sizes[0] * sizes[1] * sizes[2]
    plan = []
    for names, stages in (
        ((("expand", 1), ("mix", 1), ("depth", 1)), ("ha", "wa", "clip")),
        ((("reduce", 1), ("expand", 0)), ("ha", "wa", "clip")),
        ((("reduce", 0),), ("ha", "all")),
        ((("mix", 0), ("depth", 0)), ("ha", "all")),
    ):
        nb = narrow // LANES
        rows = {"reduce": nb * wide, "expand": nb * wide, "mix": nb * narrow, "depth": nb * 32}
        used = 0
        parts = []
        for key in names:
            parts.append((key, used, rows[key[0]]))
            used += rows[key[0]]
        padded = -(-used // (16 * world)) * 16 * world
        plan.append((parts, stages, padded, used))
    return plan


def mega_call(sizes, clips, x, cot, stride, order, w_reduce, w_mix, w_depth, w_expand, gn, sn, gw, sw):
    na, nw, nc = sizes
    ne = nw * nc
    layers, wide, narrow = w_reduce.shape
    n = x.shape[0] // SPOT
    rows = n * SPOT
    plan = pack_plan(sizes, wide, narrow)
    group_size = {"ha": na, "wa": nw, "clip": nc, "all": ne}
    vmem = lambda shape, kind: pltpu.VMEM(shape, kind)
    half = n * COLS
    kernel = functools.partial(mega, sizes, clips, n // clips, layers, wide, narrow, plan)
    spec = pl.BlockSpec(memory_space=pltpu.VMEM)
    smem = pl.BlockSpec(memory_space=pltpu.SMEM)
    hbm = pl.BlockSpec(memory_space=pl.ANY)
    n_sync = 6 * layers
    nb = narrow // LANES
    world = na * ne
    slots = world if world <= 64 and world & (world - 1) == 0 else ne
    scratch = [
        pltpu.SMEM((3, n + 1), F32),
        vmem((rows, wide), BF16), vmem((rows, wide), BF16), vmem((rows, wide), BF16), vmem((rows, wide), BF16),
        vmem((layers, nb, rows, LANES), F32),
        vmem((layers, nb, rows + 2 * SPOT, LANES), F32), vmem((layers, nb, rows + SPOT, LANES), F32),
        vmem((layers, rows, narrow), BF16), vmem((nb, rows, LANES), F32), vmem((rows, narrow), BF16),
        vmem((nb, half, LANES), F32), vmem((nb, half, LANES), F32), vmem((8, nb, n + 16, LANES), F32),
        vmem((half, LANES), F32), vmem((3, n, LANES), F32), vmem((layers, 27, 8, narrow), F32), vmem((narrow, wide), F32),
        vmem((layers, narrow, narrow), F32),
        vmem((layers, narrow, wide), BF16), vmem((wide, narrow), BF16), vmem((layers, narrow, narrow), BF16),
        vmem((2, half, narrow), BF16), vmem((2, 2, n, narrow), BF16),
        vmem((half, narrow), BF16), vmem((half, narrow), BF16), vmem((8, n, narrow), BF16),
        vmem((layers, half, narrow), BF16), vmem((layers, half, narrow), BF16), vmem((layers, 8, n, narrow), BF16),
        vmem((4 * layers, na, 2, narrow), F32), vmem((4 * layers, slots, 2, narrow), F32),
        vmem((2 * layers, na, 2, wide), F32), vmem((2 * layers, ne, 2, wide), F32),
        pltpu.SemaphoreType.DMA((4 + len(plan),)), pltpu.SemaphoreType.DMA((n_sync, 2)), pltpu.SemaphoreType.DMA((n_sync, 2)),
        pltpu.SemaphoreType.DMA((3 * layers, 8)), pltpu.SemaphoreType.DMA((3 * layers, 8)),
        pltpu.SemaphoreType.DMA((len(plan), 6)), pltpu.SemaphoreType.DMA((len(plan), 6)),
    ]
    outs_packed = []
    for number, (_, stages, padded, _) in enumerate(plan):
        scratch.append(vmem((padded if number < 2 else 16, LANES), BF16))
        recvs, gats, left = [], [], padded
        for st in stages:
            left //= group_size[st]
            recvs.append(vmem((group_size[st], left, LANES), BF16))
            gats.append(vmem((group_size[st], left, LANES), BF16))
        scratch += recvs + gats
        outs_packed.append(jax.ShapeDtypeStruct(gats[0].shape, BF16))
    shape = jax.ShapeDtypeStruct
    outs = (
        shape((rows, wide), BF16), shape((rows, wide), BF16),
        *outs_packed,
        shape((4 * layers, narrow), F32), shape((2 * layers, wide), F32),
    )
    return pl.pallas_call(
        kernel,
        out_shape=outs,
        in_specs=[smem, smem, hbm, hbm] + [spec] * 8,
        out_specs=(hbm,) * 6 + (spec,) * 2,
        scratch_shapes=scratch,
        compiler_params=pltpu.CompilerParams(
            collective_id=0, has_side_effects=True, vmem_limit_bytes=63 * 1024 * 1024
        ),
    )(stride, order, x, cot, w_reduce, w_mix, w_depth, w_expand, gn, sn, gw, sw)


def finish_kernel(plan, layers, wide, narrow, steps, *refs):
    if not ROOT_COPY:
        y_ref, g_ref, *refs = refs
        oy, og = refs[6:8]
        refs = refs[:6] + refs[8:]
        oy[...] = y_ref[...]
        og[...] = g_ref[...]
    pa, pb, pc, pd, sn, sw, owr, owm, owd, owe, ogn, osn, ogw, osw = refs
    i = pl.program_id(0)
    packed = (pa, pb, pc, pd)
    rows_r, rows_m = wide // steps, narrow // steps
    for number, (parts, _, _, _) in enumerate(plan):
        for (kind, l), row, _ in parts:
            ref = packed[number]
            if kind == "expand":
                for k in range(wide // LANES):
                    spot = pl.ds(pl.multiple_of(row + k * narrow + i * rows_m, 16), rows_m)
                    owe[l, :, k * LANES : (k + 1) * LANES] = ref[spot, :].astype(F32)
            elif kind != "depth":
                dst, size, part = (owr, wide, rows_r) if kind == "reduce" else (owm, narrow, rows_m)
                for lb in range(narrow // LANES):
                    spot = pl.ds(pl.multiple_of(row + lb * size + i * part, 16), part)
                    dst[l, :, lb * LANES : (lb + 1) * LANES] = ref[spot, :].astype(F32)
            else:
                @pl.when(i == 0)
                def _():
                    taps = jnp.concatenate([ref[row + lb * 32 : row + lb * 32 + 32, :] for lb in range(narrow // LANES)], axis=1).astype(F32)
                    for t in range(27):
                        owd[t // 9, t // 3 % 3, t % 3, l : l + 1, :] = taps[t : t + 1]

    @pl.when(i == 0)
    def _():
        for l in range(layers):
            ogn[l] = sn[4 * l : 4 * l + 2]
            osn[l] = sn[4 * l + 2 : 4 * l + 4]
        ogw[...] = sw[0:layers]
        osw[...] = sw[layers : 2 * layers]


def finish_call(plan, layers, wide, narrow, y, g, packed, small):
    steps = FINISH_STEPS
    per = y.shape[0] // steps
    packed = [p.reshape(-1, LANES) for p in packed]
    whole = lambda a: pl.BlockSpec(a.shape, lambda i: (0,) * len(a.shape), pipeline_mode=pl.Buffered(1))
    keep = lambda shape: pl.BlockSpec(shape, lambda i: (0,) * len(shape))
    big = pl.BlockSpec((per, wide), lambda i: (i, 0))
    shape = jax.ShapeDtypeStruct
    bigs = [] if ROOT_COPY else [big, big]
    tiny = ((layers, 2, narrow), (layers, 2, narrow), (layers, wide), (layers, wide))
    outs = (() if ROOT_COPY else (shape(y.shape, BF16), shape(y.shape, BF16))) + (
        shape((layers, wide, narrow), F32), shape((layers, narrow, narrow), F32),
        shape((3, 3, 3, layers, narrow), F32), shape((layers, narrow, wide), F32),
    ) + tuple(shape(a, F32) for a in tiny)
    return pl.pallas_call(
        functools.partial(finish_kernel, plan, layers, wide, narrow, steps),
        out_shape=outs,
        grid=(steps,),
        in_specs=bigs + [whole(p) for p in packed] + [whole(a) for a in small],
        out_specs=tuple(bigs) + (
            pl.BlockSpec((layers, wide // steps, narrow), lambda i: (0, i, 0)),
            pl.BlockSpec((layers, narrow // steps, narrow), lambda i: (0, i, 0)),
            keep((3, 3, 3, layers, narrow)),
            pl.BlockSpec((layers, narrow // steps, wide), lambda i: (0, i, 0)),
        ) + tuple(keep(a) for a in tiny),
        compiler_params=pltpu.CompilerParams(vmem_limit_bytes=62 * 1024 * 1024),
    )(*(() if ROOT_COPY else (y, g)), *packed, *small)


def body(
    sizes, activations, stride, clip_order, cotangent, w_reduce, w_mix, w_depth, w_expand,
    gains_narrow, shifts_narrow, gains_wide, shifts_wide,
):
    clips, frame_len, _, _, wide = activations.shape
    layers, _, narrow = w_reduce.shape
    flat = (clips * frame_len * SPOT, wide)
    res = mega_call(
        sizes, clips, activations.reshape(flat), cotangent.reshape(flat),
        stride, clip_order, w_reduce, w_mix, jnp.transpose(w_depth, (1, 2, 3, 0, 4)), w_expand,
        gains_narrow, shifts_narrow, gains_wide, shifts_wide,
    )
    out = finish_call(pack_plan(sizes, wide, narrow), layers, wide, narrow, res[0], res[1], res[2:6], res[6:])
    if ROOT_COPY:
        out = (res[0], res[1]) + tuple(out)
    return (
        out[0].reshape(activations.shape), out[1].reshape(activations.shape), out[2], out[3],
        jnp.transpose(out[4], (3, 0, 1, 2, 4)),
    ) + tuple(out[5:])


def solution(mesh):
    sizes = tuple(mesh.shape[a] for a in AXES)
    big = P("clip", None, "ha", "wa", None)
    return jax.shard_map(
        functools.partial(body, sizes),
        mesh=mesh,
        in_specs=(big, P(), P(), big) + (P(),) * 8,
        out_specs=(big, big) + (P(),) * 8,
        check_vma=False,
    )
```
